128 devices in a mesh: dyn: 16 (over y, x), col: 8 (over z, core).
Axes of the slice: x: 4, y: 4, z: 4, core: 2. Of those that a mesh axis runs over, the one named last changes fastest.
Arguments:
- tracer: bfloat16 [1024, 768, 128], P('dyn', 'col'), may hold values from -6 to 6
- temper: bfloat16 [1024, 768, 128], P('dyn', 'col'), may hold values from -6 to 6
- winds: bfloat16 [2, 1024, 768, 128], P(None, 'dyn', 'col'), may hold values from -6 to 6
- owners: int32 [196608, 1], P(('dyn', 'col')), may hold values from 0 to 127; in each aligned block of 1536 rows (0 to 1535, 1536 to 3071, ...) at most 24 rows name the same one
- classes: int32 [196608], P(('dyn', 'col')), may hold values from 0 to 3
- aerosol: bfloat16 [128, 3072, 2048], P(('dyn', 'col')), may hold values from 0.25 to 4
- band_in: bfloat16 [256, 2048], replicated, may hold values from -0.375 to 0.375
- band_out: bfloat16 [2048, 256], replicated, may hold values from -0.125 to 0.125
Outputs:
- tracer_new: bfloat16 [1024, 768, 128], P('dyn', 'col')
- column_tend: bfloat16 [196608, 256], P(('dyn', 'col'))
The draws below stay inside these ranges and needn't reach their ends.
Inputs may be any that keep to these rules, and one draw needn't show every extreme that they name: `owners`: among the 1536 columns of one device no owner is named more than 24 times, a bound that some block reaches.
All inputs are finite; a program needn't handle non-finite values.
Results may differ from the reference program's by a relative error of at most 0.005.
Values may be sent and summed in bfloat16 or wider, within the bound.
No kernel may reach another device: no remote copies, remote signals or barrier semaphores. Data moves between devices by JAX's collectives and lax.ppermute only.
A program may use at most 128 MiB of HBM per device.

```python
import math
import jax
import jax.numpy as jnp
import numpy as np
from jax import lax

LEV = 128
NB = 16
EX = 16
EY = 24
NX = 1024
NY = 768
COLS_DEV = 1536
ALLCOLS = 196608
CAP = 24
SLOTS = 3072
N_DYN = 16
N_COL = 8
DEVICES = 128


def with_ends(values, key, smallest, top_value):
    dims = values.shape
    place = [jax.random.randint(jax.random.fold_in(key, axis), (), 0, dims[axis]) for axis in range(len(dims))]
    values = values.at[tuple(place)].set(smallest)
    longest = dims.index(max(dims))
    place[longest] = (place[longest] + 1) % dims[longest]
    return values.at[tuple(place)].set(top_value)


def steps_of(key, dims, split, low, top_value):
    gain = 1.0
    for dim, shards_of in split:
        heights = jax.random.uniform(jax.random.fold_in(jax.random.fold_in(key, 6), dim), (shards_of,), jnp.float32, low / len(split), top_value / len(split))
        gain = gain * jnp.repeat(jnp.exp(heights), dims[dim] // shards_of).reshape((-1,) + (1,) * (len(dims) - 1 - dim))
    return gain


def shared_out(rng, own, number, rows, amount, top, most, lean):
    ranking = jax.random.permutation(rng, amount)
    heavy_load, usual = shares(amount, rows * top, most, lean, True), shares(amount, rows * top, most, lean, False)
    places = jnp.arange(amount)

    def named(tallies, turn):
        used = int((tallies > 0).sum())
        fixed = max(1, used // 4)
        shifted = fixed + (places - fixed + turn * (used - fixed)) % max(1, amount - fixed)
        return jnp.zeros((amount,), jnp.int32).at[ranking[jnp.where(places < fixed, places, shifted)]].set(jnp.asarray(tallies, jnp.int32))

    tallies = jnp.where(number % 4 == 0, named(heavy_load, number // 4), named(usual, number - number // 4 - 1))
    mixed = jax.random.permutation(jax.random.fold_in(own, 3), amount)
    giver, receiver = mixed[0:amount // 2 * 2:2], mixed[1:amount // 2 * 2:2]
    room = jnp.minimum(tallies[giver] - 1, most - tallies[receiver]) // 2
    room = jnp.where((giver == ranking[0]) | (receiver == ranking[0]) | (tallies[receiver] == 0), 0, jnp.maximum(room, 0))
    shifted = jax.random.randint(jax.random.fold_in(own, 4), (amount // 2,), 0, 1 << 20) % (room + 1)
    tallies = tallies.at[giver].add(-shifted).at[receiver].add(shifted)
    members = jnp.searchsorted(jnp.cumsum(tallies), jnp.arange(rows * top), side="right").astype(jnp.int32)
    table = members.reshape(top, rows).T
    table = table[jax.random.permutation(jax.random.fold_in(own, 1), rows)]
    turn = jax.random.randint(jax.random.fold_in(own, 2), (rows, 1), 0, top)
    return jnp.take_along_axis(table, (jnp.arange(top)[None, :] + turn) % top, axis=1)


def shares(number_of, total, bound, slope, full):
    loads = [(1 << 20) // math.isqrt(rank ** slope) + 1 for rank in range(1, number_of + 1)]
    largest = bound if full else min(bound, max(-(-total // number_of), total * loads[0] // sum(loads)))
    least = 1 if total - largest >= number_of - 1 else 0
    holding, surplus = [largest] + [least] * (number_of - 1), total - largest - least * (number_of - 1)
    while surplus > 0:
        free = [i for i in range(1, number_of) if holding[i] < largest] or [i for i in range(1, number_of) if holding[i] < bound]
        pool, left = sum([loads[i] for i in free]), surplus
        for i in free:
            addition = min(bound - holding[i], max(1, left * loads[i] // pool), surplus)
            holding[i] = holding[i] + addition
            surplus = surplus - addition
    return np.array(holding)


def noise(own_key, shape, width, bound, cuts=(), held_as=jnp.bfloat16):
    drawn = width * jax.random.normal(own_key, shape, jnp.float32)
    if cuts:
        drawn = drawn * steps_of(own_key, shape, cuts, -0.22, 0.18)
    return jnp.clip(drawn, -bound, bound).astype(held_as)


def setup_inputs(seed: int = 0) -> dict:
    arg_keys = jax.random.split(jax.random.key(seed), 9)
    tracer = noise(arg_keys[0], (NX, NY, LEV), 1.0, 6.0, ((0, 16), (1, 8)))
    temper = noise(arg_keys[1], (NX, NY, LEV), 1.0, 6.0, ((0, 16), (1, 8)))
    winds = noise(arg_keys[2], (2, NX, NY, LEV), 1.0, 6.0, ((1, 16), (2, 8)))
    owners_keys = jax.random.split(jax.random.fold_in(arg_keys[3], 1), ALLCOLS // COLS_DEV)
    owners_turns = jax.random.permutation(jax.random.fold_in(arg_keys[3], 3), ALLCOLS // COLS_DEV)
    owners = jax.vmap(lambda own, number: shared_out(jax.random.fold_in(arg_keys[3], 2), own, number, COLS_DEV, DEVICES, 1, CAP, 2))(owners_keys, owners_turns).reshape((ALLCOLS, 1))
    classes = with_ends(jax.random.randint(arg_keys[4], (ALLCOLS,), 0, 4), jax.random.fold_in(arg_keys[4], 1), 0, 3).astype(jnp.int32)
    aerosol = jnp.clip(jnp.exp(math.log(4.0) - 2.7725887 * jax.random.uniform(arg_keys[5], (DEVICES, SLOTS, NB * LEV), jnp.float32) ** steps_of(arg_keys[5], (DEVICES, SLOTS, NB * LEV), ((0, 128),), -0.2, 0.2)), 0.25, 4.0).astype(jnp.bfloat16)
    band_in = noise(arg_keys[6], (2 * LEV, NB * LEV), (2 * LEV) ** -0.5, 0.375)
    band_out = noise(arg_keys[7], (NB * LEV, 2 * LEV), (NB * LEV) ** -0.5, 0.125)
    return dict(tracer=tracer, temper=temper, winds=winds, owners=owners, classes=classes, aerosol=aerosol, band_in=band_in, band_out=band_out)


STEP_SIZE = 0.1

def lagrange_tables():
    points = np.array([-1.0, -1.0 / math.sqrt(5.0), 1.0 / math.sqrt(5.0), 1.0])
    products = np.array([np.prod([points[row_at] - points[inner_at] for inner_at in range(4) if inner_at != row_at]) for row_at in range(4)])
    derivative = np.zeros((4, 4))
    for row_at in range(4):
        for col_at in range(4):
            if row_at == col_at:
                derivative[row_at, col_at] = np.sum([1.0 / (points[row_at] - points[inner_at]) for inner_at in range(4) if inner_at != row_at])
            else:
                derivative[row_at, col_at] = products[row_at] / (products[col_at] * (points[row_at] - points[col_at]))
    average = np.array([[1.0 / 6.0, 5.0 / 6.0, 0.0, 0.0], [0.0, 0.0, 5.0 / 6.0, 1.0 / 6.0]])
    return (derivative, average)

def apply_small(matrix, field, axis):
    pieces = [lax.index_in_dim(field, inner_at, axis, keepdims=True) for inner_at in range(4)]
    outputs = []
    for row_at in range(matrix.shape[0]):
        total = None
        for inner_at in range(4):
            weight = float(matrix[row_at, inner_at])
            if weight != 0.0:
                term = weight * pieces[inner_at]
                total = term if total is None else total + term
        outputs.append(total)
    return jnp.concatenate(outputs, axis=axis)

def tendency(state, wind_pair, derivative):
    rows_x, cols_y, levels = state.shape
    along_x = apply_small(derivative, state.reshape(rows_x // 4, 4, cols_y, levels), 1).reshape(state.shape)
    along_y = apply_small(derivative, state.reshape(rows_x, cols_y // 4, 4, levels), 2).reshape(state.shape)
    return -(wind_pair[0] * along_x + wind_pair[1] * along_y)

def assemble_periodic(field, dimension):
    extent = field.shape[dimension]
    layout = [1, 1, 1]
    layout[dimension] = extent
    position = (jnp.arange(extent) % 4).reshape(layout)
    forward = jnp.roll(field, -1, axis=dimension)
    backward = jnp.roll(field, 1, axis=dimension)
    return jnp.where(position == 3, 0.5 * (field + forward), jnp.where(position == 0, 0.5 * (field + backward), field))

def remap(field, average):
    rows_x, cols_y, levels = field.shape
    blocks = field.reshape(rows_x // 4, 4, cols_y // 4, 4, levels)
    cells = apply_small(average, apply_small(average, blocks, 1), 3)
    return cells.reshape(rows_x // 2, cols_y // 2, levels)

def radiate(state, cost_class, optical, band_in, band_out):
    optical_depth = jnp.dot(state, band_in, preferred_element_type=jnp.float32)
    band_count = NB
    optical_depth = optical_depth.reshape(state.shape[0], band_count, -1)
    factors = optical.astype(jnp.float32).reshape(state.shape[0], band_count, -1)
    active = jnp.arange(band_count)[None, :] < (cost_class[:, None] + 1) * band_count // 4
    thinned = jnp.exp(-jax.nn.softplus(optical_depth) * factors) * active[:, :, None]
    thinned = thinned.astype(jnp.bfloat16).reshape(state.shape[0], -1)
    return jnp.dot(thinned, band_out, preferred_element_type=jnp.float32).astype(jnp.bfloat16)

def slot_ranks(owner_block):
    onehot = (owner_block[:, None] == jnp.arange(DEVICES)[None, :]).astype(jnp.int32)
    earlier = jnp.cumsum(onehot, axis=0) - onehot
    return lax.optimization_barrier(jnp.sum(earlier * onehot, axis=1))

def reference(tracer, temper, winds, owners, classes, aerosol, band_in, band_out):
    derivative, average = lagrange_tables()
    tend = tendency(tracer.astype(jnp.float32), winds.astype(jnp.float32), derivative)
    assembled = assemble_periodic(assemble_periodic(tend, 0), 1)
    tracer_new = (tracer.astype(jnp.float32) + STEP_SIZE * assembled).astype(jnp.bfloat16)
    cells_tracer = remap(tracer_new.astype(jnp.float32), average)
    cells_temper = remap(temper.astype(jnp.float32), average)
    joined = jnp.concatenate([cells_tracer, cells_temper], axis=2).astype(jnp.bfloat16)
    joined = joined.reshape(N_DYN, 2 * EX, N_COL, 2 * EY, 2 * LEV).transpose(0, 2, 1, 3, 4)
    column_state = joined.reshape(DEVICES, COLS_DEV, 2 * LEV)
    owner_block = owners[:, 0].reshape(DEVICES, COLS_DEV)

    def per_block(pieces):
        state, cost_class, owned, source = pieces
        slot = slot_ranks(owned)
        optical = aerosol[owned, source * CAP + slot, :]
        return radiate(state, cost_class, optical, band_in, band_out)
    column_tend = lax.map(per_block, (column_state, classes.reshape(DEVICES, COLS_DEV), owner_block, jnp.arange(DEVICES, dtype=jnp.int32)))
    return (tracer_new, column_tend.reshape(ALLCOLS, 2 * LEV))
```

```python
import functools
import math

import jax
import jax.numpy as jnp
import numpy as np
from jax import lax
from jax.experimental import pallas as pl
from jax.experimental.pallas import tpu as pltpu
from jax.sharding import PartitionSpec as P

STEP_SIZE = 0.1
F32, BF16, I32 = jnp.float32, jnp.bfloat16, jnp.int32
MIB = 1024 * 1024


def lagrange_tables():
    points = np.array([-1.0, -1.0 / math.sqrt(5.0), 1.0 / math.sqrt(5.0), 1.0])
    products = np.array(
        [np.prod([points[r] - points[k] for k in range(4) if k != r]) for r in range(4)]
    )
    derivative = np.zeros((4, 4))
    for r in range(4):
        for c in range(4):
            if r == c:
                derivative[r, c] = np.sum(
                    [1.0 / (points[r] - points[k]) for k in range(4) if k != r]
                )
            else:
                derivative[r, c] = products[r] / (products[c] * (points[r] - points[c]))
    average = np.array([[1.0 / 6.0, 5.0 / 6.0, 0.0, 0.0], [0.0, 0.0, 5.0 / 6.0, 1.0 / 6.0]])
    return (derivative, average)


GRAD, PG2 = lagrange_tables()


def combine(weights, pieces):
    total = None
    for weight, piece in zip(weights, pieces):
        if abs(float(weight)) > 1e-12:
            term = float(weight) * piece
            total = term if total is None else total + term
    return total


def cell_pair(nodes):
    halves = [[combine(PG2[a], [nodes[x][k] for x in range(4)]) for k in range(4)] for a in range(2)]
    return [[combine(PG2[b], halves[a]) for b in range(2)] for a in range(2)]


def call(kernel, out_shape, *args, vmem, flops=0, moved=0, **kw):
    return pl.pallas_call(
        kernel,
        out_shape=out_shape,
        compiler_params=pltpu.CompilerParams(vmem_limit_bytes=vmem * MIB),
        cost_estimate=pl.CostEstimate(flops=flops, bytes_accessed=moved, transcendentals=0),
        **kw,
    )(*args)


def full(shape):
    return pl.BlockSpec(shape, lambda *_: (0,) * len(shape))


def edges_kernel(tracer, winds, ex0, ex3, ey0, ey3, xs, xw, ys, yw, line, wind, strip, vstrip, sem):
    nx, ny, lev = tracer.shape
    ne = ny // 4
    copies = []
    for i, (x, x4, y) in enumerate(((0, 0, 0), (nx - 1, nx - 4, ny - 16))):
        copies.append((
            pltpu.make_async_copy(tracer.at[pl.ds(x4, 4)], xs.at[i], sem.at[i, 0]),
            pltpu.make_async_copy(winds.at[:, x], xw.at[i], sem.at[i, 1]),
            pltpu.make_async_copy(tracer.at[:, pl.ds(y, 16)], ys.at[i], sem.at[i, 2]),
            pltpu.make_async_copy(winds.at[:, :, pl.ds(y, 16)], yw.at[i], sem.at[i, 3]),
        ))
    for part in (0, 2):
        for group in copies:
            group[part].start()
            group[part + 1].start()

    for i, (node, out) in enumerate(((0, ex0), (3, ex3))):
        copies[i][0].wait()
        copies[i][1].wait()
        for x in range(4):
            line[pl.ds((4 * i + x) * ny, ny), :] = xs[i, x].astype(F32)
        for h in range(2):
            wind[pl.ds((2 * i + h) * ny, ny), :] = xw[i, h].astype(F32)
        nodes = [
            [line[pl.ds((4 * i + x) * ny + k, ne, stride=4), :] for k in range(4)] for x in range(4)
        ]
        for k in range(4):
            dx = combine(GRAD[node], [nodes[m][k] for m in range(4)])
            dy = combine(GRAD[k], nodes[node])
            u = wind[pl.ds(2 * i * ny + k, ne, stride=4), :]
            v = wind[pl.ds((2 * i + 1) * ny + k, ne, stride=4), :]
            out[pl.ds(k * ne, ne), :] = -(u * dx + v * dy)

    size = nx * 16
    for i, (base, node, out) in enumerate(((0, 0, ey0), (12, 3, ey3))):
        copies[i][2].wait()
        copies[i][3].wait()
        nel = nx // 4
        strip[pl.ds(i * size, size), :] = ys[i].astype(F32).reshape(size, lev)
        for h in range(2):
            vstrip[pl.ds((2 * i + h) * size, size), :] = yw[i, h].astype(F32).reshape(size, lev)
        nodes = [
            [strip[pl.ds(i * size + x * 16 + base + k, nel, stride=64), :] for k in range(4)]
            for x in range(4)
        ]
        for x in range(4):
            dx = combine(GRAD[x], [nodes[m][node] for m in range(4)])
            dy = combine(GRAD[node], nodes[x])
            at = x * 16 + base + node
            u = vstrip[pl.ds(2 * i * size + at, nel, stride=64), :]
            v = vstrip[pl.ds((2 * i + 1) * size + at, nel, stride=64), :]
            out[pl.ds(x, nel, stride=4), :] = -(u * dx + v * dy)


def edges(tracer, winds):
    nx, ny, lev = tracer.shape
    shapes = [(ny, lev)] * 2 + [(nx, lev)] * 2
    return call(
        edges_kernel,
        [jax.ShapeDtypeStruct(s, F32) for s in shapes],
        tracer, winds,
        vmem=53, flops=10**6, moved=3 * 10**6,
        in_specs=[pl.BlockSpec(memory_space=pltpu.HBM)] * 2,
        scratch_shapes=[
            pltpu.VMEM((2, 4, ny, lev), BF16),
            pltpu.VMEM((2, 2, ny, lev), BF16),
            pltpu.VMEM((2, nx, 16, lev), BF16),
            pltpu.VMEM((2, 2, nx, 16, lev), BF16),
            pltpu.VMEM((8 * ny, lev), F32),
            pltpu.VMEM((4 * ny, lev), F32),
            pltpu.VMEM((2 * nx * 16, lev), F32),
            pltpu.VMEM((4 * nx * 16, lev), F32),
            pltpu.SemaphoreType.DMA((2, 4)),
        ],
    )


def sides_kernel(ey0, ey3, xprev, xnext, out0, out3, line):
    nx, lev = ey0.shape
    ny = xprev.shape[0]
    position = lax.broadcasted_iota(I32, (nx, lev), 0) & 3
    for mid, row, out in ((ey0, 0, out0), (ey3, ny - 1, out3)):
        line[pl.ds(7, 1), :] = xprev[pl.ds(row, 1), :]
        line[pl.ds(8, nx), :] = mid[...]
        line[pl.ds(8 + nx, 1), :] = xnext[pl.ds(row, 1), :]
        here = line[pl.ds(8, nx), :]
        back = 0.5 * (here + line[pl.ds(7, nx), :])
        front = 0.5 * (here + line[pl.ds(9, nx), :])
        out[...] = jnp.where(position == 3, front, jnp.where(position == 0, back, here))


def sides(ey0, ey3, xprev, xnext):
    return call(
        sides_kernel,
        [jax.ShapeDtypeStruct(ey0.shape, F32)] * 2,
        ey0, ey3, xprev, xnext,
        vmem=4, flops=10**5, moved=2 * 10**5,
        scratch_shapes=[pltpu.VMEM((ey0.shape[0] + 16, ey0.shape[1]), F32)],
    )


GROUP = 32


def pack(cap, owners_ref, slot_ref, table_ref, values_ref, low_ref, out_ref):
    cols = owners_ref.shape[1]
    lev = out_ref.shape[1]
    rows = GROUP * cap
    each = 2 * cap + 8
    owner = owners_ref[...]
    high = owner // GROUP
    place = (owner - high * GROUP) * cap + slot_ref[...]
    sub = lax.broadcasted_iota(I32, (rows, cols), 0)
    low_ref[...] = (sub == place).astype(F32).astype(BF16)
    none = jnp.zeros((rows, cols), BF16)
    high_all = jnp.broadcast_to(high.astype(F32).astype(BF16), (rows, cols))
    for i in range(table_ref.shape[0] // GROUP):
        hot = jnp.where(high_all == jnp.full((rows, cols), float(i), BF16), low_ref[...], none)
        packed = jnp.dot(hot, values_ref[...], preferred_element_type=F32)
        pieces = []
        for o in range(GROUP):
            line = table_ref[pl.ds(i * GROUP + o, 1), :]
            pieces.append(packed[o * cap : (o + 1) * cap, :lev])
            pieces.append(packed[o * cap : (o + 1) * cap, lev:])
            pieces.append(jnp.broadcast_to(line, (8, lev)))
        out_ref[pl.ds(i * GROUP * each, GROUP * each), :] = jnp.concatenate(pieces, axis=0).astype(BF16)


def cells_of(nodes, cells_ref, row, ne):
    cells = cell_pair(nodes)
    for a in range(2):
        for b in range(2):
            cells_ref[pl.ds(row + a * 2 * ne + b, ne, stride=2), :] = cells[a][b]


def columns_kernel(owners_ref, classes_ref, temper_hbm, slot_ref, table_ref, out_ref,
                   temper_ref, nodes_ref, cells_ref, sem):
    copy = pltpu.make_async_copy(temper_hbm, temper_ref, sem)
    copy.start()
    cols = owners_ref.shape[1]
    nx, ny, lev = temper_ref.shape
    ne = ny // 4
    devices = table_ref.shape[0]
    chunk = 256
    sub = lax.broadcasted_iota(I32, (devices, chunk), 0)
    upper = (
        lax.broadcasted_iota(I32, (chunk, chunk), 0) < lax.broadcasted_iota(I32, (chunk, chunk), 1)
    ).astype(F32).astype(BF16)
    ones = jnp.ones((chunk, chunk), BF16)
    running = jnp.zeros((devices, chunk), F32)
    table = jnp.zeros((devices, 128), F32)
    slots_sub = lax.broadcasted_iota(I32, (128, chunk), 0)
    for i in range(cols // chunk):
        owner = owners_ref[:, pl.ds(i * chunk, chunk)]
        hit = sub == owner
        hot = hit.astype(F32)
        hot16 = hot.astype(BF16)
        earlier = running + jnp.dot(hot16, upper, preferred_element_type=F32)
        slot = jnp.sum(jnp.where(hit, earlier, 0.0), axis=0, keepdims=True).astype(I32)
        running = running + jnp.dot(hot16, ones, preferred_element_type=F32)
        slot_ref[:, pl.ds(i * chunk, chunk)] = slot
        cost = classes_ref[:, pl.ds(i * chunk, chunk)].astype(F32)
        placed = jnp.where(slots_sub == slot, cost, 0.0).astype(BF16)
        table = table + lax.dot_general(
            hot16, placed, (((1,), (1,)), ((), ())), preferred_element_type=F32
        )
    table_ref[...] = table
    copy.wait()

    def element(e, _):
        base = pl.multiple_of(e * 4 * ny, 8)
        for x in range(4):
            nodes_ref[pl.ds(base + x * ny, ny), :] = temper_ref[4 * e + x].astype(F32)
        nodes = [
            [nodes_ref[pl.ds(base + x * ny + k, ne, stride=4), :] for k in range(4)]
            for x in range(4)
        ]
        cells_of(nodes, cells_ref, pl.multiple_of(e * ny, 8), ne)
        return 0

    lax.fori_loop(0, nx // 4, element, 0, unroll=2)
    out_ref[...] = cells_ref[...].astype(BF16)


def columns_stage(owners, classes, temper, devices):
    nx, ny, lev = temper.shape
    cols = owners.shape[1]
    return call(
        columns_kernel,
        [
            jax.ShapeDtypeStruct((1, cols), I32),
            jax.ShapeDtypeStruct((devices, 128), F32),
            jax.ShapeDtypeStruct((cols, lev), BF16),
        ],
        owners, classes, temper,
        vmem=16, flops=10**9, moved=4 * 10**6,
        in_specs=[pl.BlockSpec(memory_space=pltpu.VMEM)] * 2
        + [pl.BlockSpec(memory_space=pltpu.HBM)],
        scratch_shapes=[
            pltpu.VMEM((nx, ny, lev), BF16),
            pltpu.VMEM((nx * ny, lev), F32),
            pltpu.VMEM((nx * ny // 4, lev), F32),
            pltpu.SemaphoreType.DMA,
        ],
    )


CHUNKS = 4


def tendency_kernel(tracer_ref, winds_ref, nodes_ref, tend_ref, u_ref, v_ref):
    nx, ny, lev = tracer_ref.shape
    ne = ny // 4

    def element(e, _):
        base = pl.multiple_of(e * 4 * ny, 8)
        for x in range(4):
            nodes_ref[pl.ds(base + x * ny, ny), :] = tracer_ref[4 * e + x].astype(F32)
            u_ref[pl.ds(base + x * ny, ny), :] = winds_ref[0, 4 * e + x].astype(F32)
            v_ref[pl.ds(base + x * ny, ny), :] = winds_ref[1, 4 * e + x].astype(F32)
        for t in range(ne // 8):
            off = t * 32
            nodes = [
                [nodes_ref[pl.ds(base + x * ny + off + k, 8, stride=4), :] for k in range(4)]
                for x in range(4)
            ]
            for x in range(4):
                for k in range(4):
                    dx = combine(GRAD[x], [nodes[m][k] for m in range(4)])
                    dy = combine(GRAD[k], nodes[x])
                    u = u_ref[pl.ds(base + x * ny + off + k, 8, stride=4), :]
                    v = v_ref[pl.ds(base + x * ny + off + k, 8, stride=4), :]
                    tend_ref[pl.ds(base + x * ny + k * ne + t * 8, 8), :] = -(u * dx + v * dy)
        return 0

    lax.fori_loop(0, nx // 4, element, 0, unroll=2)


def tendency_stage(tracer, winds):
    nx, ny, lev = tracer.shape
    in_vmem = pl.BlockSpec(memory_space=pltpu.VMEM)
    return call(
        tendency_kernel,
        [jax.ShapeDtypeStruct((nx * ny, lev), F32)] * 2,
        tracer, winds,
        vmem=20, flops=2 * 10**9, moved=8 * 10**6,
        in_specs=[in_vmem] * 2,
        out_specs=[in_vmem] * 2,
        scratch_shapes=[pltpu.VMEM((nx * ny, lev), F32)] * 2,
    )


def tracer_kernel(cap, nodes_ref, tend_ref, xprev, xnext, yprev, ynext, owners_ref, slot_ref,
                  table_ref, temper_ref, new_hbm, out_ref, new_ref, fresh_ref, cells_ref,
                  values_ref, low_ref, out_sem):
    nx, ny, lev = new_ref.shape
    ne = ny // 4
    part = nx // CHUNKS
    elements = nx // 4

    def put(c):
        rows = pl.ds(c * part, part)
        return pltpu.make_async_copy(new_ref.at[rows], new_hbm.at[rows], out_sem.at[c])

    first = lax.broadcasted_iota(I32, (ne, lev), 0) == 0
    last = lax.broadcasted_iota(I32, (ne, lev), 0) == ne - 1

    def assemble(e, _):
        base = pl.multiple_of(e * 4 * ny, 8)
        back = pl.multiple_of(jnp.maximum(e * 4 - 1, 0) * ny, 8)
        front = pl.multiple_of(jnp.minimum(e * 4 + 4, nx - 1) * ny, 8)
        rounded = []
        for x in range(4):
            lines = [tend_ref[pl.ds(base + x * ny + k * ne, ne), :] for k in range(4)]
            if x == 0:
                other = [
                    jnp.where(e == 0, xprev[pl.ds(k * ne, ne), :], tend_ref[pl.ds(back + k * ne, ne), :])
                    for k in range(4)
                ]
                lines = [0.5 * (lines[k] + other[k]) for k in range(4)]
            if x == 3:
                other = [
                    jnp.where(
                        e == elements - 1,
                        xnext[pl.ds(k * ne, ne), :],
                        tend_ref[pl.ds(front + k * ne, ne), :],
                    )
                    for k in range(4)
                ]
                lines = [0.5 * (lines[k] + other[k]) for k in range(4)]
            before = yprev[pl.ds(4 * e + x, 1), :]
            after = ynext[pl.ds(4 * e + x, 1), :]
            low = jnp.where(first, before, pltpu.roll(lines[3], 1, 0))
            high = jnp.where(last, after, pltpu.roll(lines[0], ne - 1, 0))
            whole = [0.5 * (lines[0] + low), lines[1], lines[2], 0.5 * (lines[3] + high)]
            row = []
            for k in range(4):
                where = pl.ds(base + x * ny + k, ne, stride=4)
                fresh = (nodes_ref[where, :] + STEP_SIZE * whole[k]).astype(BF16).astype(F32)
                fresh_ref[where, :] = fresh
                row.append(fresh)
            rounded.append(row)
            new_ref[4 * e + x] = fresh_ref[pl.ds(base + x * ny, ny), :].astype(BF16)
        cells_of(rounded, cells_ref, pl.multiple_of(e * ny, 8), ne)
        return 0

    per = part // 4
    for c in range(CHUNKS):
        lax.fori_loop(c * per, (c + 1) * per, assemble, 0, unroll=2)
        put(c).start()
    values_ref[:, :lev] = cells_ref[...].astype(BF16)
    values_ref[:, lev:] = temper_ref[...]
    pack(cap, owners_ref, slot_ref, table_ref, values_ref, low_ref, out_ref)
    for c in range(CHUNKS):
        put(c).wait()


def tracer_stage(shape, nodes, tend, halos, owners, slots, table, temper_cells, cap):
    nx, ny, lev = shape
    cols = owners.shape[1]
    devices = table.shape[0]
    in_vmem = pl.BlockSpec(memory_space=pltpu.VMEM)
    return call(
        functools.partial(tracer_kernel, cap),
        [
            jax.ShapeDtypeStruct((nx, ny, lev), BF16),
            jax.ShapeDtypeStruct((devices * (2 * cap + 8), lev), BF16),
        ],
        nodes, tend, *halos, owners, slots, table, temper_cells,
        vmem=30, flops=4 * 10**9, moved=8 * 10**6,
        in_specs=[in_vmem] * 10,
        out_specs=[pl.BlockSpec(memory_space=pltpu.HBM), in_vmem],
        scratch_shapes=[
            pltpu.VMEM((nx, ny, lev), BF16),
            pltpu.VMEM((nx * ny, lev), F32),
            pltpu.VMEM((cols, lev), F32),
            pltpu.VMEM((cols, 2 * lev), BF16),
            pltpu.VMEM((GROUP * cap, cols), BF16),
            pltpu.SemaphoreType.DMA((CHUNKS,)),
        ],
    )


PIECES = 2


def radiate_kernel(cap, x_ref, aerosol_hbm, win_ref, wout_ref, out_ref, aerosol_ref,
                   depth_a, depth_b, trans_a, trans_b, mask_a, mask_b, sem):
    blocks, rows, width = aerosol_ref.shape
    lev = x_ref.shape[1]
    each = 2 * cap + 8
    sources = rows // cap
    piece = rows // PIECES

    def fetches(block):
        return [
            pltpu.make_async_copy(
                aerosol_hbm.at[pl.ds(block * rows + j * piece, piece)],
                aerosol_ref.at[block, pl.ds(j * piece, piece)],
                sem.at[block, j],
            )
            for j in range(PIECES)
        ]

    for block in range(blocks):
        for copy in fetches(block):
            copy.start()

    lane = lax.broadcasted_iota(I32, (8, lev), 1)
    sub = lax.broadcasted_iota(I32, (8, lev), 0)
    ones = jnp.ones((lev, lev), BF16)

    def begin(block, depth, mask):
        tracer, temper, mine = [], [], []
        for s in range(sources):
            lines = x_ref[pl.ds((block * sources + s) * each, each), :].astype(F32)
            tracer.append(lines[:cap])
            temper.append(lines[cap : 2 * cap])
            mine += [jnp.where(lane == sub + 8 * j, lines[2 * cap :], 0.0) for j in range(cap // 8)]
        state = -jnp.concatenate(
            [jnp.concatenate(tracer, axis=0), jnp.concatenate(temper, axis=0)], axis=1
        ).astype(BF16)
        mine = jnp.concatenate(mine, axis=0).astype(BF16)
        cost = jnp.dot(mine, ones, preferred_element_type=F32)
        for g in range(1, 4):
            mask[g - 1] = (cost > g - 0.5).astype(F32).astype(BF16)
        depth[...] = jnp.dot(state, win_ref[...], preferred_element_type=F32)

    def middle(block, depth, mask, trans):
        step, tile = 256, 64
        parts = width // step
        for i, r in [(i, r) for i in range(parts) for r in range(0, rows, tile)]:
            at, line = pl.ds(i * step, step), pl.ds(r, tile)
            capped = jnp.minimum(depth[line, at], 80.0)
            soft = capped - jnp.log(1.0 + jnp.exp(capped))
            kept = jnp.exp(soft * aerosol_ref[block, line, at].astype(F32)).astype(BF16)
            group = i * 4 // parts
            if group:
                kept = kept * jnp.concatenate([mask[group - 1, line]] * (step // lev), axis=1)
            trans[line, at] = kept

    def finish(block, trans):
        out_ref[pl.ds(block * rows, rows), :] = jnp.dot(
            trans[...], wout_ref[...], preferred_element_type=F32
        ).astype(BF16)

    begin(0, depth_a, mask_a)

    def pair(i, _):
        first = 2 * i
        for copy in fetches(first) + fetches(first + 1):
            copy.wait()
        begin(first + 1, depth_b, mask_b)
        finish(jnp.maximum(first - 1, 0), trans_b)
        middle(first, depth_a, mask_a, trans_a)
        begin(jnp.minimum(first + 2, blocks - 1), depth_a, mask_a)
        finish(first, trans_a)
        middle(first + 1, depth_b, mask_b, trans_b)
        return 0

    lax.fori_loop(0, blocks // 2, pair, 0)
    finish(blocks - 1, trans_b)


def radiate(arrived, aerosol, band_in, band_out, cap):
    lev = arrived.shape[1]
    rows, width = aerosol.shape
    block = 16 * cap
    in_vmem = pl.BlockSpec(memory_space=pltpu.VMEM)
    return call(
        functools.partial(radiate_kernel, cap),
        jax.ShapeDtypeStruct((rows, 2 * lev), BF16),
        arrived, aerosol, band_in, band_out,
        vmem=46, flops=7 * 10**9, moved=20 * 10**6,
        in_specs=[in_vmem, pl.BlockSpec(memory_space=pltpu.HBM), in_vmem, in_vmem],
        scratch_shapes=[
            pltpu.VMEM((rows // block, block, width), BF16),
            pltpu.VMEM((block, width), F32),
            pltpu.VMEM((block, width), F32),
            pltpu.VMEM((block, width), BF16),
            pltpu.VMEM((block, width), BF16),
            pltpu.VMEM((3, block, lev), BF16),
            pltpu.VMEM((3, block, lev), BF16),
            pltpu.SemaphoreType.DMA((rows // block, PIECES)),
        ],
    )


def gather_kernel(cap, owners_ref, slot_ref, back_ref, out_hbm, out_ref, hot_ref, sem):
    cols, rows = out_ref.shape[0], back_ref.shape[0]
    block, wide = hot_ref.shape[1], 128
    lane = lax.broadcasted_iota(I32, (wide, wide), 1)
    none = jnp.zeros((wide, wide), BF16)

    def ship(i):
        at = pl.ds(i * block, block)
        return pltpu.make_async_copy(out_ref.at[at], out_hbm.at[at], sem.at[i])

    for i in range(cols // block):
        for j in range(block // wide):
            at = pl.ds(i * block + j * wide, wide)
            line = (owners_ref[:, at] * cap + slot_ref[:, at]).astype(F32)
            place = jnp.transpose(jnp.broadcast_to(line, (wide, wide))).astype(I32)
            high = (place >> 7).astype(F32).astype(BF16)
            low = (lane == (place & (wide - 1))).astype(F32).astype(BF16)
            for r in range(rows // wide):
                here = jnp.full((wide, wide), float(r), BF16)
                hot_ref[i % 2, pl.ds(j * wide, wide), pl.ds(r * wide, wide)] = jnp.where(
                    high == here, low, none
                )
        out_ref[pl.ds(i * block, block), :] = jnp.dot(
            hot_ref[i % 2], back_ref[...], preferred_element_type=F32
        ).astype(BF16)
        ship(i).start()
    for i in range(cols // block):
        ship(i).wait()


def gather(owners, slots, back, cap):
    return call(
        functools.partial(gather_kernel, cap),
        jax.ShapeDtypeStruct((owners.shape[1], back.shape[1]), BF16),
        owners, slots, back,
        vmem=24, flops=3 * 10**9, moved=3 * 10**6,
        in_specs=[pl.BlockSpec(memory_space=pltpu.VMEM)] * 3,
        out_specs=pl.BlockSpec(memory_space=pl.ANY),
        scratch_shapes=[
            pltpu.VMEM((owners.shape[1], back.shape[1]), BF16),
            pltpu.VMEM((2, owners.shape[1] // 4, back.shape[0]), BF16),
            pltpu.SemaphoreType.DMA((4,)),
        ],
    )


def exchange(x):
    return lax.all_to_all(x, ("dyn", "col"), split_axis=0, concat_axis=0, tiled=True)


def shards(tracer, temper, winds, owners, classes, aerosol, band_in, band_out):
    n_dyn, n_col = lax.axis_size("dyn"), lax.axis_size("col")
    devices = n_dyn * n_col
    lev = tracer.shape[2]
    cap = aerosol.shape[1] // devices

    def send(x, by_dyn, by_col):
        pairs = [
            (i * n_col + j, ((i + by_dyn) % n_dyn) * n_col + (j + by_col) % n_col)
            for i in range(n_dyn)
            for j in range(n_col)
        ]
        return lax.ppermute(x, ("dyn", "col"), pairs)

    owners = owners.reshape(1, -1)
    ex0, ex3, ey0, ey3 = edges(tracer, winds)
    xprev, xnext = send(ex3, 1, 0), send(ex0, -1, 0)
    nodes, tend = tendency_stage(tracer, winds)
    slots, table, temper_cells = columns_stage(owners, classes.reshape(1, -1), temper, devices)
    side0, side3 = sides(ey0, ey3, xprev, xnext)
    yprev, ynext = send(side3, 0, 1), send(side0, 0, -1)
    tracer_new, outgoing = tracer_stage(
        tracer.shape, nodes, tend, (xprev, xnext, yprev, ynext), owners, slots, table, temper_cells, cap
    )
    each = 2 * cap + 8
    arrived = exchange(outgoing.reshape(devices, each, lev)).reshape(-1, lev)
    result = radiate(arrived, aerosol[0], band_in, band_out, cap)
    back = exchange(result.reshape(devices, cap, 2 * lev)).reshape(-1, 2 * lev)
    return (tracer_new, gather(owners, slots, back, cap))


def solution(mesh):
    return jax.shard_map(
        shards,
        mesh=mesh,
        in_specs=(
            P("dyn", "col", None),
            P("dyn", "col", None),
            P(None, "dyn", "col", None),
            P(("dyn", "col"), None),
            P(("dyn", "col")),
            P(("dyn", "col"), None, None),
            P(),
            P(),
        ),
        out_specs=(P("dyn", "col", None), P(("dyn", "col"), None)),
        check_vma=False,
    )
```

```python
import functools
import math

import jax
import jax.numpy as jnp
import numpy as np
from jax import lax
from jax.experimental import pallas as pl
from jax.experimental.pallas import tpu as pltpu
from jax.sharding import PartitionSpec as P

STEP_SIZE = 0.1
F32, BF16, I32 = jnp.float32, jnp.bfloat16, jnp.int32
MIB = 1024 * 1024
LOG2E = 1.4426950408889634


def lagrange_tables():
    points = np.array([-1.0, -1.0 / math.sqrt(5.0), 1.0 / math.sqrt(5.0), 1.0])
    products = np.array(
        [np.prod([points[r] - points[k] for k in range(4) if k != r]) for r in range(4)]
    )
    derivative = np.zeros((4, 4))
    for r in range(4):
        for c in range(4):
            if r == c:
                derivative[r, c] = np.sum(
                    [1.0 / (points[r] - points[k]) for k in range(4) if k != r]
                )
            else:
                derivative[r, c] = products[r] / (products[c] * (points[r] - points[c]))
    average = np.array([[1.0 / 6.0, 5.0 / 6.0, 0.0, 0.0], [0.0, 0.0, 5.0 / 6.0, 1.0 / 6.0]])
    return (derivative, average)


GRAD, PG2 = lagrange_tables()


def combine(weights, pieces):
    total = None
    for weight, piece in zip(weights, pieces):
        if abs(float(weight)) > 1e-12:
            term = float(weight) * piece
            total = term if total is None else total + term
    return total


def cell_pair(nodes):
    halves = [[combine(PG2[a], [nodes[x][k] for x in range(4)]) for k in range(4)] for a in range(2)]
    return [[combine(-LOG2E * PG2[b], halves[a]) for b in range(2)] for a in range(2)]


def call(kernel, out_shape, *args, vmem, flops=0, moved=0, **kw):
    return pl.pallas_call(
        kernel,
        out_shape=out_shape,
        compiler_params=pltpu.CompilerParams(vmem_limit_bytes=vmem * MIB),
        cost_estimate=pl.CostEstimate(flops=flops, bytes_accessed=moved, transcendentals=0),
        **kw,
    )(*args)


def full(shape):
    return pl.BlockSpec(shape, lambda *_: (0,) * len(shape))


def edges_kernel(tracer, winds, ex0, ex3, ey0, ey3, xs, xw, ys, yw, line, wind, strip, vstrip, sem):
    nx, ny, lev = tracer.shape
    ne = ny // 4
    copies = []
    for i, (x, x4, y) in enumerate(((0, 0, 0), (nx - 1, nx - 4, ny - 16))):
        copies.append((
            pltpu.make_async_copy(tracer.at[pl.ds(x4, 4)], xs.at[i], sem.at[i, 0]),
            pltpu.make_async_copy(winds.at[:, x], xw.at[i], sem.at[i, 1]),
            pltpu.make_async_copy(tracer.at[:, pl.ds(y, 16)], ys.at[i], sem.at[i, 2]),
            pltpu.make_async_copy(winds.at[:, :, pl.ds(y, 16)], yw.at[i], sem.at[i, 3]),
        ))
    for part in (0, 2):
        for group in copies:
            group[part].start()
            group[part + 1].start()

    for i, (node, out) in enumerate(((0, ex0), (3, ex3))):
        copies[i][0].wait()
        copies[i][1].wait()
        for x in range(4):
            line[pl.ds((4 * i + x) * ny, ny), :] = xs[i, x].astype(F32)
        for h in range(2):
            wind[pl.ds((2 * i + h) * ny, ny), :] = xw[i, h].astype(F32)
        nodes = [
            [line[pl.ds((4 * i + x) * ny + k, ne, stride=4), :] for k in range(4)] for x in range(4)
        ]
        for k in range(4):
            dx = combine(GRAD[node], [nodes[m][k] for m in range(4)])
            dy = combine(GRAD[k], nodes[node])
            u = wind[pl.ds(2 * i * ny + k, ne, stride=4), :]
            v = wind[pl.ds((2 * i + 1) * ny + k, ne, stride=4), :]
            out[pl.ds(k * ne, ne), :] = -(u * dx + v * dy)

    size = nx * 16
    for i, (base, node, out) in enumerate(((0, 0, ey0), (12, 3, ey3))):
        copies[i][2].wait()
        copies[i][3].wait()
        nel = nx // 4
        strip[pl.ds(i * size, size), :] = ys[i].astype(F32).reshape(size, lev)
        for h in range(2):
            vstrip[pl.ds((2 * i + h) * size, size), :] = yw[i, h].astype(F32).reshape(size, lev)
        nodes = [
            [strip[pl.ds(i * size + x * 16 + base + k, nel, stride=64), :] for k in range(4)]
            for x in range(4)
        ]
        for x in range(4):
            dx = combine(GRAD[x], [nodes[m][node] for m in range(4)])
            dy = combine(GRAD[node], nodes[x])
            at = x * 16 + base + node
            u = vstrip[pl.ds(2 * i * size + at, nel, stride=64), :]
            v = vstrip[pl.ds((2 * i + 1) * size + at, nel, stride=64), :]
            out[pl.ds(x, nel, stride=4), :] = -(u * dx + v * dy)


def edges(tracer, winds):
    nx, ny, lev = tracer.shape
    shapes = [(ny, lev)] * 2 + [(nx, lev)] * 2
    return call(
        edges_kernel,
        [jax.ShapeDtypeStruct(s, F32) for s in shapes],
        tracer, winds,
        vmem=53, flops=10**6, moved=3 * 10**6,
        in_specs=[pl.BlockSpec(memory_space=pltpu.HBM)] * 2,
        scratch_shapes=[
            pltpu.VMEM((2, 4, ny, lev), BF16),
            pltpu.VMEM((2, 2, ny, lev), BF16),
            pltpu.VMEM((2, nx, 16, lev), BF16),
            pltpu.VMEM((2, 2, nx, 16, lev), BF16),
            pltpu.VMEM((8 * ny, lev), F32),
            pltpu.VMEM((4 * ny, lev), F32),
            pltpu.VMEM((2 * nx * 16, lev), F32),
            pltpu.VMEM((4 * nx * 16, lev), F32),
            pltpu.SemaphoreType.DMA((2, 4)),
        ],
    )


def sides_kernel(ey0, ey3, xprev, xnext, out0, out3, line):
    nx, lev = ey0.shape
    ny = xprev.shape[0]
    position = lax.broadcasted_iota(I32, (nx, lev), 0) & 3
    for mid, row, out in ((ey0, 0, out0), (ey3, ny - 1, out3)):
        line[pl.ds(7, 1), :] = xprev[pl.ds(row, 1), :]
        line[pl.ds(8, nx), :] = mid[...]
        line[pl.ds(8 + nx, 1), :] = xnext[pl.ds(row, 1), :]
        here = line[pl.ds(8, nx), :]
        back = 0.5 * (here + line[pl.ds(7, nx), :])
        front = 0.5 * (here + line[pl.ds(9, nx), :])
        out[...] = jnp.where(position == 3, front, jnp.where(position == 0, back, here))


def sides(ey0, ey3, xprev, xnext):
    return call(
        sides_kernel,
        [jax.ShapeDtypeStruct(ey0.shape, F32)] * 2,
        ey0, ey3, xprev, xnext,
        vmem=4, flops=10**5, moved=2 * 10**5,
        scratch_shapes=[pltpu.VMEM((ey0.shape[0] + 16, ey0.shape[1]), F32)],
    )


GROUP = 32


def pack(cap, owners_ref, slot_ref, table_ref, values_ref, low_ref, out_ref):
    cols = owners_ref.shape[1]
    lev = out_ref.shape[1]
    rows = GROUP * cap
    each = 2 * cap + 8
    owner = owners_ref[...]
    high = owner // GROUP
    place = (owner - high * GROUP) * cap + slot_ref[...]
    sub = lax.broadcasted_iota(I32, (rows, cols), 0)
    low_ref[...] = (sub == place).astype(F32).astype(BF16)
    none = jnp.zeros((rows, cols), BF16)
    high_all = jnp.broadcast_to(high.astype(F32).astype(BF16), (rows, cols))
    for i in range(table_ref.shape[0] // GROUP):
        hot = jnp.where(high_all == jnp.full((rows, cols), float(i), BF16), low_ref[...], none)
        packed = jnp.dot(hot, values_ref[...], preferred_element_type=F32)
        pieces = []
        for o in range(GROUP):
            line = table_ref[pl.ds(i * GROUP + o, 1), :]
            pieces.append(packed[o * cap : (o + 1) * cap, :lev])
            pieces.append(packed[o * cap : (o + 1) * cap, lev:])
            pieces.append(jnp.broadcast_to(line, (8, lev)))
        out_ref[pl.ds(i * GROUP * each, GROUP * each), :] = jnp.concatenate(pieces, axis=0).astype(BF16)


def cells_of(nodes, cells_ref, row, ne):
    cells = cell_pair(nodes)
    for a in range(2):
        for b in range(2):
            cells_ref[pl.ds(row + a * 2 * ne + b, ne, stride=2), :] = cells[a][b]


def columns_kernel(owners_ref, classes_ref, temper_hbm, slot_ref, table_ref, out_ref,
                   temper_ref, nodes_ref, cells_ref, sem):
    copy = pltpu.make_async_copy(temper_hbm, temper_ref, sem)
    copy.start()
    cols = owners_ref.shape[1]
    nx, ny, lev = temper_ref.shape
    ne = ny // 4
    devices = table_ref.shape[0]
    chunk = 256
    sub = lax.broadcasted_iota(I32, (devices, chunk), 0)
    upper = (
        lax.broadcasted_iota(I32, (chunk, chunk), 0) < lax.broadcasted_iota(I32, (chunk, chunk), 1)
    ).astype(F32).astype(BF16)
    ones = jnp.ones((chunk, chunk), BF16)
    running = jnp.zeros((devices, chunk), F32)
    table = jnp.zeros((devices, 128), F32)
    slots_sub = lax.broadcasted_iota(I32, (128, chunk), 0)
    for i in range(cols // chunk):
        owner = owners_ref[:, pl.ds(i * chunk, chunk)]
        hit = sub == owner
        hot = hit.astype(F32)
        hot16 = hot.astype(BF16)
        earlier = running + jnp.dot(hot16, upper, preferred_element_type=F32)
        slot = jnp.sum(jnp.where(hit, earlier, 0.0), axis=0, keepdims=True).astype(I32)
        running = running + jnp.dot(hot16, ones, preferred_element_type=F32)
        slot_ref[:, pl.ds(i * chunk, chunk)] = slot
        cost = classes_ref[:, pl.ds(i * chunk, chunk)].astype(F32)
        placed = jnp.where(slots_sub == slot, cost, 0.0).astype(BF16)
        table = table + lax.dot_general(
            hot16, placed, (((1,), (1,)), ((), ())), preferred_element_type=F32
        )
    table_ref[...] = table
    copy.wait()

    def element(e, _):
        base = pl.multiple_of(e * 4 * ny, 8)
        for x in range(4):
            nodes_ref[pl.ds(base + x * ny, ny), :] = temper_ref[4 * e + x].astype(F32)
        nodes = [
            [nodes_ref[pl.ds(base + x * ny + k, ne, stride=4), :] for k in range(4)]
            for x in range(4)
        ]
        cells_of(nodes, cells_ref, pl.multiple_of(e * ny, 8), ne)
        return 0

    lax.fori_loop(0, nx // 4, element, 0, unroll=2)
    out_ref[...] = cells_ref[...].astype(BF16)


def columns_stage(owners, classes, temper, devices):
    nx, ny, lev = temper.shape
    cols = owners.shape[1]
    return call(
        columns_kernel,
        [
            jax.ShapeDtypeStruct((1, cols), I32),
            jax.ShapeDtypeStruct((devices, 128), F32),
            jax.ShapeDtypeStruct((cols, lev), BF16),
        ],
        owners, classes, temper,
        vmem=16, flops=10**9, moved=4 * 10**6,
        in_specs=[pl.BlockSpec(memory_space=pltpu.VMEM)] * 2
        + [pl.BlockSpec(memory_space=pltpu.HBM)],
        scratch_shapes=[
            pltpu.VMEM((nx, ny, lev), BF16),
            pltpu.VMEM((nx * ny, lev), F32),
            pltpu.VMEM((nx * ny // 4, lev), F32),
            pltpu.SemaphoreType.DMA,
        ],
    )


CHUNKS = 4


def tendency_kernel(tracer_ref, winds_ref, nodes_ref, tend_ref, u_ref, v_ref):
    nx, ny, lev = tracer_ref.shape
    ne = ny // 4

    def element(e, _):
        base = pl.multiple_of(e * 4 * ny, 8)
        for x in range(4):
            nodes_ref[pl.ds(base + x * ny, ny), :] = tracer_ref[4 * e + x].astype(F32)
            u_ref[pl.ds(base + x * ny, ny), :] = winds_ref[0, 4 * e + x].astype(F32)
            v_ref[pl.ds(base + x * ny, ny), :] = winds_ref[1, 4 * e + x].astype(F32)
        for t in range(ne // 8):
            off = t * 32
            nodes = [
                [nodes_ref[pl.ds(base + x * ny + off + k, 8, stride=4), :] for k in range(4)]
                for x in range(4)
            ]
            for x in range(4):
                for k in range(4):
                    dx = combine(GRAD[x], [nodes[m][k] for m in range(4)])
                    dy = combine(GRAD[k], nodes[x])
                    u = u_ref[pl.ds(base + x * ny + off + k, 8, stride=4), :]
                    v = v_ref[pl.ds(base + x * ny + off + k, 8, stride=4), :]
                    tend_ref[pl.ds(base + x * ny + k * ne + t * 8, 8), :] = -(u * dx + v * dy)
        return 0

    lax.fori_loop(0, nx // 4, element, 0, unroll=2)


def tendency_stage(tracer, winds):
    nx, ny, lev = tracer.shape
    in_vmem = pl.BlockSpec(memory_space=pltpu.VMEM)
    return call(
        tendency_kernel,
        [jax.ShapeDtypeStruct((nx * ny, lev), F32)] * 2,
        tracer, winds,
        vmem=20, flops=2 * 10**9, moved=8 * 10**6,
        in_specs=[in_vmem] * 2,
        out_specs=[in_vmem] * 2,
        scratch_shapes=[pltpu.VMEM((nx * ny, lev), F32)] * 2,
    )


def tracer_kernel(cap, nodes_ref, tend_ref, xprev, xnext, yprev, ynext, owners_ref, slot_ref,
                  table_ref, temper_ref, new_hbm, out_ref, new_ref, fresh_ref, cells_ref,
                  values_ref, low_ref, out_sem):
    nx, ny, lev = new_ref.shape
    ne = ny // 4
    part = nx // CHUNKS
    elements = nx // 4

    def put(c):
        rows = pl.ds(c * part, part)
        return pltpu.make_async_copy(new_ref.at[rows], new_hbm.at[rows], out_sem.at[c])

    first = lax.broadcasted_iota(I32, (ne, lev), 0) == 0
    last = lax.broadcasted_iota(I32, (ne, lev), 0) == ne - 1

    def assemble(e, _):
        base = pl.multiple_of(e * 4 * ny, 8)
        back = pl.multiple_of(jnp.maximum(e * 4 - 1, 0) * ny, 8)
        front = pl.multiple_of(jnp.minimum(e * 4 + 4, nx - 1) * ny, 8)
        rounded = []
        for x in range(4):
            lines = [tend_ref[pl.ds(base + x * ny + k * ne, ne), :] for k in range(4)]
            if x == 0:
                other = [
                    jnp.where(e == 0, xprev[pl.ds(k * ne, ne), :], tend_ref[pl.ds(back + k * ne, ne), :])
                    for k in range(4)
                ]
                lines = [0.5 * (lines[k] + other[k]) for k in range(4)]
            if x == 3:
                other = [
                    jnp.where(
                        e == elements - 1,
                        xnext[pl.ds(k * ne, ne), :],
                        tend_ref[pl.ds(front + k * ne, ne), :],
                    )
                    for k in range(4)
                ]
                lines = [0.5 * (lines[k] + other[k]) for k in range(4)]
            before = yprev[pl.ds(4 * e + x, 1), :]
            after = ynext[pl.ds(4 * e + x, 1), :]
            low = jnp.where(first, before, pltpu.roll(lines[3], 1, 0))
            high = jnp.where(last, after, pltpu.roll(lines[0], ne - 1, 0))
            whole = [0.5 * (lines[0] + low), lines[1], lines[2], 0.5 * (lines[3] + high)]
            row = []
            for k in range(4):
                where = pl.ds(base + x * ny + k, ne, stride=4)
                fresh = (nodes_ref[where, :] + STEP_SIZE * whole[k]).astype(BF16).astype(F32)
                fresh_ref[where, :] = fresh
                row.append(fresh)
            rounded.append(row)
            new_ref[4 * e + x] = fresh_ref[pl.ds(base + x * ny, ny), :].astype(BF16)
        cells_of(rounded, cells_ref, pl.multiple_of(e * ny, 8), ne)
        return 0

    per = part // 4
    for c in range(CHUNKS):
        lax.fori_loop(c * per, (c + 1) * per, assemble, 0, unroll=2)
        put(c).start()
    values_ref[:, :lev] = cells_ref[...].astype(BF16)
    values_ref[:, lev:] = temper_ref[...]
    pack(cap, owners_ref, slot_ref, table_ref, values_ref, low_ref, out_ref)
    for c in range(CHUNKS):
        put(c).wait()


def tracer_stage(shape, nodes, tend, halos, owners, slots, table, temper_cells, cap):
    nx, ny, lev = shape
    cols = owners.shape[1]
    devices = table.shape[0]
    in_vmem = pl.BlockSpec(memory_space=pltpu.VMEM)
    return call(
        functools.partial(tracer_kernel, cap),
        [
            jax.ShapeDtypeStruct((nx, ny, lev), BF16),
            jax.ShapeDtypeStruct((devices * (2 * cap + 8), lev), BF16),
        ],
        nodes, tend, *halos, owners, slots, table, temper_cells,
        vmem=30, flops=4 * 10**9, moved=8 * 10**6,
        in_specs=[in_vmem] * 10,
        out_specs=[pl.BlockSpec(memory_space=pltpu.HBM), in_vmem],
        scratch_shapes=[
            pltpu.VMEM((nx, ny, lev), BF16),
            pltpu.VMEM((nx * ny, lev), F32),
            pltpu.VMEM((cols, lev), F32),
            pltpu.VMEM((cols, 2 * lev), BF16),
            pltpu.VMEM((GROUP * cap, cols), BF16),
            pltpu.SemaphoreType.DMA((CHUNKS,)),
        ],
    )


PIECES = 2


def radiate_kernel(cap, x_ref, aerosol_hbm, win_ref, wout_ref, out_ref, aerosol_ref,
                   depth_a, depth_b, trans_a, trans_b, bound_a, bound_b, sem):
    blocks, rows, width = aerosol_ref.shape
    lev = x_ref.shape[1]
    each = 2 * cap + 8
    sources = rows // cap
    piece = rows // PIECES

    def fetches(block):
        return [
            pltpu.make_async_copy(
                aerosol_hbm.at[pl.ds(block * rows + j * piece, piece)],
                aerosol_ref.at[block, pl.ds(j * piece, piece)],
                sem.at[block, j],
            )
            for j in range(PIECES)
        ]

    for block in range(blocks):
        for copy in fetches(block):
            copy.start()

    lane = lax.broadcasted_iota(I32, (8, lev), 1)
    sub = lax.broadcasted_iota(I32, (8, lev), 0)
    ones = jnp.ones((lev, lev), BF16)

    def begin(block, depth, bound):
        tracer, temper, mine = [], [], []
        for s in range(sources):
            lines = x_ref[pl.ds((block * sources + s) * each, each), :].astype(F32)
            tracer.append(lines[:cap])
            temper.append(lines[cap : 2 * cap])
            mine += [jnp.where(lane == sub + 8 * j, lines[2 * cap :], 0.0) for j in range(cap // 8)]
        state = jnp.concatenate(
            [jnp.concatenate(tracer, axis=0), jnp.concatenate(temper, axis=0)], axis=1
        ).astype(BF16)
        mine = jnp.concatenate(mine, axis=0).astype(BF16)
        cost = jnp.dot(mine, ones, preferred_element_type=F32)
        for g in range(1, 4):
            bound[g - 1] = jnp.where(cost > g - 0.5, 120.0, -1e30)
        depth[...] = jnp.dot(state, win_ref[...], preferred_element_type=F32)

    def middle(block, depth, bound, trans):
        step, tile = 256, 64
        parts = width // step
        for i, r in [(i, r) for i in range(parts) for r in range(0, rows, tile)]:
            at, line = pl.ds(i * step, step), pl.ds(r, tile)
            group = i * 4 // parts
            top = jnp.concatenate([bound[group - 1, line]] * (step // lev), axis=1) if group else 120.0
            capped = jnp.minimum(depth[line, at], top)
            soft = capped - jnp.log2(1.0 + jnp.exp2(capped))
            kept = jnp.exp2(soft * aerosol_ref[block, line, at].astype(F32)).astype(BF16)
            trans[line, at] = kept

    def finish(block, trans):
        out_ref[pl.ds(block * rows, rows), :] = jnp.dot(
            trans[...], wout_ref[...], preferred_element_type=F32
        ).astype(BF16)

    begin(0, depth_a, bound_a)

    def pair(i, _):
        first = 2 * i
        for copy in fetches(first):
            copy.wait()
        begin(first + 1, depth_b, bound_b)
        finish(jnp.maximum(first - 1, 0), trans_b)
        middle(first, depth_a, bound_a, trans_a)
        for copy in fetches(first + 1):
            copy.wait()
        begin(jnp.minimum(first + 2, blocks - 1), depth_a, bound_a)
        finish(first, trans_a)
        middle(first + 1, depth_b, bound_b, trans_b)
        return 0

    lax.fori_loop(0, blocks // 2, pair, 0)
    finish(blocks - 1, trans_b)


def radiate(arrived, aerosol, band_in, band_out, cap):
    lev = arrived.shape[1]
    rows, width = aerosol.shape
    block = 16 * cap
    in_vmem = pl.BlockSpec(memory_space=pltpu.VMEM)
    return call(
        functools.partial(radiate_kernel, cap),
        jax.ShapeDtypeStruct((rows, 2 * lev), BF16),
        arrived, aerosol, band_in, band_out,
        vmem=46, flops=7 * 10**9, moved=20 * 10**6,
        in_specs=[in_vmem, pl.BlockSpec(memory_space=pltpu.HBM), in_vmem, in_vmem],
        scratch_shapes=[
            pltpu.VMEM((rows // block, block, width), BF16),
            pltpu.VMEM((block, width), F32),
            pltpu.VMEM((block, width), F32),
            pltpu.VMEM((block, width), BF16),
            pltpu.VMEM((block, width), BF16),
            pltpu.VMEM((3, block, lev), F32),
            pltpu.VMEM((3, block, lev), F32),
            pltpu.SemaphoreType.DMA((rows // block, PIECES)),
        ],
    )


def gather_kernel(cap, owners_ref, slot_ref, back_ref, out_hbm, out_ref, hot_ref, sem):
    cols, rows = out_ref.shape[0], back_ref.shape[0]
    block, wide = hot_ref.shape[1], 128
    lane = lax.broadcasted_iota(I32, (wide, wide), 1)
    none = jnp.zeros((wide, wide), BF16)

    def ship(i):
        at = pl.ds(i * block, block)
        return pltpu.make_async_copy(out_ref.at[at], out_hbm.at[at], sem.at[i])

    for i in range(cols // block):
        for j in range(block // wide):
            at = pl.ds(i * block + j * wide, wide)
            line = (owners_ref[:, at] * cap + slot_ref[:, at]).astype(F32)
            place = jnp.transpose(jnp.broadcast_to(line, (wide, wide))).astype(I32)
            high = (place >> 7).astype(F32).astype(BF16)
            low = (lane == (place & (wide - 1))).astype(F32).astype(BF16)
            for r in range(rows // wide):
                here = jnp.full((wide, wide), float(r), BF16)
                hot_ref[i % 2, pl.ds(j * wide, wide), pl.ds(r * wide, wide)] = jnp.where(
                    high == here, low, none
                )
        out_ref[pl.ds(i * block, block), :] = jnp.dot(
            hot_ref[i % 2], back_ref[...], preferred_element_type=F32
        ).astype(BF16)
        ship(i).start()
    for i in range(cols // block):
        ship(i).wait()


def gather(owners, slots, back, cap):
    return call(
        functools.partial(gather_kernel, cap),
        jax.ShapeDtypeStruct((owners.shape[1], back.shape[1]), BF16),
        owners, slots, back,
        vmem=24, flops=3 * 10**9, moved=3 * 10**6,
        in_specs=[pl.BlockSpec(memory_space=pltpu.VMEM)] * 3,
        out_specs=pl.BlockSpec(memory_space=pl.ANY),
        scratch_shapes=[
            pltpu.VMEM((owners.shape[1], back.shape[1]), BF16),
            pltpu.VMEM((2, owners.shape[1] // 4, back.shape[0]), BF16),
            pltpu.SemaphoreType.DMA((4,)),
        ],
    )


def exchange(x):
    return lax.all_to_all(x, ("dyn", "col"), split_axis=0, concat_axis=0, tiled=True)


def shards(tracer, temper, winds, owners, classes, aerosol, band_in, band_out):
    n_dyn, n_col = lax.axis_size("dyn"), lax.axis_size("col")
    devices = n_dyn * n_col
    lev = tracer.shape[2]
    cap = aerosol.shape[1] // devices

    def send(x, by_dyn, by_col):
        pairs = [
            (i * n_col + j, ((i + by_dyn) % n_dyn) * n_col + (j + by_col) % n_col)
            for i in range(n_dyn)
            for j in range(n_col)
        ]
        return lax.ppermute(x, ("dyn", "col"), pairs)

    owners = owners.reshape(1, -1)
    ex0, ex3, ey0, ey3 = edges(tracer, winds)
    xprev, xnext = send(ex3, 1, 0), send(ex0, -1, 0)
    nodes, tend = tendency_stage(tracer, winds)
    slots, table, temper_cells = columns_stage(owners, classes.reshape(1, -1), temper, devices)
    side0, side3 = sides(ey0, ey3, xprev, xnext)
    yprev, ynext = send(side3, 0, 1), send(side0, 0, -1)
    tracer_new, outgoing = tracer_stage(
        tracer.shape, nodes, tend, (xprev, xnext, yprev, ynext), owners, slots, table, temper_cells, cap
    )
    each = 2 * cap + 8
    arrived = exchange(outgoing.reshape(devices, each, lev)).reshape(-1, lev)
    result = radiate(arrived, aerosol[0], band_in, band_out, cap)
    back = exchange(result.reshape(devices, cap, 2 * lev)).reshape(-1, 2 * lev)
    return (tracer_new, gather(owners, slots, back, cap))


def solution(mesh):
    return jax.shard_map(
        shards,
        mesh=mesh,
        in_specs=(
            P("dyn", "col", None),
            P("dyn", "col", None),
            P(None, "dyn", "col", None),
            P(("dyn", "col"), None),
            P(("dyn", "col")),
            P(("dyn", "col"), None, None),
            P(),
            P(),
        ),
        out_specs=(P("dyn", "col", None), P(("dyn", "col"), None)),
        check_vma=False,
    )
```

```python
import functools
import math

import jax
import jax.numpy as jnp
import numpy as np
from jax import lax
from jax.experimental import pallas as pl
from jax.experimental.pallas import tpu as pltpu
from jax.sharding import PartitionSpec as P

STEP_SIZE = 0.1
F32, BF16, I32 = jnp.float32, jnp.bfloat16, jnp.int32
MIB = 1024 * 1024
LOG2E = 1.4426950408889634


def lagrange_tables():
    points = np.array([-1.0, -1.0 / math.sqrt(5.0), 1.0 / math.sqrt(5.0), 1.0])
    products = np.array(
        [np.prod([points[r] - points[k] for k in range(4) if k != r]) for r in range(4)]
    )
    derivative = np.zeros((4, 4))
    for r in range(4):
        for c in range(4):
            if r == c:
                derivative[r, c] = np.sum(
                    [1.0 / (points[r] - points[k]) for k in range(4) if k != r]
                )
            else:
                derivative[r, c] = products[r] / (products[c] * (points[r] - points[c]))
    average = np.array([[1.0 / 6.0, 5.0 / 6.0, 0.0, 0.0], [0.0, 0.0, 5.0 / 6.0, 1.0 / 6.0]])
    return (derivative, average)


GRAD, PG2 = lagrange_tables()


def combine(weights, pieces):
    total = None
    for weight, piece in zip(weights, pieces):
        if abs(float(weight)) > 1e-12:
            term = float(weight) * piece
            total = term if total is None else total + term
    return total


def cell_pair(nodes):
    halves = [[combine(PG2[a], [nodes[x][k] for x in range(4)]) for k in range(4)] for a in range(2)]
    return [[combine(PG2[b], halves[a]) for b in range(2)] for a in range(2)]


def call(kernel, out_shape, *args, vmem, flops=0, moved=0, **kw):
    return pl.pallas_call(
        kernel,
        out_shape=out_shape,
        compiler_params=pltpu.CompilerParams(vmem_limit_bytes=vmem * MIB),
        cost_estimate=pl.CostEstimate(flops=flops, bytes_accessed=moved, transcendentals=0),
        **kw,
    )(*args)


def full(shape):
    return pl.BlockSpec(shape, lambda *_: (0,) * len(shape))


def edges_kernel(tracer, winds, ex0, ex3, ey0, ey3, xs, xw, ys, yw, line, wind, strip, vstrip, sem):
    nx, ny, lev = tracer.shape
    ne = ny // 4
    copies = []
    for i, (x, x4, y) in enumerate(((0, 0, 0), (nx - 1, nx - 4, ny - 16))):
        copies.append((
            pltpu.make_async_copy(tracer.at[pl.ds(x4, 4)], xs.at[i], sem.at[i, 0]),
            pltpu.make_async_copy(winds.at[:, x], xw.at[i], sem.at[i, 1]),
            pltpu.make_async_copy(tracer.at[:, pl.ds(y, 16)], ys.at[i], sem.at[i, 2]),
            pltpu.make_async_copy(winds.at[:, :, pl.ds(y, 16)], yw.at[i], sem.at[i, 3]),
        ))
    for part in (0, 2):
        for group in copies:
            group[part].start()
            group[part + 1].start()

    for i, (node, out) in enumerate(((0, ex0), (3, ex3))):
        copies[i][0].wait()
        copies[i][1].wait()
        for x in range(4):
            line[pl.ds((4 * i + x) * ny, ny), :] = xs[i, x].astype(F32)
        for h in range(2):
            wind[pl.ds((2 * i + h) * ny, ny), :] = xw[i, h].astype(F32)
        nodes = [
            [line[pl.ds((4 * i + x) * ny + k, ne, stride=4), :] for k in range(4)] for x in range(4)
        ]
        for k in range(4):
            dx = combine(GRAD[node], [nodes[m][k] for m in range(4)])
            dy = combine(GRAD[k], nodes[node])
            u = wind[pl.ds(2 * i * ny + k, ne, stride=4), :]
            v = wind[pl.ds((2 * i + 1) * ny + k, ne, stride=4), :]
            out[pl.ds(k * ne, ne), :] = -(u * dx + v * dy)

    size = nx * 16
    for i, (base, node, out) in enumerate(((0, 0, ey0), (12, 3, ey3))):
        copies[i][2].wait()
        copies[i][3].wait()
        nel = nx // 4
        strip[pl.ds(i * size, size), :] = ys[i].astype(F32).reshape(size, lev)
        for h in range(2):
            vstrip[pl.ds((2 * i + h) * size, size), :] = yw[i, h].astype(F32).reshape(size, lev)
        nodes = [
            [strip[pl.ds(i * size + x * 16 + base + k, nel, stride=64), :] for k in range(4)]
            for x in range(4)
        ]
        for x in range(4):
            dx = combine(GRAD[x], [nodes[m][node] for m in range(4)])
            dy = combine(GRAD[node], nodes[x])
            at = x * 16 + base + node
            u = vstrip[pl.ds(2 * i * size + at, nel, stride=64), :]
            v = vstrip[pl.ds((2 * i + 1) * size + at, nel, stride=64), :]
            out[pl.ds(x, nel, stride=4), :] = -(u * dx + v * dy)


def edges(tracer, winds):
    nx, ny, lev = tracer.shape
    shapes = [(ny, lev)] * 2 + [(nx, lev)] * 2
    return call(
        edges_kernel,
        [jax.ShapeDtypeStruct(s, F32) for s in shapes],
        tracer, winds,
        vmem=53, flops=10**6, moved=3 * 10**6,
        in_specs=[pl.BlockSpec(memory_space=pltpu.HBM)] * 2,
        scratch_shapes=[
            pltpu.VMEM((2, 4, ny, lev), BF16),
            pltpu.VMEM((2, 2, ny, lev), BF16),
            pltpu.VMEM((2, nx, 16, lev), BF16),
            pltpu.VMEM((2, 2, nx, 16, lev), BF16),
            pltpu.VMEM((8 * ny, lev), F32),
            pltpu.VMEM((4 * ny, lev), F32),
            pltpu.VMEM((2 * nx * 16, lev), F32),
            pltpu.VMEM((4 * nx * 16, lev), F32),
            pltpu.SemaphoreType.DMA((2, 4)),
        ],
    )


def sides_kernel(ey0, ey3, xprev, xnext, out0, out3, line):
    nx, lev = ey0.shape
    ny = xprev.shape[0]
    position = lax.broadcasted_iota(I32, (nx, lev), 0) & 3
    for mid, row, out in ((ey0, 0, out0), (ey3, ny - 1, out3)):
        line[pl.ds(7, 1), :] = xprev[pl.ds(row, 1), :]
        line[pl.ds(8, nx), :] = mid[...]
        line[pl.ds(8 + nx, 1), :] = xnext[pl.ds(row, 1), :]
        here = line[pl.ds(8, nx), :]
        back = 0.5 * (here + line[pl.ds(7, nx), :])
        front = 0.5 * (here + line[pl.ds(9, nx), :])
        out[...] = jnp.where(position == 3, front, jnp.where(position == 0, back, here))


def sides(ey0, ey3, xprev, xnext):
    return call(
        sides_kernel,
        [jax.ShapeDtypeStruct(ey0.shape, F32)] * 2,
        ey0, ey3, xprev, xnext,
        vmem=4, flops=10**5, moved=2 * 10**5,
        scratch_shapes=[pltpu.VMEM((ey0.shape[0] + 16, ey0.shape[1]), F32)],
    )


GROUP = 32


def pack(cap, owners_ref, slot_ref, table_ref, values_ref, low_ref, out_ref):
    cols = owners_ref.shape[1]
    lev = out_ref.shape[1]
    rows = GROUP * cap
    each = 2 * cap + 8
    owner = owners_ref[...]
    high = owner // GROUP
    place = (owner - high * GROUP) * cap + slot_ref[...]
    sub = lax.broadcasted_iota(I32, (rows, cols), 0)
    low_ref[...] = (sub == place).astype(F32).astype(BF16)
    none = jnp.zeros((rows, cols), BF16)
    high_all = jnp.broadcast_to(high.astype(F32).astype(BF16), (rows, cols))
    for i in range(table_ref.shape[0] // GROUP):
        hot = jnp.where(high_all == jnp.full((rows, cols), float(i), BF16), low_ref[...], none)
        packed = jnp.dot(hot, values_ref[...], preferred_element_type=F32)
        pieces = []
        for o in range(GROUP):
            line = table_ref[pl.ds(i * GROUP + o, 1), :]
            pieces.append(packed[o * cap : (o + 1) * cap, :lev])
            pieces.append(packed[o * cap : (o + 1) * cap, lev:])
            pieces.append(jnp.broadcast_to(line, (8, lev)))
        out_ref[pl.ds(i * GROUP * each, GROUP * each), :] = jnp.concatenate(pieces, axis=0).astype(BF16)


def cells_of(nodes, cells_ref, row, ne):
    cells = cell_pair(nodes)
    for a in range(2):
        for b in range(2):
            cells_ref[pl.ds(row + a * 2 * ne + b, ne, stride=2), :] = cells[a][b]


def columns_kernel(owners_ref, classes_ref, temper_hbm, slot_ref, table_ref, out_ref,
                   temper_ref, nodes_ref, cells_ref, sem):
    copy = pltpu.make_async_copy(temper_hbm, temper_ref, sem)
    copy.start()
    cols = owners_ref.shape[1]
    nx, ny, lev = temper_ref.shape
    ne = ny // 4
    devices = table_ref.shape[0]
    chunk = 256
    sub = lax.broadcasted_iota(I32, (devices, chunk), 0)
    upper = (
        lax.broadcasted_iota(I32, (chunk, chunk), 0) < lax.broadcasted_iota(I32, (chunk, chunk), 1)
    ).astype(F32).astype(BF16)
    ones = jnp.ones((chunk, chunk), BF16)
    running = jnp.zeros((devices, chunk), F32)
    table = jnp.zeros((devices, 128), F32)
    slots_sub = lax.broadcasted_iota(I32, (128, chunk), 0)
    for i in range(cols // chunk):
        owner = owners_ref[:, pl.ds(i * chunk, chunk)]
        hit = sub == owner
        hot = hit.astype(F32)
        hot16 = hot.astype(BF16)
        earlier = running + jnp.dot(hot16, upper, preferred_element_type=F32)
        slot = jnp.sum(jnp.where(hit, earlier, 0.0), axis=0, keepdims=True).astype(I32)
        running = running + jnp.dot(hot16, ones, preferred_element_type=F32)
        slot_ref[:, pl.ds(i * chunk, chunk)] = slot
        cost = classes_ref[:, pl.ds(i * chunk, chunk)].astype(F32)
        placed = jnp.where(slots_sub == slot, cost, 0.0).astype(BF16)
        table = table + lax.dot_general(
            hot16, placed, (((1,), (1,)), ((), ())), preferred_element_type=F32
        )
    table_ref[...] = table
    copy.wait()

    def element(e, _):
        base = pl.multiple_of(e * 4 * ny, 8)
        for x in range(4):
            nodes_ref[pl.ds(base + x * ny, ny), :] = temper_ref[4 * e + x].astype(F32)
        nodes = [
            [nodes_ref[pl.ds(base + x * ny + k, ne, stride=4), :] for k in range(4)]
            for x in range(4)
        ]
        cells_of(nodes, cells_ref, pl.multiple_of(e * ny, 8), ne)
        return 0

    lax.fori_loop(0, nx // 4, element, 0, unroll=2)
    out_ref[...] = cells_ref[...].astype(BF16)


def columns_stage(owners, classes, temper, devices):
    nx, ny, lev = temper.shape
    cols = owners.shape[1]
    return call(
        columns_kernel,
        [
            jax.ShapeDtypeStruct((1, cols), I32),
            jax.ShapeDtypeStruct((devices, 128), F32),
            jax.ShapeDtypeStruct((cols, lev), BF16),
        ],
        owners, classes, temper,
        vmem=16, flops=10**9, moved=4 * 10**6,
        in_specs=[pl.BlockSpec(memory_space=pltpu.VMEM)] * 2
        + [pl.BlockSpec(memory_space=pltpu.HBM)],
        scratch_shapes=[
            pltpu.VMEM((nx, ny, lev), BF16),
            pltpu.VMEM((nx * ny, lev), F32),
            pltpu.VMEM((nx * ny // 4, lev), F32),
            pltpu.SemaphoreType.DMA,
        ],
    )


CHUNKS = 4


def tendency_kernel(tracer_ref, winds_ref, nodes_ref, tend_ref, u_ref, v_ref):
    nx, ny, lev = tracer_ref.shape
    ne = ny // 4

    def element(e, _):
        base = pl.multiple_of(e * 4 * ny, 8)
        for x in range(4):
            nodes_ref[pl.ds(base + x * ny, ny), :] = tracer_ref[4 * e + x].astype(F32)
            u_ref[pl.ds(base + x * ny, ny), :] = winds_ref[0, 4 * e + x].astype(F32)
            v_ref[pl.ds(base + x * ny, ny), :] = winds_ref[1, 4 * e + x].astype(F32)
        for t in range(ne // 8):
            off = t * 32
            nodes = [
                [nodes_ref[pl.ds(base + x * ny + off + k, 8, stride=4), :] for k in range(4)]
                for x in range(4)
            ]
            for x in range(4):
                for k in range(4):
                    dx = combine(GRAD[x], [nodes[m][k] for m in range(4)])
                    dy = combine(GRAD[k], nodes[x])
                    u = u_ref[pl.ds(base + x * ny + off + k, 8, stride=4), :]
                    v = v_ref[pl.ds(base + x * ny + off + k, 8, stride=4), :]
                    tend_ref[pl.ds(base + x * ny + k * ne + t * 8, 8), :] = -(u * dx + v * dy)
        return 0

    lax.fori_loop(0, nx // 4, element, 0, unroll=2)


def tendency_stage(tracer, winds):
    nx, ny, lev = tracer.shape
    in_vmem = pl.BlockSpec(memory_space=pltpu.VMEM)
    return call(
        tendency_kernel,
        [jax.ShapeDtypeStruct((nx * ny, lev), F32)] * 2,
        tracer, winds,
        vmem=20, flops=2 * 10**9, moved=8 * 10**6,
        in_specs=[in_vmem] * 2,
        out_specs=[in_vmem] * 2,
        scratch_shapes=[pltpu.VMEM((nx * ny, lev), F32)] * 2,
    )


def tracer_kernel(cap, nodes_ref, tend_ref, xprev, xnext, yprev, ynext, owners_ref, slot_ref,
                  table_ref, temper_ref, new_hbm, out_ref, new_ref, fresh_ref, cells_ref,
                  values_ref, low_ref, out_sem):
    nx, ny, lev = new_ref.shape
    ne = ny // 4
    part = nx // CHUNKS
    elements = nx // 4

    def put(c):
        rows = pl.ds(c * part, part)
        return pltpu.make_async_copy(new_ref.at[rows], new_hbm.at[rows], out_sem.at[c])

    first = lax.broadcasted_iota(I32, (ne, lev), 0) == 0
    last = lax.broadcasted_iota(I32, (ne, lev), 0) == ne - 1

    def assemble(e, _):
        base = pl.multiple_of(e * 4 * ny, 8)
        back = pl.multiple_of(jnp.maximum(e * 4 - 1, 0) * ny, 8)
        front = pl.multiple_of(jnp.minimum(e * 4 + 4, nx - 1) * ny, 8)
        rounded = []
        for x in range(4):
            lines = [tend_ref[pl.ds(base + x * ny + k * ne, ne), :] for k in range(4)]
            if x == 0:
                other = [
                    jnp.where(e == 0, xprev[pl.ds(k * ne, ne), :], tend_ref[pl.ds(back + k * ne, ne), :])
                    for k in range(4)
                ]
                lines = [0.5 * (lines[k] + other[k]) for k in range(4)]
            if x == 3:
                other = [
                    jnp.where(
                        e == elements - 1,
                        xnext[pl.ds(k * ne, ne), :],
                        tend_ref[pl.ds(front + k * ne, ne), :],
                    )
                    for k in range(4)
                ]
                lines = [0.5 * (lines[k] + other[k]) for k in range(4)]
            before = yprev[pl.ds(4 * e + x, 1), :]
            after = ynext[pl.ds(4 * e + x, 1), :]
            low = jnp.where(first, before, pltpu.roll(lines[3], 1, 0))
            high = jnp.where(last, after, pltpu.roll(lines[0], ne - 1, 0))
            whole = [0.5 * (lines[0] + low), lines[1], lines[2], 0.5 * (lines[3] + high)]
            row = []
            for k in range(4):
                where = pl.ds(base + x * ny + k, ne, stride=4)
                fresh = (nodes_ref[where, :] + STEP_SIZE * whole[k]).astype(BF16).astype(F32)
                fresh_ref[where, :] = fresh
                row.append(fresh)
            rounded.append(row)
            new_ref[4 * e + x] = fresh_ref[pl.ds(base + x * ny, ny), :].astype(BF16)
        cells_of(rounded, cells_ref, pl.multiple_of(e * ny, 8), ne)
        return 0

    per = part // 4
    for c in range(CHUNKS):
        lax.fori_loop(c * per, (c + 1) * per, assemble, 0, unroll=2)
        put(c).start()
    values_ref[:, :lev] = cells_ref[...].astype(BF16)
    values_ref[:, lev:] = temper_ref[...]
    pack(cap, owners_ref, slot_ref, table_ref, values_ref, low_ref, out_ref)
    for c in range(CHUNKS):
        put(c).wait()


def tracer_stage(shape, nodes, tend, halos, owners, slots, table, temper_cells, cap):
    nx, ny, lev = shape
    cols = owners.shape[1]
    devices = table.shape[0]
    in_vmem = pl.BlockSpec(memory_space=pltpu.VMEM)
    return call(
        functools.partial(tracer_kernel, cap),
        [
            jax.ShapeDtypeStruct((nx, ny, lev), BF16),
            jax.ShapeDtypeStruct((devices * (2 * cap + 8), lev), BF16),
        ],
        nodes, tend, *halos, owners, slots, table, temper_cells,
        vmem=30, flops=4 * 10**9, moved=8 * 10**6,
        in_specs=[in_vmem] * 10,
        out_specs=[pl.BlockSpec(memory_space=pltpu.HBM), in_vmem],
        scratch_shapes=[
            pltpu.VMEM((nx, ny, lev), BF16),
            pltpu.VMEM((nx * ny, lev), F32),
            pltpu.VMEM((cols, lev), F32),
            pltpu.VMEM((cols, 2 * lev), BF16),
            pltpu.VMEM((GROUP * cap, cols), BF16),
            pltpu.SemaphoreType.DMA((CHUNKS,)),
        ],
    )


PIECES = 2


def radiate_kernel(cap, x_ref, aerosol_hbm, win_ref, wout_ref, out_ref, aerosol_ref, scaled_ref,
                   depth_a, depth_b, trans_a, trans_b, bound_a, bound_b, sem):
    blocks, rows, width = aerosol_ref.shape
    lev = x_ref.shape[1]
    each = 2 * cap + 8
    sources = rows // cap
    piece = rows // PIECES

    def fetches(block):
        return [
            pltpu.make_async_copy(
                aerosol_hbm.at[pl.ds(block * rows + j * piece, piece)],
                aerosol_ref.at[block, pl.ds(j * piece, piece)],
                sem.at[block, j],
            )
            for j in range(PIECES)
        ]

    for block in range(blocks):
        for copy in fetches(block):
            copy.start()

    deep = win_ref.shape[0]
    for r in range(0, deep, 32):
        weight = win_ref[pl.ds(r, 32), :].astype(F32) * -LOG2E
        high = weight.astype(BF16)
        scaled_ref[pl.ds(r, 32), :] = high
        scaled_ref[pl.ds(deep + r, 32), :] = (weight - high.astype(F32)).astype(BF16)

    lane = lax.broadcasted_iota(I32, (8, lev), 1)
    sub = lax.broadcasted_iota(I32, (8, lev), 0)
    ones = jnp.ones((lev, lev), BF16)

    def begin(block, depth, bound):
        tracer, temper, mine = [], [], []
        for s in range(sources):
            lines = x_ref[pl.ds((block * sources + s) * each, each), :].astype(F32)
            tracer.append(lines[:cap])
            temper.append(lines[cap : 2 * cap])
            mine += [jnp.where(lane == sub + 8 * j, lines[2 * cap :], 0.0) for j in range(cap // 8)]
        state = jnp.concatenate(
            [jnp.concatenate(tracer, axis=0), jnp.concatenate(temper, axis=0)], axis=1
        ).astype(BF16)
        state = jnp.concatenate([state, state], axis=1)
        mine = jnp.concatenate(mine, axis=0).astype(BF16)
        cost = jnp.dot(mine, ones, preferred_element_type=F32)
        for g in range(1, 4):
            bound[g - 1] = jnp.where(cost > g - 0.5, 120.0, -1e30)
        depth[...] = jnp.dot(state, scaled_ref[...], preferred_element_type=F32)

    def middle(block, depth, bound, trans):
        step, tile = 256, 64
        parts = width // step
        for i, r in [(i, r) for i in range(parts) for r in range(0, rows, tile)]:
            at, line = pl.ds(i * step, step), pl.ds(r, tile)
            group = i * 4 // parts
            top = jnp.concatenate([bound[group - 1, line]] * (step // lev), axis=1) if group else 120.0
            capped = jnp.minimum(depth[line, at], top)
            soft = capped - jnp.log2(1.0 + jnp.exp2(capped))
            kept = jnp.exp2(soft * aerosol_ref[block, line, at].astype(F32)).astype(BF16)
            trans[line, at] = kept

    def finish(block, trans):
        out_ref[pl.ds(block * rows, rows), :] = jnp.dot(
            trans[...], wout_ref[...], preferred_element_type=F32
        ).astype(BF16)

    begin(0, depth_a, bound_a)

    def pair(i, _):
        first = 2 * i
        for copy in fetches(first):
            copy.wait()
        begin(first + 1, depth_b, bound_b)
        finish(jnp.maximum(first - 1, 0), trans_b)
        middle(first, depth_a, bound_a, trans_a)
        for copy in fetches(first + 1):
            copy.wait()
        begin(jnp.minimum(first + 2, blocks - 1), depth_a, bound_a)
        finish(first, trans_a)
        middle(first + 1, depth_b, bound_b, trans_b)
        return 0

    lax.fori_loop(0, blocks // 2, pair, 0)
    finish(blocks - 1, trans_b)


def radiate(arrived, aerosol, band_in, band_out, cap):
    lev = arrived.shape[1]
    rows, width = aerosol.shape
    block = 16 * cap
    in_vmem = pl.BlockSpec(memory_space=pltpu.VMEM)
    return call(
        functools.partial(radiate_kernel, cap),
        jax.ShapeDtypeStruct((rows, 2 * lev), BF16),
        arrived, aerosol, band_in, band_out,
        vmem=46, flops=7 * 10**9, moved=20 * 10**6,
        in_specs=[in_vmem, pl.BlockSpec(memory_space=pltpu.HBM), in_vmem, in_vmem],
        scratch_shapes=[
            pltpu.VMEM((rows // block, block, width), BF16),
            pltpu.VMEM((2 * band_in.shape[0], width), BF16),
            pltpu.VMEM((block, width), F32),
            pltpu.VMEM((block, width), F32),
            pltpu.VMEM((block, width), BF16),
            pltpu.VMEM((block, width), BF16),
            pltpu.VMEM((3, block, lev), F32),
            pltpu.VMEM((3, block, lev), F32),
            pltpu.SemaphoreType.DMA((rows // block, PIECES)),
        ],
    )


def gather_kernel(cap, owners_ref, slot_ref, back_ref, out_hbm, out_ref, hot_ref, sem):
    cols, rows = out_ref.shape[0], back_ref.shape[0]
    block, wide = hot_ref.shape[1], 128
    lane = lax.broadcasted_iota(I32, (wide, wide), 1)
    none = jnp.zeros((wide, wide), BF16)

    def ship(i):
        at = pl.ds(i * block, block)
        return pltpu.make_async_copy(out_ref.at[at], out_hbm.at[at], sem.at[i])

    for i in range(cols // block):
        for j in range(block // wide):
            at = pl.ds(i * block + j * wide, wide)
            line = (owners_ref[:, at] * cap + slot_ref[:, at]).astype(F32)
            place = jnp.transpose(jnp.broadcast_to(line, (wide, wide))).astype(I32)
            high = (place >> 7).astype(F32).astype(BF16)
            low = (lane == (place & (wide - 1))).astype(F32).astype(BF16)
            for r in range(rows // wide):
                here = jnp.full((wide, wide), float(r), BF16)
                hot_ref[i % 2, pl.ds(j * wide, wide), pl.ds(r * wide, wide)] = jnp.where(
                    high == here, low, none
                )
        out_ref[pl.ds(i * block, block), :] = jnp.dot(
            hot_ref[i % 2], back_ref[...], preferred_element_type=F32
        ).astype(BF16)
        ship(i).start()
    for i in range(cols // block):
        ship(i).wait()


def gather(owners, slots, back, cap):
    return call(
        functools.partial(gather_kernel, cap),
        jax.ShapeDtypeStruct((owners.shape[1], back.shape[1]), BF16),
        owners, slots, back,
        vmem=24, flops=3 * 10**9, moved=3 * 10**6,
        in_specs=[pl.BlockSpec(memory_space=pltpu.VMEM)] * 3,
        out_specs=pl.BlockSpec(memory_space=pl.ANY),
        scratch_shapes=[
            pltpu.VMEM((owners.shape[1], back.shape[1]), BF16),
            pltpu.VMEM((2, owners.shape[1] // 4, back.shape[0]), BF16),
            pltpu.SemaphoreType.DMA((4,)),
        ],
    )


def exchange(x):
    return lax.all_to_all(x, ("dyn", "col"), split_axis=0, concat_axis=0, tiled=True)


def shards(tracer, temper, winds, owners, classes, aerosol, band_in, band_out):
    n_dyn, n_col = lax.axis_size("dyn"), lax.axis_size("col")
    devices = n_dyn * n_col
    lev = tracer.shape[2]
    cap = aerosol.shape[1] // devices

    def send(x, by_dyn, by_col):
        pairs = [
            (i * n_col + j, ((i + by_dyn) % n_dyn) * n_col + (j + by_col) % n_col)
            for i in range(n_dyn)
            for j in range(n_col)
        ]
        return lax.ppermute(x, ("dyn", "col"), pairs)

    owners = owners.reshape(1, -1)
    ex0, ex3, ey0, ey3 = edges(tracer, winds)
    xprev, xnext = send(ex3, 1, 0), send(ex0, -1, 0)
    nodes, tend = tendency_stage(tracer, winds)
    slots, table, temper_cells = columns_stage(owners, classes.reshape(1, -1), temper, devices)
    side0, side3 = sides(ey0, ey3, xprev, xnext)
    yprev, ynext = send(side3, 0, 1), send(side0, 0, -1)
    tracer_new, outgoing = tracer_stage(
        tracer.shape, nodes, tend, (xprev, xnext, yprev, ynext), owners, slots, table, temper_cells, cap
    )
    each = 2 * cap + 8
    arrived = exchange(outgoing.reshape(devices, each, lev)).reshape(-1, lev)
    result = radiate(arrived, aerosol[0], band_in, band_out, cap)
    back = exchange(result.reshape(devices, cap, 2 * lev)).reshape(-1, 2 * lev)
    return (tracer_new, gather(owners, slots, back, cap))


def solution(mesh):
    return jax.shard_map(
        shards,
        mesh=mesh,
        in_specs=(
            P("dyn", "col", None),
            P("dyn", "col", None),
            P(None, "dyn", "col", None),
            P(("dyn", "col"), None),
            P(("dyn", "col")),
            P(("dyn", "col"), None, None),
            P(),
            P(),
        ),
        out_specs=(P("dyn", "col", None), P(("dyn", "col"), None)),
        check_vma=False,
    )
```

```python
import functools
import math

import jax
import jax.numpy as jnp
import numpy as np
from jax import lax
from jax.experimental import pallas as pl
from jax.experimental.pallas import tpu as pltpu
from jax.sharding import PartitionSpec as P

STEP_SIZE = 0.1
F32, BF16, I32 = jnp.float32, jnp.bfloat16, jnp.int32
MIB = 1024 * 1024
LOG2E = 1.4426950408889634


def lagrange_tables():
    points = np.array([-1.0, -1.0 / math.sqrt(5.0), 1.0 / math.sqrt(5.0), 1.0])
    products = np.array(
        [np.prod([points[r] - points[k] for k in range(4) if k != r]) for r in range(4)]
    )
    derivative = np.zeros((4, 4))
    for r in range(4):
        for c in range(4):
            if r == c:
                derivative[r, c] = np.sum(
                    [1.0 / (points[r] - points[k]) for k in range(4) if k != r]
                )
            else:
                derivative[r, c] = products[r] / (products[c] * (points[r] - points[c]))
    average = np.array([[1.0 / 6.0, 5.0 / 6.0, 0.0, 0.0], [0.0, 0.0, 5.0 / 6.0, 1.0 / 6.0]])
    return (derivative, average)


GRAD, PG2 = lagrange_tables()


def combine(weights, pieces):
    total = None
    for weight, piece in zip(weights, pieces):
        if abs(float(weight)) > 1e-12:
            term = float(weight) * piece
            total = term if total is None else total + term
    return total


def cell_pair(nodes):
    halves = [[combine(PG2[a], [nodes[x][k] for x in range(4)]) for k in range(4)] for a in range(2)]
    return [[combine(PG2[b], halves[a]) for b in range(2)] for a in range(2)]


def call(kernel, out_shape, *args, vmem, flops=0, moved=0, **kw):
    return pl.pallas_call(
        kernel,
        out_shape=out_shape,
        compiler_params=pltpu.CompilerParams(vmem_limit_bytes=vmem * MIB),
        cost_estimate=pl.CostEstimate(flops=flops, bytes_accessed=moved, transcendentals=0),
        **kw,
    )(*args)


def full(shape):
    return pl.BlockSpec(shape, lambda *_: (0,) * len(shape))


def edges_kernel(tracer, winds, ex0, ex3, ey0, ey3, xs, xw, ys, yw, line, wind, strip, vstrip, sem):
    nx, ny, lev = tracer.shape
    ne = ny // 4
    copies = []
    for i, (x, x4, y) in enumerate(((0, 0, 0), (nx - 1, nx - 4, ny - 16))):
        copies.append((
            pltpu.make_async_copy(tracer.at[pl.ds(x4, 4)], xs.at[i], sem.at[i, 0]),
            pltpu.make_async_copy(winds.at[:, x], xw.at[i], sem.at[i, 1]),
            pltpu.make_async_copy(tracer.at[:, pl.ds(y, 16)], ys.at[i], sem.at[i, 2]),
            pltpu.make_async_copy(winds.at[:, :, pl.ds(y, 16)], yw.at[i], sem.at[i, 3]),
        ))
    for part in (0, 2):
        for group in copies:
            group[part].start()
            group[part + 1].start()

    for i, (node, out) in enumerate(((0, ex0), (3, ex3))):
        copies[i][0].wait()
        copies[i][1].wait()
        for x in range(4):
            line[pl.ds((4 * i + x) * ny, ny), :] = xs[i, x].astype(F32)
        for h in range(2):
            wind[pl.ds((2 * i + h) * ny, ny), :] = xw[i, h].astype(F32)
        nodes = [
            [line[pl.ds((4 * i + x) * ny + k, ne, stride=4), :] for k in range(4)] for x in range(4)
        ]
        for k in range(4):
            dx = combine(GRAD[node], [nodes[m][k] for m in range(4)])
            dy = combine(GRAD[k], nodes[node])
            u = wind[pl.ds(2 * i * ny + k, ne, stride=4), :]
            v = wind[pl.ds((2 * i + 1) * ny + k, ne, stride=4), :]
            out[pl.ds(k * ne, ne), :] = -(u * dx + v * dy)

    size = nx * 16
    for i, (base, node, out) in enumerate(((0, 0, ey0), (12, 3, ey3))):
        copies[i][2].wait()
        copies[i][3].wait()
        nel = nx // 4
        strip[pl.ds(i * size, size), :] = ys[i].astype(F32).reshape(size, lev)
        for h in range(2):
            vstrip[pl.ds((2 * i + h) * size, size), :] = yw[i, h].astype(F32).reshape(size, lev)
        nodes = [
            [strip[pl.ds(i * size + x * 16 + base + k, nel, stride=64), :] for k in range(4)]
            for x in range(4)
        ]
        for x in range(4):
            dx = combine(GRAD[x], [nodes[m][node] for m in range(4)])
            dy = combine(GRAD[node], nodes[x])
            at = x * 16 + base + node
            u = vstrip[pl.ds(2 * i * size + at, nel, stride=64), :]
            v = vstrip[pl.ds((2 * i + 1) * size + at, nel, stride=64), :]
            out[pl.ds(x, nel, stride=4), :] = -(u * dx + v * dy)


def edges(tracer, winds):
    nx, ny, lev = tracer.shape
    shapes = [(ny, lev)] * 2 + [(nx, lev)] * 2
    return call(
        edges_kernel,
        [jax.ShapeDtypeStruct(s, F32) for s in shapes],
        tracer, winds,
        vmem=53, flops=10**6, moved=3 * 10**6,
        in_specs=[pl.BlockSpec(memory_space=pltpu.HBM)] * 2,
        scratch_shapes=[
            pltpu.VMEM((2, 4, ny, lev), BF16),
            pltpu.VMEM((2, 2, ny, lev), BF16),
            pltpu.VMEM((2, nx, 16, lev), BF16),
            pltpu.VMEM((2, 2, nx, 16, lev), BF16),
            pltpu.VMEM((8 * ny, lev), F32),
            pltpu.VMEM((4 * ny, lev), F32),
            pltpu.VMEM((2 * nx * 16, lev), F32),
            pltpu.VMEM((4 * nx * 16, lev), F32),
            pltpu.SemaphoreType.DMA((2, 4)),
        ],
    )


def sides_kernel(ey0, ey3, xprev, xnext, out0, out3, line):
    nx, lev = ey0.shape
    ny = xprev.shape[0]
    position = lax.broadcasted_iota(I32, (nx, lev), 0) & 3
    for mid, row, out in ((ey0, 0, out0), (ey3, ny - 1, out3)):
        line[pl.ds(7, 1), :] = xprev[pl.ds(row, 1), :]
        line[pl.ds(8, nx), :] = mid[...]
        line[pl.ds(8 + nx, 1), :] = xnext[pl.ds(row, 1), :]
        here = line[pl.ds(8, nx), :]
        back = 0.5 * (here + line[pl.ds(7, nx), :])
        front = 0.5 * (here + line[pl.ds(9, nx), :])
        out[...] = jnp.where(position == 3, front, jnp.where(position == 0, back, here))


def sides(ey0, ey3, xprev, xnext):
    return call(
        sides_kernel,
        [jax.ShapeDtypeStruct(ey0.shape, F32)] * 2,
        ey0, ey3, xprev, xnext,
        vmem=4, flops=10**5, moved=2 * 10**5,
        scratch_shapes=[pltpu.VMEM((ey0.shape[0] + 16, ey0.shape[1]), F32)],
    )


GROUP = 32


def pack(cap, owners_ref, slot_ref, table_ref, values_ref, low_ref, out_ref):
    cols = owners_ref.shape[1]
    lev = out_ref.shape[1]
    rows = GROUP * cap
    each = 2 * cap + 8
    owner = owners_ref[...]
    high = owner // GROUP
    place = (owner - high * GROUP) * cap + slot_ref[...]
    sub = lax.broadcasted_iota(I32, (rows, cols), 0)
    low_ref[...] = (sub == place).astype(F32).astype(BF16)
    none = jnp.zeros((rows, cols), BF16)
    high_all = jnp.broadcast_to(high.astype(F32).astype(BF16), (rows, cols))
    for i in range(table_ref.shape[0] // GROUP):
        hot = jnp.where(high_all == jnp.full((rows, cols), float(i), BF16), low_ref[...], none)
        packed = jnp.dot(hot, values_ref[...], preferred_element_type=F32)
        pieces = []
        for o in range(GROUP):
            line = table_ref[pl.ds(i * GROUP + o, 1), :]
            pieces.append(packed[o * cap : (o + 1) * cap, :lev])
            pieces.append(packed[o * cap : (o + 1) * cap, lev:])
            pieces.append(jnp.broadcast_to(line, (8, lev)))
        out_ref[pl.ds(i * GROUP * each, GROUP * each), :] = jnp.concatenate(pieces, axis=0).astype(BF16)


def cells_of(nodes, cells_ref, row, ne):
    cells = cell_pair(nodes)
    for a in range(2):
        for b in range(2):
            cells_ref[pl.ds(row + a * 2 * ne + b, ne, stride=2), :] = cells[a][b]


def columns_kernel(owners_ref, classes_ref, temper_hbm, slot_ref, table_ref, out_ref,
                   temper_ref, nodes_ref, cells_ref, sem):
    copy = pltpu.make_async_copy(temper_hbm, temper_ref, sem)
    copy.start()
    cols = owners_ref.shape[1]
    nx, ny, lev = temper_ref.shape
    ne = ny // 4
    devices = table_ref.shape[0]
    chunk = 256
    sub = lax.broadcasted_iota(I32, (devices, chunk), 0)
    upper = (
        lax.broadcasted_iota(I32, (chunk, chunk), 0) < lax.broadcasted_iota(I32, (chunk, chunk), 1)
    ).astype(F32).astype(BF16)
    ones = jnp.ones((chunk, chunk), BF16)
    running = jnp.zeros((devices, chunk), F32)
    table = jnp.zeros((devices, 128), F32)
    slots_sub = lax.broadcasted_iota(I32, (128, chunk), 0)
    for i in range(cols // chunk):
        owner = owners_ref[:, pl.ds(i * chunk, chunk)]
        hit = sub == owner
        hot = hit.astype(F32)
        hot16 = hot.astype(BF16)
        earlier = running + jnp.dot(hot16, upper, preferred_element_type=F32)
        slot = jnp.sum(jnp.where(hit, earlier, 0.0), axis=0, keepdims=True).astype(I32)
        running = running + jnp.dot(hot16, ones, preferred_element_type=F32)
        slot_ref[:, pl.ds(i * chunk, chunk)] = slot
        cost = classes_ref[:, pl.ds(i * chunk, chunk)].astype(F32)
        placed = jnp.where(slots_sub == slot, cost, 0.0).astype(BF16)
        table = table + lax.dot_general(
            hot16, placed, (((1,), (1,)), ((), ())), preferred_element_type=F32
        )
    table_ref[...] = table
    copy.wait()

    def element(e, _):
        base = pl.multiple_of(e * 4 * ny, 8)
        for x in range(4):
            nodes_ref[pl.ds(base + x * ny, ny), :] = temper_ref[4 * e + x].astype(F32)
        nodes = [
            [nodes_ref[pl.ds(base + x * ny + k, ne, stride=4), :] for k in range(4)]
            for x in range(4)
        ]
        cells_of(nodes, cells_ref, pl.multiple_of(e * ny, 8), ne)
        return 0

    lax.fori_loop(0, nx // 4, element, 0, unroll=2)
    out_ref[...] = cells_ref[...].astype(BF16)


def columns_stage(owners, classes, temper, devices):
    nx, ny, lev = temper.shape
    cols = owners.shape[1]
    return call(
        columns_kernel,
        [
            jax.ShapeDtypeStruct((1, cols), I32),
            jax.ShapeDtypeStruct((devices, 128), F32),
            jax.ShapeDtypeStruct((cols, lev), BF16),
        ],
        owners, classes, temper,
        vmem=16, flops=10**9, moved=4 * 10**6,
        in_specs=[pl.BlockSpec(memory_space=pltpu.VMEM)] * 2
        + [pl.BlockSpec(memory_space=pltpu.HBM)],
        scratch_shapes=[
            pltpu.VMEM((nx, ny, lev), BF16),
            pltpu.VMEM((nx * ny, lev), F32),
            pltpu.VMEM((nx * ny // 4, lev), F32),
            pltpu.SemaphoreType.DMA,
        ],
    )


CHUNKS = 4


def tendency_kernel(tracer_ref, winds_ref, nodes_ref, tend_ref, u_ref, v_ref):
    nx, ny, lev = tracer_ref.shape
    ne = ny // 4

    def element(e, _):
        base = pl.multiple_of(e * 4 * ny, 8)
        for x in range(4):
            nodes_ref[pl.ds(base + x * ny, ny), :] = tracer_ref[4 * e + x].astype(F32)
            u_ref[pl.ds(base + x * ny, ny), :] = winds_ref[0, 4 * e + x].astype(F32)
            v_ref[pl.ds(base + x * ny, ny), :] = winds_ref[1, 4 * e + x].astype(F32)
        for t in range(ne // 8):
            off = t * 32
            nodes = [
                [nodes_ref[pl.ds(base + x * ny + off + k, 8, stride=4), :] for k in range(4)]
                for x in range(4)
            ]
            for x in range(4):
                for k in range(4):
                    dx = combine(GRAD[x], [nodes[m][k] for m in range(4)])
                    dy = combine(GRAD[k], nodes[x])
                    u = u_ref[pl.ds(base + x * ny + off + k, 8, stride=4), :]
                    v = v_ref[pl.ds(base + x * ny + off + k, 8, stride=4), :]
                    tend_ref[pl.ds(base + x * ny + k * ne + t * 8, 8), :] = -(u * dx + v * dy)
        return 0

    lax.fori_loop(0, nx // 4, element, 0, unroll=2)


def tendency_stage(tracer, winds):
    nx, ny, lev = tracer.shape
    in_vmem = pl.BlockSpec(memory_space=pltpu.VMEM)
    return call(
        tendency_kernel,
        [jax.ShapeDtypeStruct((nx * ny, lev), F32)] * 2,
        tracer, winds,
        vmem=20, flops=2 * 10**9, moved=8 * 10**6,
        in_specs=[in_vmem] * 2,
        out_specs=[in_vmem] * 2,
        scratch_shapes=[pltpu.VMEM((nx * ny, lev), F32)] * 2,
    )


def tracer_kernel(cap, nodes_ref, tend_ref, xprev, xnext, yprev, ynext, owners_ref, slot_ref,
                  table_ref, temper_ref, new_hbm, out_ref, new_ref, fresh_ref, cells_ref,
                  values_ref, low_ref, out_sem):
    nx, ny, lev = new_ref.shape
    ne = ny // 4
    part = nx // CHUNKS
    elements = nx // 4

    def put(c):
        rows = pl.ds(c * part, part)
        return pltpu.make_async_copy(new_ref.at[rows], new_hbm.at[rows], out_sem.at[c])

    first = lax.broadcasted_iota(I32, (ne, lev), 0) == 0
    last = lax.broadcasted_iota(I32, (ne, lev), 0) == ne - 1

    def assemble(e, _):
        base = pl.multiple_of(e * 4 * ny, 8)
        back = pl.multiple_of(jnp.maximum(e * 4 - 1, 0) * ny, 8)
        front = pl.multiple_of(jnp.minimum(e * 4 + 4, nx - 1) * ny, 8)
        rounded = []
        for x in range(4):
            lines = [tend_ref[pl.ds(base + x * ny + k * ne, ne), :] for k in range(4)]
            if x == 0:
                other = [
                    jnp.where(e == 0, xprev[pl.ds(k * ne, ne), :], tend_ref[pl.ds(back + k * ne, ne), :])
                    for k in range(4)
                ]
                lines = [0.5 * (lines[k] + other[k]) for k in range(4)]
            if x == 3:
                other = [
                    jnp.where(
                        e == elements - 1,
                        xnext[pl.ds(k * ne, ne), :],
                        tend_ref[pl.ds(front + k * ne, ne), :],
                    )
                    for k in range(4)
                ]
                lines = [0.5 * (lines[k] + other[k]) for k in range(4)]
            before = yprev[pl.ds(4 * e + x, 1), :]
            after = ynext[pl.ds(4 * e + x, 1), :]
            low = jnp.where(first, before, pltpu.roll(lines[3], 1, 0))
            high = jnp.where(last, after, pltpu.roll(lines[0], ne - 1, 0))
            whole = [0.5 * (lines[0] + low), lines[1], lines[2], 0.5 * (lines[3] + high)]
            row = []
            for k in range(4):
                where = pl.ds(base + x * ny + k, ne, stride=4)
                fresh = (nodes_ref[where, :] + STEP_SIZE * whole[k]).astype(BF16).astype(F32)
                fresh_ref[where, :] = fresh
                row.append(fresh)
            rounded.append(row)
            new_ref[4 * e + x] = fresh_ref[pl.ds(base + x * ny, ny), :].astype(BF16)
        cells_of(rounded, cells_ref, pl.multiple_of(e * ny, 8), ne)
        return 0

    per = part // 4
    for c in range(CHUNKS):
        lax.fori_loop(c * per, (c + 1) * per, assemble, 0, unroll=2)
        put(c).start()
    values_ref[:, :lev] = cells_ref[...].astype(BF16)
    values_ref[:, lev:] = temper_ref[...]
    pack(cap, owners_ref, slot_ref, table_ref, values_ref, low_ref, out_ref)
    for c in range(CHUNKS):
        put(c).wait()


def tracer_stage(shape, nodes, tend, halos, owners, slots, table, temper_cells, cap):
    nx, ny, lev = shape
    cols = owners.shape[1]
    devices = table.shape[0]
    in_vmem = pl.BlockSpec(memory_space=pltpu.VMEM)
    return call(
        functools.partial(tracer_kernel, cap),
        [
            jax.ShapeDtypeStruct((nx, ny, lev), BF16),
            jax.ShapeDtypeStruct((devices * (2 * cap + 8), lev), BF16),
        ],
        nodes, tend, *halos, owners, slots, table, temper_cells,
        vmem=30, flops=4 * 10**9, moved=8 * 10**6,
        in_specs=[in_vmem] * 10,
        out_specs=[pl.BlockSpec(memory_space=pltpu.HBM), in_vmem],
        scratch_shapes=[
            pltpu.VMEM((nx, ny, lev), BF16),
            pltpu.VMEM((nx * ny, lev), F32),
            pltpu.VMEM((cols, lev), F32),
            pltpu.VMEM((cols, 2 * lev), BF16),
            pltpu.VMEM((GROUP * cap, cols), BF16),
            pltpu.SemaphoreType.DMA((CHUNKS,)),
        ],
    )


PIECES = 2


def radiate_kernel(cap, x_ref, aerosol_hbm, win_ref, wout_ref, out_ref, aerosol_ref,
                   depth_a, depth_b, trans_a, trans_b, bound_a, bound_b, sem):
    blocks, rows, width = aerosol_ref.shape
    lev = x_ref.shape[1]
    each = 2 * cap + 8
    sources = rows // cap
    piece = rows // PIECES

    def fetches(block):
        return [
            pltpu.make_async_copy(
                aerosol_hbm.at[pl.ds(block * rows + j * piece, piece)],
                aerosol_ref.at[block, pl.ds(j * piece, piece)],
                sem.at[block, j],
            )
            for j in range(PIECES)
        ]

    for block in range(blocks):
        for copy in fetches(block):
            copy.start()

    lane = lax.broadcasted_iota(I32, (8, lev), 1)
    sub = lax.broadcasted_iota(I32, (8, lev), 0)
    ones = jnp.ones((lev, lev), BF16)

    def begin(block, bound):
        tracer, temper, mine = [], [], []
        for s in range(sources):
            lines = x_ref[pl.ds((block * sources + s) * each, each), :].astype(F32)
            tracer.append(lines[:cap])
            temper.append(lines[cap : 2 * cap])
            mine += [jnp.where(lane == sub + 8 * j, lines[2 * cap :], 0.0) for j in range(cap // 8)]
        state = -jnp.concatenate(
            [jnp.concatenate(tracer, axis=0), jnp.concatenate(temper, axis=0)], axis=1
        ).astype(BF16)
        mine = jnp.concatenate(mine, axis=0).astype(BF16)
        cost = jnp.dot(mine, ones, preferred_element_type=F32)
        for g in range(1, 4):
            bound[g - 1] = jnp.where(cost > g - 0.5, 120.0, -1e30)
        return state

    half = width // 2

    def deepen(state, depth, h):
        at = pl.ds(h * half, half)
        depth[:, at] = jnp.dot(state, win_ref[:, at], preferred_element_type=F32)

    step, tile = 256, 64
    parts = width // step

    def middle(block, depth, bound, trans, chunks):
        for i, r in [(i, r) for i in chunks for r in range(0, rows, tile)]:
            at, line = pl.ds(i * step, step), pl.ds(r, tile)
            group = i * 4 // parts
            top = jnp.concatenate([bound[group - 1, line]] * (step // lev), axis=1) if group else 120.0
            capped = jnp.minimum(depth[line, at] * LOG2E, top)
            soft = capped - jnp.log2(1.0 + jnp.exp2(capped))
            kept = jnp.exp2(soft * aerosol_ref[block, line, at].astype(F32)).astype(BF16)
            trans[line, at] = kept

    def finish(block, trans):
        out_ref[pl.ds(block * rows, rows), :] = jnp.dot(
            trans[...], wout_ref[...], preferred_element_type=F32
        ).astype(BF16)

    def advance(block, following, depth, bound, trans, depth_next, bound_next, before, trans_before):
        for copy in fetches(block):
            copy.wait()
        state = begin(following, bound_next)
        deepen(state, depth_next, 0)
        middle(block, depth, bound, trans, range(0, 3))
        finish(before, trans_before)
        middle(block, depth, bound, trans, range(3, 6))
        deepen(state, depth_next, 1)
        middle(block, depth, bound, trans, range(6, parts))

    state = begin(0, bound_a)
    deepen(state, depth_a, 0)
    deepen(state, depth_a, 1)

    def pair(i, _):
        first = 2 * i
        later = jnp.minimum(first + 2, blocks - 1)
        before = jnp.maximum(first - 1, 0)
        advance(first, first + 1, depth_a, bound_a, trans_a, depth_b, bound_b, before, trans_b)
        advance(first + 1, later, depth_b, bound_b, trans_b, depth_a, bound_a, first, trans_a)
        return 0

    lax.fori_loop(0, blocks // 2, pair, 0)
    finish(blocks - 1, trans_b)


def radiate(arrived, aerosol, band_in, band_out, cap):
    lev = arrived.shape[1]
    rows, width = aerosol.shape
    block = 16 * cap
    in_vmem = pl.BlockSpec(memory_space=pltpu.VMEM)
    return call(
        functools.partial(radiate_kernel, cap),
        jax.ShapeDtypeStruct((rows, 2 * lev), BF16),
        arrived, aerosol, band_in, band_out,
        vmem=46, flops=7 * 10**9, moved=20 * 10**6,
        in_specs=[in_vmem, pl.BlockSpec(memory_space=pltpu.HBM), in_vmem, in_vmem],
        scratch_shapes=[
            pltpu.VMEM((rows // block, block, width), BF16),
            pltpu.VMEM((block, width), F32),
            pltpu.VMEM((block, width), F32),
            pltpu.VMEM((block, width), BF16),
            pltpu.VMEM((block, width), BF16),
            pltpu.VMEM((3, block, lev), F32),
            pltpu.VMEM((3, block, lev), F32),
            pltpu.SemaphoreType.DMA((rows // block, PIECES)),
        ],
    )


def gather_kernel(cap, owners_ref, slot_ref, back_ref, out_hbm, out_ref, hot_ref, sem):
    cols, rows = out_ref.shape[0], back_ref.shape[0]
    block, wide = hot_ref.shape[1], 128
    lane = lax.broadcasted_iota(I32, (wide, wide), 1)
    none = jnp.zeros((wide, wide), BF16)

    def ship(i):
        at = pl.ds(i * block, block)
        return pltpu.make_async_copy(out_ref.at[at], out_hbm.at[at], sem.at[i])

    for i in range(cols // block):
        for j in range(block // wide):
            at = pl.ds(i * block + j * wide, wide)
            line = (owners_ref[:, at] * cap + slot_ref[:, at]).astype(F32)
            place = jnp.transpose(jnp.broadcast_to(line, (wide, wide))).astype(I32)
            high = (place >> 7).astype(F32).astype(BF16)
            low = (lane == (place & (wide - 1))).astype(F32).astype(BF16)
            for r in range(rows // wide):
                here = jnp.full((wide, wide), float(r), BF16)
                hot_ref[i % 2, pl.ds(j * wide, wide), pl.ds(r * wide, wide)] = jnp.where(
                    high == here, low, none
                )
        out_ref[pl.ds(i * block, block), :] = jnp.dot(
            hot_ref[i % 2], back_ref[...], preferred_element_type=F32
        ).astype(BF16)
        ship(i).start()
    for i in range(cols // block):
        ship(i).wait()


def gather(owners, slots, back, cap):
    return call(
        functools.partial(gather_kernel, cap),
        jax.ShapeDtypeStruct((owners.shape[1], back.shape[1]), BF16),
        owners, slots, back,
        vmem=24, flops=3 * 10**9, moved=3 * 10**6,
        in_specs=[pl.BlockSpec(memory_space=pltpu.VMEM)] * 3,
        out_specs=pl.BlockSpec(memory_space=pl.ANY),
        scratch_shapes=[
            pltpu.VMEM((owners.shape[1], back.shape[1]), BF16),
            pltpu.VMEM((2, owners.shape[1] // 4, back.shape[0]), BF16),
            pltpu.SemaphoreType.DMA((4,)),
        ],
    )


def exchange(x):
    return lax.all_to_all(x, ("dyn", "col"), split_axis=0, concat_axis=0, tiled=True)


def shards(tracer, temper, winds, owners, classes, aerosol, band_in, band_out):
    n_dyn, n_col = lax.axis_size("dyn"), lax.axis_size("col")
    devices = n_dyn * n_col
    lev = tracer.shape[2]
    cap = aerosol.shape[1] // devices

    def send(x, by_dyn, by_col):
        pairs = [
            (i * n_col + j, ((i + by_dyn) % n_dyn) * n_col + (j + by_col) % n_col)
            for i in range(n_dyn)
            for j in range(n_col)
        ]
        return lax.ppermute(x, ("dyn", "col"), pairs)

    owners = owners.reshape(1, -1)
    ex0, ex3, ey0, ey3 = edges(tracer, winds)
    xprev, xnext = send(ex3, 1, 0), send(ex0, -1, 0)
    nodes, tend = tendency_stage(tracer, winds)
    slots, table, temper_cells = columns_stage(owners, classes.reshape(1, -1), temper, devices)
    side0, side3 = sides(ey0, ey3, xprev, xnext)
    yprev, ynext = send(side3, 0, 1), send(side0, 0, -1)
    tracer_new, outgoing = tracer_stage(
        tracer.shape, nodes, tend, (xprev, xnext, yprev, ynext), owners, slots, table, temper_cells, cap
    )
    each = 2 * cap + 8
    arrived = exchange(outgoing.reshape(devices, each, lev)).reshape(-1, lev)
    result = radiate(arrived, aerosol[0], band_in, band_out, cap)
    back = exchange(result.reshape(devices, cap, 2 * lev)).reshape(-1, 2 * lev)
    return (tracer_new, gather(owners, slots, back, cap))


def solution(mesh):
    return jax.shard_map(
        shards,
        mesh=mesh,
        in_specs=(
            P("dyn", "col", None),
            P("dyn", "col", None),
            P(None, "dyn", "col", None),
            P(("dyn", "col"), None),
            P(("dyn", "col")),
            P(("dyn", "col"), None, None),
            P(),
            P(),
        ),
        out_specs=(P("dyn", "col", None), P(("dyn", "col"), None)),
        check_vma=False,
    )
```

```python
import functools
import math

import jax
import jax.numpy as jnp
import numpy as np
from jax import lax
from jax.experimental import pallas as pl
from jax.experimental.pallas import tpu as pltpu
from jax.sharding import PartitionSpec as P

STEP_SIZE = 0.1
F32, BF16, I32 = jnp.float32, jnp.bfloat16, jnp.int32
MIB = 1024 * 1024
LOG2E = 1.4426950408889634


def lagrange_tables():
    points = np.array([-1.0, -1.0 / math.sqrt(5.0), 1.0 / math.sqrt(5.0), 1.0])
    products = np.array(
        [np.prod([points[r] - points[k] for k in range(4) if k != r]) for r in range(4)]
    )
    derivative = np.zeros((4, 4))
    for r in range(4):
        for c in range(4):
            if r == c:
                derivative[r, c] = np.sum(
                    [1.0 / (points[r] - points[k]) for k in range(4) if k != r]
                )
            else:
                derivative[r, c] = products[r] / (products[c] * (points[r] - points[c]))
    average = np.array([[1.0 / 6.0, 5.0 / 6.0, 0.0, 0.0], [0.0, 0.0, 5.0 / 6.0, 1.0 / 6.0]])
    return (derivative, average)


GRAD, PG2 = lagrange_tables()


def combine(weights, pieces):
    total = None
    for weight, piece in zip(weights, pieces):
        if abs(float(weight)) > 1e-12:
            term = float(weight) * piece
            total = term if total is None else total + term
    return total


def cell_pair(nodes):
    halves = [[combine(PG2[a], [nodes[x][k] for x in range(4)]) for k in range(4)] for a in range(2)]
    return [[combine(PG2[b], halves[a]) for b in range(2)] for a in range(2)]


def call(kernel, out_shape, *args, vmem, flops=0, moved=0, **kw):
    return pl.pallas_call(
        kernel,
        out_shape=out_shape,
        compiler_params=pltpu.CompilerParams(vmem_limit_bytes=vmem * MIB),
        cost_estimate=pl.CostEstimate(flops=flops, bytes_accessed=moved, transcendentals=0),
        **kw,
    )(*args)


def full(shape):
    return pl.BlockSpec(shape, lambda *_: (0,) * len(shape))


def edges_kernel(tracer, winds, ex0, ex3, ey0, ey3, xs, xw, ys, yw, line, wind, strip, vstrip, sem):
    nx, ny, lev = tracer.shape
    ne = ny // 4
    copies = []
    for i, (x, x4, y) in enumerate(((0, 0, 0), (nx - 1, nx - 4, ny - 16))):
        copies.append((
            pltpu.make_async_copy(tracer.at[pl.ds(x4, 4)], xs.at[i], sem.at[i, 0]),
            pltpu.make_async_copy(winds.at[:, x], xw.at[i], sem.at[i, 1]),
            pltpu.make_async_copy(tracer.at[:, pl.ds(y, 16)], ys.at[i], sem.at[i, 2]),
            pltpu.make_async_copy(winds.at[:, :, pl.ds(y, 16)], yw.at[i], sem.at[i, 3]),
        ))
    for part in (0, 2):
        for group in copies:
            group[part].start()
            group[part + 1].start()

    for i, (node, out) in enumerate(((0, ex0), (3, ex3))):
        copies[i][0].wait()
        copies[i][1].wait()
        for x in range(4):
            line[pl.ds((4 * i + x) * ny, ny), :] = xs[i, x].astype(F32)
        for h in range(2):
            wind[pl.ds((2 * i + h) * ny, ny), :] = xw[i, h].astype(F32)
        nodes = [
            [line[pl.ds((4 * i + x) * ny + k, ne, stride=4), :] for k in range(4)] for x in range(4)
        ]
        for k in range(4):
            dx = combine(GRAD[node], [nodes[m][k] for m in range(4)])
            dy = combine(GRAD[k], nodes[node])
            u = wind[pl.ds(2 * i * ny + k, ne, stride=4), :]
            v = wind[pl.ds((2 * i + 1) * ny + k, ne, stride=4), :]
            out[pl.ds(k * ne, ne), :] = -(u * dx + v * dy)

    size = nx * 16
    for i, (base, node, out) in enumerate(((0, 0, ey0), (12, 3, ey3))):
        copies[i][2].wait()
        copies[i][3].wait()
        nel = nx // 4
        strip[pl.ds(i * size, size), :] = ys[i].astype(F32).reshape(size, lev)
        for h in range(2):
            vstrip[pl.ds((2 * i + h) * size, size), :] = yw[i, h].astype(F32).reshape(size, lev)
        nodes = [
            [strip[pl.ds(i * size + x * 16 + base + k, nel, stride=64), :] for k in range(4)]
            for x in range(4)
        ]
        for x in range(4):
            dx = combine(GRAD[x], [nodes[m][node] for m in range(4)])
            dy = combine(GRAD[node], nodes[x])
            at = x * 16 + base + node
            u = vstrip[pl.ds(2 * i * size + at, nel, stride=64), :]
            v = vstrip[pl.ds((2 * i + 1) * size + at, nel, stride=64), :]
            out[pl.ds(x, nel, stride=4), :] = -(u * dx + v * dy)


def edges(tracer, winds):
    nx, ny, lev = tracer.shape
    shapes = [(ny, lev)] * 2 + [(nx, lev)] * 2
    return call(
        edges_kernel,
        [jax.ShapeDtypeStruct(s, F32) for s in shapes],
        tracer, winds,
        vmem=53, flops=10**6, moved=3 * 10**6,
        in_specs=[pl.BlockSpec(memory_space=pltpu.HBM)] * 2,
        scratch_shapes=[
            pltpu.VMEM((2, 4, ny, lev), BF16),
            pltpu.VMEM((2, 2, ny, lev), BF16),
            pltpu.VMEM((2, nx, 16, lev), BF16),
            pltpu.VMEM((2, 2, nx, 16, lev), BF16),
            pltpu.VMEM((8 * ny, lev), F32),
            pltpu.VMEM((4 * ny, lev), F32),
            pltpu.VMEM((2 * nx * 16, lev), F32),
            pltpu.VMEM((4 * nx * 16, lev), F32),
            pltpu.SemaphoreType.DMA((2, 4)),
        ],
    )


def sides_kernel(ey0, ey3, xprev, xnext, out0, out3, line):
    nx, lev = ey0.shape
    ny = xprev.shape[0]
    position = lax.broadcasted_iota(I32, (nx, lev), 0) & 3
    for mid, row, out in ((ey0, 0, out0), (ey3, ny - 1, out3)):
        line[pl.ds(7, 1), :] = xprev[pl.ds(row, 1), :]
        line[pl.ds(8, nx), :] = mid[...]
        line[pl.ds(8 + nx, 1), :] = xnext[pl.ds(row, 1), :]
        here = line[pl.ds(8, nx), :]
        back = 0.5 * (here + line[pl.ds(7, nx), :])
        front = 0.5 * (here + line[pl.ds(9, nx), :])
        out[...] = jnp.where(position == 3, front, jnp.where(position == 0, back, here))


def sides(ey0, ey3, xprev, xnext):
    return call(
        sides_kernel,
        [jax.ShapeDtypeStruct(ey0.shape, F32)] * 2,
        ey0, ey3, xprev, xnext,
        vmem=4, flops=10**5, moved=2 * 10**5,
        scratch_shapes=[pltpu.VMEM((ey0.shape[0] + 16, ey0.shape[1]), F32)],
    )


GROUP = 32


def pack(cap, owners_ref, slot_ref, table_ref, values_ref, low_ref, out_ref):
    cols = owners_ref.shape[1]
    lev = out_ref.shape[1]
    rows = GROUP * cap
    each = 2 * cap + 8
    owner = owners_ref[...]
    high = owner // GROUP
    place = (owner - high * GROUP) * cap + slot_ref[...]
    sub = lax.broadcasted_iota(I32, (rows, cols), 0)
    low_ref[...] = (sub == place).astype(F32).astype(BF16)
    none = jnp.zeros((rows, cols), BF16)
    high_all = jnp.broadcast_to(high.astype(F32).astype(BF16), (rows, cols))
    for i in range(table_ref.shape[0] // GROUP):
        hot = jnp.where(high_all == jnp.full((rows, cols), float(i), BF16), low_ref[...], none)
        packed = jnp.dot(hot, values_ref[...], preferred_element_type=F32)
        pieces = []
        for o in range(GROUP):
            line = table_ref[pl.ds(i * GROUP + o, 1), :]
            pieces.append(packed[o * cap : (o + 1) * cap, :lev])
            pieces.append(packed[o * cap : (o + 1) * cap, lev:])
            pieces.append(jnp.broadcast_to(line, (8, lev)))
        out_ref[pl.ds(i * GROUP * each, GROUP * each), :] = jnp.concatenate(pieces, axis=0).astype(BF16)


def cells_of(nodes, cells_ref, row, ne):
    cells = cell_pair(nodes)
    for a in range(2):
        for b in range(2):
            cells_ref[pl.ds(row + a * 2 * ne + b, ne, stride=2), :] = cells[a][b]


def columns_kernel(owners_ref, classes_ref, temper_hbm, slot_ref, table_ref, out_ref,
                   temper_ref, nodes_ref, cells_ref, sem):
    copy = pltpu.make_async_copy(temper_hbm, temper_ref, sem)
    copy.start()
    cols = owners_ref.shape[1]
    nx, ny, lev = temper_ref.shape
    ne = ny // 4
    devices = table_ref.shape[0]
    chunk = 256
    sub = lax.broadcasted_iota(I32, (devices, chunk), 0)
    upper = (
        lax.broadcasted_iota(I32, (chunk, chunk), 0) < lax.broadcasted_iota(I32, (chunk, chunk), 1)
    ).astype(F32).astype(BF16)
    ones = jnp.ones((chunk, chunk), BF16)
    running = jnp.zeros((devices, chunk), F32)
    table = jnp.zeros((devices, 128), F32)
    slots_sub = lax.broadcasted_iota(I32, (128, chunk), 0)
    for i in range(cols // chunk):
        owner = owners_ref[:, pl.ds(i * chunk, chunk)]
        hit = sub == owner
        hot = hit.astype(F32)
        hot16 = hot.astype(BF16)
        earlier = running + jnp.dot(hot16, upper, preferred_element_type=F32)
        slot = jnp.sum(jnp.where(hit, earlier, 0.0), axis=0, keepdims=True).astype(I32)
        running = running + jnp.dot(hot16, ones, preferred_element_type=F32)
        slot_ref[:, pl.ds(i * chunk, chunk)] = slot
        cost = classes_ref[:, pl.ds(i * chunk, chunk)].astype(F32)
        placed = jnp.where(slots_sub == slot, cost, 0.0).astype(BF16)
        table = table + lax.dot_general(
            hot16, placed, (((1,), (1,)), ((), ())), preferred_element_type=F32
        )
    table_ref[...] = table
    copy.wait()

    def element(e, _):
        base = pl.multiple_of(e * 4 * ny, 8)
        for x in range(4):
            nodes_ref[pl.ds(base + x * ny, ny), :] = temper_ref[4 * e + x].astype(F32)
        nodes = [
            [nodes_ref[pl.ds(base + x * ny + k, ne, stride=4), :] for k in range(4)]
            for x in range(4)
        ]
        cells_of(nodes, cells_ref, pl.multiple_of(e * ny, 8), ne)
        return 0

    lax.fori_loop(0, nx // 4, element, 0, unroll=2)
    out_ref[...] = cells_ref[...].astype(BF16)


def columns_stage(owners, classes, temper, devices):
    nx, ny, lev = temper.shape
    cols = owners.shape[1]
    return call(
        columns_kernel,
        [
            jax.ShapeDtypeStruct((1, cols), I32),
            jax.ShapeDtypeStruct((devices, 128), F32),
            jax.ShapeDtypeStruct((cols, lev), BF16),
        ],
        owners, classes, temper,
        vmem=16, flops=10**9, moved=4 * 10**6,
        in_specs=[pl.BlockSpec(memory_space=pltpu.VMEM)] * 2
        + [pl.BlockSpec(memory_space=pltpu.HBM)],
        scratch_shapes=[
            pltpu.VMEM((nx, ny, lev), BF16),
            pltpu.VMEM((nx * ny, lev), F32),
            pltpu.VMEM((nx * ny // 4, lev), F32),
            pltpu.SemaphoreType.DMA,
        ],
    )


CHUNKS = 4


def tendency_kernel(tracer_ref, winds_ref, nodes_ref, tend_ref, u_ref, v_ref):
    nx, ny, lev = tracer_ref.shape
    ne = ny // 4

    def element(e, _):
        base = pl.multiple_of(e * 4 * ny, 8)
        for x in range(4):
            nodes_ref[pl.ds(base + x * ny, ny), :] = tracer_ref[4 * e + x].astype(F32)
            u_ref[pl.ds(base + x * ny, ny), :] = winds_ref[0, 4 * e + x].astype(F32)
            v_ref[pl.ds(base + x * ny, ny), :] = winds_ref[1, 4 * e + x].astype(F32)
        for t in range(ne // 8):
            off = t * 32
            nodes = [
                [nodes_ref[pl.ds(base + x * ny + off + k, 8, stride=4), :] for k in range(4)]
                for x in range(4)
            ]
            for x in range(4):
                for k in range(4):
                    dx = combine(GRAD[x], [nodes[m][k] for m in range(4)])
                    dy = combine(GRAD[k], nodes[x])
                    u = u_ref[pl.ds(base + x * ny + off + k, 8, stride=4), :]
                    v = v_ref[pl.ds(base + x * ny + off + k, 8, stride=4), :]
                    tend_ref[pl.ds(base + x * ny + k * ne + t * 8, 8), :] = -(u * dx + v * dy)
        return 0

    lax.fori_loop(0, nx // 4, element, 0, unroll=2)


def tendency_stage(tracer, winds):
    nx, ny, lev = tracer.shape
    in_vmem = pl.BlockSpec(memory_space=pltpu.VMEM)
    return call(
        tendency_kernel,
        [jax.ShapeDtypeStruct((nx * ny, lev), F32)] * 2,
        tracer, winds,
        vmem=20, flops=2 * 10**9, moved=8 * 10**6,
        in_specs=[in_vmem] * 2,
        out_specs=[in_vmem] * 2,
        scratch_shapes=[pltpu.VMEM((nx * ny, lev), F32)] * 2,
    )


def tracer_kernel(cap, nodes_ref, tend_ref, xprev, xnext, yprev, ynext, owners_ref, slot_ref,
                  table_ref, temper_ref, new_hbm, out_ref, new_ref, fresh_ref, cells_ref,
                  values_ref, low_ref, out_sem):
    nx, ny, lev = new_ref.shape
    ne = ny // 4
    part = nx // CHUNKS
    elements = nx // 4

    def put(c):
        rows = pl.ds(c * part, part)
        return pltpu.make_async_copy(new_ref.at[rows], new_hbm.at[rows], out_sem.at[c])

    first = lax.broadcasted_iota(I32, (ne, lev), 0) == 0
    last = lax.broadcasted_iota(I32, (ne, lev), 0) == ne - 1

    def assemble(e, _):
        base = pl.multiple_of(e * 4 * ny, 8)
        back = pl.multiple_of(jnp.maximum(e * 4 - 1, 0) * ny, 8)
        front = pl.multiple_of(jnp.minimum(e * 4 + 4, nx - 1) * ny, 8)
        rounded = []
        for x in range(4):
            lines = [tend_ref[pl.ds(base + x * ny + k * ne, ne), :] for k in range(4)]
            if x == 0:
                other = [
                    jnp.where(e == 0, xprev[pl.ds(k * ne, ne), :], tend_ref[pl.ds(back + k * ne, ne), :])
                    for k in range(4)
                ]
                lines = [0.5 * (lines[k] + other[k]) for k in range(4)]
            if x == 3:
                other = [
                    jnp.where(
                        e == elements - 1,
                        xnext[pl.ds(k * ne, ne), :],
                        tend_ref[pl.ds(front + k * ne, ne), :],
                    )
                    for k in range(4)
                ]
                lines = [0.5 * (lines[k] + other[k]) for k in range(4)]
            before = yprev[pl.ds(4 * e + x, 1), :]
            after = ynext[pl.ds(4 * e + x, 1), :]
            low = jnp.where(first, before, pltpu.roll(lines[3], 1, 0))
            high = jnp.where(last, after, pltpu.roll(lines[0], ne - 1, 0))
            whole = [0.5 * (lines[0] + low), lines[1], lines[2], 0.5 * (lines[3] + high)]
            row = []
            for k in range(4):
                where = pl.ds(base + x * ny + k, ne, stride=4)
                fresh = (nodes_ref[where, :] + STEP_SIZE * whole[k]).astype(BF16).astype(F32)
                fresh_ref[where, :] = fresh
                row.append(fresh)
            rounded.append(row)
            new_ref[4 * e + x] = fresh_ref[pl.ds(base + x * ny, ny), :].astype(BF16)
        cells_of(rounded, cells_ref, pl.multiple_of(e * ny, 8), ne)
        return 0

    per = part // 4
    for c in range(CHUNKS):
        lax.fori_loop(c * per, (c + 1) * per, assemble, 0, unroll=2)
        put(c).start()
    values_ref[:, :lev] = cells_ref[...].astype(BF16)
    values_ref[:, lev:] = temper_ref[...]
    pack(cap, owners_ref, slot_ref, table_ref, values_ref, low_ref, out_ref)
    for c in range(CHUNKS):
        put(c).wait()


def tracer_stage(shape, nodes, tend, halos, owners, slots, table, temper_cells, cap):
    nx, ny, lev = shape
    cols = owners.shape[1]
    devices = table.shape[0]
    in_vmem = pl.BlockSpec(memory_space=pltpu.VMEM)
    return call(
        functools.partial(tracer_kernel, cap),
        [
            jax.ShapeDtypeStruct((nx, ny, lev), BF16),
            jax.ShapeDtypeStruct((devices * (2 * cap + 8), lev), BF16),
        ],
        nodes, tend, *halos, owners, slots, table, temper_cells,
        vmem=30, flops=4 * 10**9, moved=8 * 10**6,
        in_specs=[in_vmem] * 10,
        out_specs=[pl.BlockSpec(memory_space=pltpu.HBM), in_vmem],
        scratch_shapes=[
            pltpu.VMEM((nx, ny, lev), BF16),
            pltpu.VMEM((nx * ny, lev), F32),
            pltpu.VMEM((cols, lev), F32),
            pltpu.VMEM((cols, 2 * lev), BF16),
            pltpu.VMEM((GROUP * cap, cols), BF16),
            pltpu.SemaphoreType.DMA((CHUNKS,)),
        ],
    )


PIECES = 2


def radiate_kernel(cap, x_ref, aerosol_hbm, win_ref, wout_ref, out_ref, aerosol_ref,
                   depth_a, depth_b, trans_a, trans_b, bound_a, bound_b, sem):
    blocks, rows, width = aerosol_ref.shape
    lev = x_ref.shape[1]
    each = 2 * cap + 8
    sources = rows // cap
    piece = rows // PIECES

    def fetches(block):
        return [
            pltpu.make_async_copy(
                aerosol_hbm.at[pl.ds(block * rows + j * piece, piece)],
                aerosol_ref.at[block, pl.ds(j * piece, piece)],
                sem.at[block, j],
            )
            for j in range(PIECES)
        ]

    for block in range(blocks):
        for copy in fetches(block):
            copy.start()

    lane = lax.broadcasted_iota(I32, (8, lev), 1)
    sub = lax.broadcasted_iota(I32, (8, lev), 0)
    ones = jnp.ones((lev, lev), BF16)

    def begin(block, bound):
        tracer, temper, mine = [], [], []
        for s in range(sources):
            lines = x_ref[pl.ds((block * sources + s) * each, each), :].astype(F32)
            tracer.append(lines[:cap])
            temper.append(lines[cap : 2 * cap])
            mine += [jnp.where(lane == sub + 8 * j, lines[2 * cap :], 0.0) for j in range(cap // 8)]
        state = -jnp.concatenate(
            [jnp.concatenate(tracer, axis=0), jnp.concatenate(temper, axis=0)], axis=1
        ).astype(BF16)
        mine = jnp.concatenate(mine, axis=0).astype(BF16)
        cost = jnp.dot(mine, ones, preferred_element_type=F32)
        for g in range(1, 4):
            bound[g - 1] = jnp.where(cost > g - 0.5, 120.0, -1e30)
        return state

    half = width // 2

    def deepen(state, depth, h):
        at = pl.ds(h * half, half)
        depth[:, at] = jnp.dot(state, win_ref[:, at], preferred_element_type=F32)

    step, tile = 256, 64
    parts = width // step

    def middle(block, depth, bound, trans, chunks):
        for i, r in [(i, r) for i in chunks for r in range(0, rows, tile)]:
            at, line = pl.ds(i * step, step), pl.ds(r, tile)
            group = i * 4 // parts
            top = jnp.concatenate([bound[group - 1, line]] * (step // lev), axis=1) if group else 120.0
            capped = jnp.minimum(depth[line, at] * LOG2E, top)
            soft = capped - jnp.log2(1.0 + jnp.exp2(capped))
            kept = jnp.exp2(soft * aerosol_ref[block, line, at].astype(F32)).astype(BF16)
            trans[line, at] = kept

    size = rows // 2

    def finish(block, trans, h):
        out_ref[pl.ds(block * rows + h * size, size), :] = jnp.dot(
            trans[pl.ds(h * size, size), :], wout_ref[...], preferred_element_type=F32
        ).astype(BF16)

    def advance(block, following, depth, bound, trans, depth_next, bound_next, before, trans_before):
        for copy in fetches(block):
            copy.wait()
        state = begin(following, bound_next)
        deepen(state, depth_next, 0)
        middle(block, depth, bound, trans, range(0, 2))
        finish(before, trans_before, 0)
        middle(block, depth, bound, trans, range(2, 4))
        finish(before, trans_before, 1)
        middle(block, depth, bound, trans, range(4, 6))
        deepen(state, depth_next, 1)
        middle(block, depth, bound, trans, range(6, parts))

    state = begin(0, bound_a)
    deepen(state, depth_a, 0)
    deepen(state, depth_a, 1)

    def pair(i, _):
        first = 2 * i
        later = jnp.minimum(first + 2, blocks - 1)
        before = jnp.maximum(first - 1, 0)
        advance(first, first + 1, depth_a, bound_a, trans_a, depth_b, bound_b, before, trans_b)
        advance(first + 1, later, depth_b, bound_b, trans_b, depth_a, bound_a, first, trans_a)
        return 0

    lax.fori_loop(0, blocks // 2, pair, 0)
    finish(blocks - 1, trans_b, 0)
    finish(blocks - 1, trans_b, 1)


def radiate(arrived, aerosol, band_in, band_out, cap):
    lev = arrived.shape[1]
    rows, width = aerosol.shape
    block = 16 * cap
    in_vmem = pl.BlockSpec(memory_space=pltpu.VMEM)
    return call(
        functools.partial(radiate_kernel, cap),
        jax.ShapeDtypeStruct((rows, 2 * lev), BF16),
        arrived, aerosol, band_in, band_out,
        vmem=46, flops=7 * 10**9, moved=20 * 10**6,
        in_specs=[in_vmem, pl.BlockSpec(memory_space=pltpu.HBM), in_vmem, in_vmem],
        scratch_shapes=[
            pltpu.VMEM((rows // block, block, width), BF16),
            pltpu.VMEM((block, width), F32),
            pltpu.VMEM((block, width), F32),
            pltpu.VMEM((block, width), BF16),
            pltpu.VMEM((block, width), BF16),
            pltpu.VMEM((3, block, lev), F32),
            pltpu.VMEM((3, block, lev), F32),
            pltpu.SemaphoreType.DMA((rows // block, PIECES)),
        ],
    )


def gather_kernel(cap, owners_ref, slot_ref, back_ref, out_hbm, out_ref, hot_ref, sem):
    cols, rows = out_ref.shape[0], back_ref.shape[0]
    block, wide = hot_ref.shape[1], 128
    lane = lax.broadcasted_iota(I32, (wide, wide), 1)
    none = jnp.zeros((wide, wide), BF16)

    def ship(i):
        at = pl.ds(i * block, block)
        return pltpu.make_async_copy(out_ref.at[at], out_hbm.at[at], sem.at[i])

    for i in range(cols // block):
        for j in range(block // wide):
            at = pl.ds(i * block + j * wide, wide)
            line = (owners_ref[:, at] * cap + slot_ref[:, at]).astype(F32)
            place = jnp.transpose(jnp.broadcast_to(line, (wide, wide))).astype(I32)
            high = (place >> 7).astype(F32).astype(BF16)
            low = (lane == (place & (wide - 1))).astype(F32).astype(BF16)
            for r in range(rows // wide):
                here = jnp.full((wide, wide), float(r), BF16)
                hot_ref[i % 2, pl.ds(j * wide, wide), pl.ds(r * wide, wide)] = jnp.where(
                    high == here, low, none
                )
        out_ref[pl.ds(i * block, block), :] = jnp.dot(
            hot_ref[i % 2], back_ref[...], preferred_element_type=F32
        ).astype(BF16)
        ship(i).start()
    for i in range(cols // block):
        ship(i).wait()


def gather(owners, slots, back, cap):
    return call(
        functools.partial(gather_kernel, cap),
        jax.ShapeDtypeStruct((owners.shape[1], back.shape[1]), BF16),
        owners, slots, back,
        vmem=24, flops=3 * 10**9, moved=3 * 10**6,
        in_specs=[pl.BlockSpec(memory_space=pltpu.VMEM)] * 3,
        out_specs=pl.BlockSpec(memory_space=pl.ANY),
        scratch_shapes=[
            pltpu.VMEM((owners.shape[1], back.shape[1]), BF16),
            pltpu.VMEM((2, owners.shape[1] // 4, back.shape[0]), BF16),
            pltpu.SemaphoreType.DMA((4,)),
        ],
    )


def exchange(x):
    return lax.all_to_all(x, ("dyn", "col"), split_axis=0, concat_axis=0, tiled=True)


def shards(tracer, temper, winds, owners, classes, aerosol, band_in, band_out):
    n_dyn, n_col = lax.axis_size("dyn"), lax.axis_size("col")
    devices = n_dyn * n_col
    lev = tracer.shape[2]
    cap = aerosol.shape[1] // devices

    def send(x, by_dyn, by_col):
        pairs = [
            (i * n_col + j, ((i + by_dyn) % n_dyn) * n_col + (j + by_col) % n_col)
            for i in range(n_dyn)
            for j in range(n_col)
        ]
        return lax.ppermute(x, ("dyn", "col"), pairs)

    owners = owners.reshape(1, -1)
    ex0, ex3, ey0, ey3 = edges(tracer, winds)
    xprev, xnext = send(ex3, 1, 0), send(ex0, -1, 0)
    nodes, tend = tendency_stage(tracer, winds)
    slots, table, temper_cells = columns_stage(owners, classes.reshape(1, -1), temper, devices)
    side0, side3 = sides(ey0, ey3, xprev, xnext)
    yprev, ynext = send(side3, 0, 1), send(side0, 0, -1)
    tracer_new, outgoing = tracer_stage(
        tracer.shape, nodes, tend, (xprev, xnext, yprev, ynext), owners, slots, table, temper_cells, cap
    )
    each = 2 * cap + 8
    arrived = exchange(outgoing.reshape(devices, each, lev)).reshape(-1, lev)
    result = radiate(arrived, aerosol[0], band_in, band_out, cap)
    back = exchange(result.reshape(devices, cap, 2 * lev)).reshape(-1, 2 * lev)
    return (tracer_new, gather(owners, slots, back, cap))


def solution(mesh):
    return jax.shard_map(
        shards,
        mesh=mesh,
        in_specs=(
            P("dyn", "col", None),
            P("dyn", "col", None),
            P(None, "dyn", "col", None),
            P(("dyn", "col"), None),
            P(("dyn", "col")),
            P(("dyn", "col"), None, None),
            P(),
            P(),
        ),
        out_specs=(P("dyn", "col", None), P(("dyn", "col"), None)),
        check_vma=False,
    )
```

```python
import functools
import math

import jax
import jax.numpy as jnp
import numpy as np
from jax import lax
from jax.experimental import pallas as pl
from jax.experimental.pallas import tpu as pltpu
from jax.sharding import PartitionSpec as P

STEP_SIZE = 0.1
F32, BF16, I32 = jnp.float32, jnp.bfloat16, jnp.int32
MIB = 1024 * 1024
LOG2E = 1.4426950408889634


def lagrange_tables():
    points = np.array([-1.0, -1.0 / math.sqrt(5.0), 1.0 / math.sqrt(5.0), 1.0])
    products = np.array(
        [np.prod([points[r] - points[k] for k in range(4) if k != r]) for r in range(4)]
    )
    derivative = np.zeros((4, 4))
    for r in range(4):
        for c in range(4):
            if r == c:
                derivative[r, c] = np.sum(
                    [1.0 / (points[r] - points[k]) for k in range(4) if k != r]
                )
            else:
                derivative[r, c] = products[r] / (products[c] * (points[r] - points[c]))
    average = np.array([[1.0 / 6.0, 5.0 / 6.0, 0.0, 0.0], [0.0, 0.0, 5.0 / 6.0, 1.0 / 6.0]])
    return (derivative, average)


GRAD, PG2 = lagrange_tables()


def combine(weights, pieces):
    total = None
    for weight, piece in zip(weights, pieces):
        if abs(float(weight)) > 1e-12:
            term = float(weight) * piece
            total = term if total is None else total + term
    return total


def cell_pair(nodes):
    halves = [[combine(PG2[a], [nodes[x][k] for x in range(4)]) for k in range(4)] for a in range(2)]
    return [[combine(PG2[b], halves[a]) for b in range(2)] for a in range(2)]


def call(kernel, out_shape, *args, vmem, flops=0, moved=0, **kw):
    return pl.pallas_call(
        kernel,
        out_shape=out_shape,
        compiler_params=pltpu.CompilerParams(vmem_limit_bytes=vmem * MIB),
        cost_estimate=pl.CostEstimate(flops=flops, bytes_accessed=moved, transcendentals=0),
        **kw,
    )(*args)


def full(shape):
    return pl.BlockSpec(shape, lambda *_: (0,) * len(shape))


def edges_kernel(tracer, winds, ex0, ex3, ey0, ey3, xs, xw, ys, yw, line, wind, strip, vstrip, sem):
    nx, ny, lev = tracer.shape
    ne = ny // 4
    copies = []
    for i, (x, x4, y) in enumerate(((0, 0, 0), (nx - 1, nx - 4, ny - 16))):
        copies.append((
            pltpu.make_async_copy(tracer.at[pl.ds(x4, 4)], xs.at[i], sem.at[i, 0]),
            pltpu.make_async_copy(winds.at[:, x], xw.at[i], sem.at[i, 1]),
            pltpu.make_async_copy(tracer.at[:, pl.ds(y, 16)], ys.at[i], sem.at[i, 2]),
            pltpu.make_async_copy(winds.at[:, :, pl.ds(y, 16)], yw.at[i], sem.at[i, 3]),
        ))
    for part in (0, 2):
        for group in copies:
            group[part].start()
            group[part + 1].start()

    for i, (node, out) in enumerate(((0, ex0), (3, ex3))):
        copies[i][0].wait()
        copies[i][1].wait()
        for x in range(4):
            line[pl.ds((4 * i + x) * ny, ny), :] = xs[i, x].astype(F32)
        for h in range(2):
            wind[pl.ds((2 * i + h) * ny, ny), :] = xw[i, h].astype(F32)
        nodes = [
            [line[pl.ds((4 * i + x) * ny + k, ne, stride=4), :] for k in range(4)] for x in range(4)
        ]
        for k in range(4):
            dx = combine(GRAD[node], [nodes[m][k] for m in range(4)])
            dy = combine(GRAD[k], nodes[node])
            u = wind[pl.ds(2 * i * ny + k, ne, stride=4), :]
            v = wind[pl.ds((2 * i + 1) * ny + k, ne, stride=4), :]
            out[pl.ds(k * ne, ne), :] = -(u * dx + v * dy)

    size = nx * 16
    for i, (base, node, out) in enumerate(((0, 0, ey0), (12, 3, ey3))):
        copies[i][2].wait()
        copies[i][3].wait()
        nel = nx // 4
        strip[pl.ds(i * size, size), :] = ys[i].astype(F32).reshape(size, lev)
        for h in range(2):
            vstrip[pl.ds((2 * i + h) * size, size), :] = yw[i, h].astype(F32).reshape(size, lev)
        nodes = [
            [strip[pl.ds(i * size + x * 16 + base + k, nel, stride=64), :] for k in range(4)]
            for x in range(4)
        ]
        for x in range(4):
            dx = combine(GRAD[x], [nodes[m][node] for m in range(4)])
            dy = combine(GRAD[node], nodes[x])
            at = x * 16 + base + node
            u = vstrip[pl.ds(2 * i * size + at, nel, stride=64), :]
            v = vstrip[pl.ds((2 * i + 1) * size + at, nel, stride=64), :]
            out[pl.ds(x, nel, stride=4), :] = -(u * dx + v * dy)


def edges(tracer, winds):
    nx, ny, lev = tracer.shape
    shapes = [(ny, lev)] * 2 + [(nx, lev)] * 2
    return call(
        edges_kernel,
        [jax.ShapeDtypeStruct(s, F32) for s in shapes],
        tracer, winds,
        vmem=53, flops=10**6, moved=3 * 10**6,
        in_specs=[pl.BlockSpec(memory_space=pltpu.HBM)] * 2,
        scratch_shapes=[
            pltpu.VMEM((2, 4, ny, lev), BF16),
            pltpu.VMEM((2, 2, ny, lev), BF16),
            pltpu.VMEM((2, nx, 16, lev), BF16),
            pltpu.VMEM((2, 2, nx, 16, lev), BF16),
            pltpu.VMEM((8 * ny, lev), F32),
            pltpu.VMEM((4 * ny, lev), F32),
            pltpu.VMEM((2 * nx * 16, lev), F32),
            pltpu.VMEM((4 * nx * 16, lev), F32),
            pltpu.SemaphoreType.DMA((2, 4)),
        ],
    )


def sides_kernel(ey0, ey3, xprev, xnext, out0, out3, line):
    nx, lev = ey0.shape
    ny = xprev.shape[0]
    position = lax.broadcasted_iota(I32, (nx, lev), 0) & 3
    for mid, row, out in ((ey0, 0, out0), (ey3, ny - 1, out3)):
        line[pl.ds(7, 1), :] = xprev[pl.ds(row, 1), :]
        line[pl.ds(8, nx), :] = mid[...]
        line[pl.ds(8 + nx, 1), :] = xnext[pl.ds(row, 1), :]
        here = line[pl.ds(8, nx), :]
        back = 0.5 * (here + line[pl.ds(7, nx), :])
        front = 0.5 * (here + line[pl.ds(9, nx), :])
        out[...] = jnp.where(position == 3, front, jnp.where(position == 0, back, here))


def sides(ey0, ey3, xprev, xnext):
    return call(
        sides_kernel,
        [jax.ShapeDtypeStruct(ey0.shape, F32)] * 2,
        ey0, ey3, xprev, xnext,
        vmem=4, flops=10**5, moved=2 * 10**5,
        scratch_shapes=[pltpu.VMEM((ey0.shape[0] + 16, ey0.shape[1]), F32)],
    )


GROUP = 32


def pack(cap, owners_ref, slot_ref, table_ref, values_ref, low_ref, out_ref):
    cols = owners_ref.shape[1]
    lev = out_ref.shape[1]
    rows = GROUP * cap
    each = 2 * cap + 8
    owner = owners_ref[...]
    high = owner // GROUP
    place = (owner - high * GROUP) * cap + slot_ref[...]
    sub = lax.broadcasted_iota(I32, (rows, cols), 0)
    low_ref[...] = (sub == place).astype(F32).astype(BF16)
    none = jnp.zeros((rows, cols), BF16)
    high_all = jnp.broadcast_to(high.astype(F32).astype(BF16), (rows, cols))
    for i in range(table_ref.shape[0] // GROUP):
        hot = jnp.where(high_all == jnp.full((rows, cols), float(i), BF16), low_ref[...], none)
        packed = jnp.dot(hot, values_ref[...], preferred_element_type=F32)
        pieces = []
        for o in range(GROUP):
            line = table_ref[pl.ds(i * GROUP + o, 1), :]
            pieces.append(packed[o * cap : (o + 1) * cap, :lev])
            pieces.append(packed[o * cap : (o + 1) * cap, lev:])
            pieces.append(jnp.broadcast_to(line, (8, lev)))
        out_ref[pl.ds(i * GROUP * each, GROUP * each), :] = jnp.concatenate(pieces, axis=0).astype(BF16)


def cells_of(nodes, cells_ref, row, ne):
    cells = cell_pair(nodes)
    for a in range(2):
        for b in range(2):
            cells_ref[pl.ds(row + a * 2 * ne + b, ne, stride=2), :] = cells[a][b]


def columns_kernel(owners_ref, classes_ref, temper_hbm, slot_ref, table_ref, out_ref,
                   temper_ref, nodes_ref, cells_ref, sem):
    copy = pltpu.make_async_copy(temper_hbm, temper_ref, sem)
    copy.start()
    cols = owners_ref.shape[1]
    nx, ny, lev = temper_ref.shape
    ne = ny // 4
    devices = table_ref.shape[0]
    chunk = 256
    sub = lax.broadcasted_iota(I32, (devices, chunk), 0)
    upper = (
        lax.broadcasted_iota(I32, (chunk, chunk), 0) < lax.broadcasted_iota(I32, (chunk, chunk), 1)
    ).astype(F32).astype(BF16)
    ones = jnp.ones((chunk, chunk), BF16)
    running = jnp.zeros((devices, chunk), F32)
    table = jnp.zeros((devices, 128), F32)
    slots_sub = lax.broadcasted_iota(I32, (128, chunk), 0)
    for i in range(cols // chunk):
        owner = owners_ref[:, pl.ds(i * chunk, chunk)]
        hit = sub == owner
        hot = hit.astype(F32)
        hot16 = hot.astype(BF16)
        earlier = running + jnp.dot(hot16, upper, preferred_element_type=F32)
        slot = jnp.sum(jnp.where(hit, earlier, 0.0), axis=0, keepdims=True).astype(I32)
        running = running + jnp.dot(hot16, ones, preferred_element_type=F32)
        slot_ref[:, pl.ds(i * chunk, chunk)] = slot
        cost = classes_ref[:, pl.ds(i * chunk, chunk)].astype(F32)
        placed = jnp.where(slots_sub == slot, cost, 0.0).astype(BF16)
        table = table + lax.dot_general(
            hot16, placed, (((1,), (1,)), ((), ())), preferred_element_type=F32
        )
    table_ref[...] = table
    copy.wait()

    def element(e, _):
        base = pl.multiple_of(e * 4 * ny, 8)
        for x in range(4):
            nodes_ref[pl.ds(base + x * ny, ny), :] = temper_ref[4 * e + x].astype(F32)
        nodes = [
            [nodes_ref[pl.ds(base + x * ny + k, ne, stride=4), :] for k in range(4)]
            for x in range(4)
        ]
        cells_of(nodes, cells_ref, pl.multiple_of(e * ny, 8), ne)
        return 0

    lax.fori_loop(0, nx // 4, element, 0, unroll=2)
    out_ref[...] = cells_ref[...].astype(BF16)


def columns_stage(owners, classes, temper, devices):
    nx, ny, lev = temper.shape
    cols = owners.shape[1]
    return call(
        columns_kernel,
        [
            jax.ShapeDtypeStruct((1, cols), I32),
            jax.ShapeDtypeStruct((devices, 128), F32),
            jax.ShapeDtypeStruct((cols, lev), BF16),
        ],
        owners, classes, temper,
        vmem=16, flops=10**9, moved=4 * 10**6,
        in_specs=[pl.BlockSpec(memory_space=pltpu.VMEM)] * 2
        + [pl.BlockSpec(memory_space=pltpu.HBM)],
        scratch_shapes=[
            pltpu.VMEM((nx, ny, lev), BF16),
            pltpu.VMEM((nx * ny, lev), F32),
            pltpu.VMEM((nx * ny // 4, lev), F32),
            pltpu.SemaphoreType.DMA,
        ],
    )


CHUNKS = 4


def tendency_kernel(tracer_ref, winds_ref, nodes_ref, tend_ref, u_ref, v_ref):
    nx, ny, lev = tracer_ref.shape
    ne = ny // 4

    def element(e, _):
        base = pl.multiple_of(e * 4 * ny, 8)
        for x in range(4):
            nodes_ref[pl.ds(base + x * ny, ny), :] = tracer_ref[4 * e + x].astype(F32)
            u_ref[pl.ds(base + x * ny, ny), :] = winds_ref[0, 4 * e + x].astype(F32)
            v_ref[pl.ds(base + x * ny, ny), :] = winds_ref[1, 4 * e + x].astype(F32)
        for t in range(ne // 8):
            off = t * 32
            nodes = [
                [nodes_ref[pl.ds(base + x * ny + off + k, 8, stride=4), :] for k in range(4)]
                for x in range(4)
            ]
            for x in range(4):
                for k in range(4):
                    dx = combine(GRAD[x], [nodes[m][k] for m in range(4)])
                    dy = combine(GRAD[k], nodes[x])
                    u = u_ref[pl.ds(base + x * ny + off + k, 8, stride=4), :]
                    v = v_ref[pl.ds(base + x * ny + off + k, 8, stride=4), :]
                    tend_ref[pl.ds(base + x * ny + k * ne + t * 8, 8), :] = -(u * dx + v * dy)
        return 0

    lax.fori_loop(0, nx // 4, element, 0, unroll=2)


def tendency_stage(tracer, winds):
    nx, ny, lev = tracer.shape
    in_vmem = pl.BlockSpec(memory_space=pltpu.VMEM)
    return call(
        tendency_kernel,
        [jax.ShapeDtypeStruct((nx * ny, lev), F32)] * 2,
        tracer, winds,
        vmem=20, flops=2 * 10**9, moved=8 * 10**6,
        in_specs=[in_vmem] * 2,
        out_specs=[in_vmem] * 2,
        scratch_shapes=[pltpu.VMEM((nx * ny, lev), F32)] * 2,
    )


def tracer_kernel(cap, nodes_ref, tend_ref, xprev, xnext, yprev, ynext, owners_ref, slot_ref,
                  table_ref, temper_ref, new_hbm, out_ref, new_ref, fresh_ref, cells_ref,
                  values_ref, low_ref, out_sem):
    nx, ny, lev = new_ref.shape
    ne = ny // 4
    part = nx // CHUNKS
    elements = nx // 4

    def put(c):
        rows = pl.ds(c * part, part)
        return pltpu.make_async_copy(new_ref.at[rows], new_hbm.at[rows], out_sem.at[c])

    first = lax.broadcasted_iota(I32, (ne, lev), 0) == 0
    last = lax.broadcasted_iota(I32, (ne, lev), 0) == ne - 1

    def assemble(e, _):
        base = pl.multiple_of(e * 4 * ny, 8)
        back = pl.multiple_of(jnp.maximum(e * 4 - 1, 0) * ny, 8)
        front = pl.multiple_of(jnp.minimum(e * 4 + 4, nx - 1) * ny, 8)
        rounded = []
        for x in range(4):
            lines = [tend_ref[pl.ds(base + x * ny + k * ne, ne), :] for k in range(4)]
            if x == 0:
                other = [
                    jnp.where(e == 0, xprev[pl.ds(k * ne, ne), :], tend_ref[pl.ds(back + k * ne, ne), :])
                    for k in range(4)
                ]
                lines = [0.5 * (lines[k] + other[k]) for k in range(4)]
            if x == 3:
                other = [
                    jnp.where(
                        e == elements - 1,
                        xnext[pl.ds(k * ne, ne), :],
                        tend_ref[pl.ds(front + k * ne, ne), :],
                    )
                    for k in range(4)
                ]
                lines = [0.5 * (lines[k] + other[k]) for k in range(4)]
            before = yprev[pl.ds(4 * e + x, 1), :]
            after = ynext[pl.ds(4 * e + x, 1), :]
            low = jnp.where(first, before, pltpu.roll(lines[3], 1, 0))
            high = jnp.where(last, after, pltpu.roll(lines[0], ne - 1, 0))
            whole = [0.5 * (lines[0] + low), lines[1], lines[2], 0.5 * (lines[3] + high)]
            row = []
            for k in range(4):
                where = pl.ds(base + x * ny + k, ne, stride=4)
                fresh = (nodes_ref[where, :] + STEP_SIZE * whole[k]).astype(BF16).astype(F32)
                fresh_ref[where, :] = fresh
                row.append(fresh)
            rounded.append(row)
            new_ref[4 * e + x] = fresh_ref[pl.ds(base + x * ny, ny), :].astype(BF16)
        cells_of(rounded, cells_ref, pl.multiple_of(e * ny, 8), ne)
        return 0

    per = part // 4
    for c in range(CHUNKS):
        lax.fori_loop(c * per, (c + 1) * per, assemble, 0, unroll=2)
        put(c).start()
    values_ref[:, :lev] = cells_ref[...].astype(BF16)
    values_ref[:, lev:] = temper_ref[...]
    pack(cap, owners_ref, slot_ref, table_ref, values_ref, low_ref, out_ref)
    for c in range(CHUNKS):
        put(c).wait()


def tracer_stage(shape, nodes, tend, halos, owners, slots, table, temper_cells, cap):
    nx, ny, lev = shape
    cols = owners.shape[1]
    devices = table.shape[0]
    in_vmem = pl.BlockSpec(memory_space=pltpu.VMEM)
    return call(
        functools.partial(tracer_kernel, cap),
        [
            jax.ShapeDtypeStruct((nx, ny, lev), BF16),
            jax.ShapeDtypeStruct((devices * (2 * cap + 8), lev), BF16),
        ],
        nodes, tend, *halos, owners, slots, table, temper_cells,
        vmem=30, flops=4 * 10**9, moved=8 * 10**6,
        in_specs=[in_vmem] * 10,
        out_specs=[pl.BlockSpec(memory_space=pltpu.HBM), in_vmem],
        scratch_shapes=[
            pltpu.VMEM((nx, ny, lev), BF16),
            pltpu.VMEM((nx * ny, lev), F32),
            pltpu.VMEM((cols, lev), F32),
            pltpu.VMEM((cols, 2 * lev), BF16),
            pltpu.VMEM((GROUP * cap, cols), BF16),
            pltpu.SemaphoreType.DMA((CHUNKS,)),
        ],
    )


PIECES = 2


def radiate_kernel(cap, x_ref, aerosol_hbm, win_ref, wout_ref, out_ref, aerosol_ref,
                   depth_a, depth_b, trans_a, trans_b, bound_a, bound_b, sem):
    blocks, rows, width = aerosol_ref.shape
    lev = x_ref.shape[1]
    each = 2 * cap + 8
    sources = rows // cap
    piece = rows // PIECES

    def fetches(block):
        return [
            pltpu.make_async_copy(
                aerosol_hbm.at[pl.ds(block * rows + j * piece, piece)],
                aerosol_ref.at[block, pl.ds(j * piece, piece)],
                sem.at[block, j],
            )
            for j in range(PIECES)
        ]

    for block in range(blocks):
        for copy in fetches(block):
            copy.start()

    lane = lax.broadcasted_iota(I32, (8, lev), 1)
    sub = lax.broadcasted_iota(I32, (8, lev), 0)
    ones = jnp.ones((lev, lev), BF16)

    def begin(block, bound):
        tracer, temper, mine = [], [], []
        for s in range(sources):
            lines = x_ref[pl.ds((block * sources + s) * each, each), :].astype(F32)
            tracer.append(lines[:cap])
            temper.append(lines[cap : 2 * cap])
            mine += [jnp.where(lane == sub + 8 * j, lines[2 * cap :], 0.0) for j in range(cap // 8)]
        state = jnp.concatenate(
            [jnp.concatenate(tracer, axis=0), jnp.concatenate(temper, axis=0)], axis=1
        ).astype(BF16)
        mine = jnp.concatenate(mine, axis=0).astype(BF16)
        cost = jnp.dot(mine, ones, preferred_element_type=F32)
        for g in range(1, 4):
            bound[g - 1] = jnp.where(cost > g - 0.5, 120.0, -1e30)
        return state

    half = width // 2

    def deepen(state, depth, h):
        at = pl.ds(h * half, half)
        depth[:, at] = jnp.dot(state, win_ref[:, at], preferred_element_type=F32)

    step, tile = 256, 64
    parts = width // step

    def middle(block, depth, bound, trans, chunks):
        for i, r in [(i, r) for i in chunks for r in range(0, rows, tile)]:
            at, line = pl.ds(i * step, step), pl.ds(r, tile)
            group = i * 4 // parts
            top = jnp.concatenate([bound[group - 1, line]] * (step // lev), axis=1) if group else 120.0
            capped = jnp.minimum(depth[line, at] * -LOG2E, top)
            soft = capped - jnp.log2(1.0 + jnp.exp2(capped))
            kept = jnp.exp2(soft * aerosol_ref[block, line, at].astype(F32)).astype(BF16)
            trans[line, at] = kept

    def finish(block, trans):
        out_ref[pl.ds(block * rows, rows), :] = jnp.dot(
            trans[...], wout_ref[...], preferred_element_type=F32
        ).astype(BF16)

    def advance(block, following, depth, bound, trans, depth_next, bound_next, before, trans_before):
        for copy in fetches(block):
            copy.wait()
        state = begin(following, bound_next)
        deepen(state, depth_next, 0)
        middle(block, depth, bound, trans, range(0, 3))
        finish(before, trans_before)
        middle(block, depth, bound, trans, range(3, 6))
        deepen(state, depth_next, 1)
        middle(block, depth, bound, trans, range(6, parts))

    state = begin(0, bound_a)
    deepen(state, depth_a, 0)
    deepen(state, depth_a, 1)

    def pair(i, _):
        first = 2 * i
        later = jnp.minimum(first + 2, blocks - 1)
        before = jnp.maximum(first - 1, 0)
        advance(first, first + 1, depth_a, bound_a, trans_a, depth_b, bound_b, before, trans_b)
        advance(first + 1, later, depth_b, bound_b, trans_b, depth_a, bound_a, first, trans_a)
        return 0

    lax.fori_loop(0, blocks // 2, pair, 0)
    finish(blocks - 1, trans_b)


def radiate(arrived, aerosol, band_in, band_out, cap):
    lev = arrived.shape[1]
    rows, width = aerosol.shape
    block = 8 * cap
    in_vmem = pl.BlockSpec(memory_space=pltpu.VMEM)
    return call(
        functools.partial(radiate_kernel, cap),
        jax.ShapeDtypeStruct((rows, 2 * lev), BF16),
        arrived, aerosol, band_in, band_out,
        vmem=46, flops=7 * 10**9, moved=20 * 10**6,
        in_specs=[in_vmem, pl.BlockSpec(memory_space=pltpu.HBM), in_vmem, in_vmem],
        scratch_shapes=[
            pltpu.VMEM((rows // block, block, width), BF16),
            pltpu.VMEM((block, width), F32),
            pltpu.VMEM((block, width), F32),
            pltpu.VMEM((block, width), BF16),
            pltpu.VMEM((block, width), BF16),
            pltpu.VMEM((3, block, lev), F32),
            pltpu.VMEM((3, block, lev), F32),
            pltpu.SemaphoreType.DMA((rows // block, PIECES)),
        ],
    )


def gather_kernel(cap, owners_ref, slot_ref, back_ref, out_hbm, out_ref, hot_ref, sem):
    cols, rows = out_ref.shape[0], back_ref.shape[0]
    block, wide = hot_ref.shape[1], 128
    lane = lax.broadcasted_iota(I32, (wide, wide), 1)
    none = jnp.zeros((wide, wide), BF16)

    def ship(i):
        at = pl.ds(i * block, block)
        return pltpu.make_async_copy(out_ref.at[at], out_hbm.at[at], sem.at[i])

    for i in range(cols // block):
        for j in range(block // wide):
            at = pl.ds(i * block + j * wide, wide)
            line = (owners_ref[:, at] * cap + slot_ref[:, at]).astype(F32)
            place = jnp.transpose(jnp.broadcast_to(line, (wide, wide))).astype(I32)
            high = (place >> 7).astype(F32).astype(BF16)
            low = (lane == (place & (wide - 1))).astype(F32).astype(BF16)
            for r in range(rows // wide):
                here = jnp.full((wide, wide), float(r), BF16)
                hot_ref[i % 2, pl.ds(j * wide, wide), pl.ds(r * wide, wide)] = jnp.where(
                    high == here, low, none
                )
        out_ref[pl.ds(i * block, block), :] = jnp.dot(
            hot_ref[i % 2], back_ref[...], preferred_element_type=F32
        ).astype(BF16)
        ship(i).start()
    for i in range(cols // block):
        ship(i).wait()


def gather(owners, slots, back, cap):
    return call(
        functools.partial(gather_kernel, cap),
        jax.ShapeDtypeStruct((owners.shape[1], back.shape[1]), BF16),
        owners, slots, back,
        vmem=24, flops=3 * 10**9, moved=3 * 10**6,
        in_specs=[pl.BlockSpec(memory_space=pltpu.VMEM)] * 3,
        out_specs=pl.BlockSpec(memory_space=pl.ANY),
        scratch_shapes=[
            pltpu.VMEM((owners.shape[1], back.shape[1]), BF16),
            pltpu.VMEM((2, owners.shape[1] // 4, back.shape[0]), BF16),
            pltpu.SemaphoreType.DMA((4,)),
        ],
    )


def exchange(x):
    return lax.all_to_all(x, ("dyn", "col"), split_axis=0, concat_axis=0, tiled=True)


def shards(tracer, temper, winds, owners, classes, aerosol, band_in, band_out):
    n_dyn, n_col = lax.axis_size("dyn"), lax.axis_size("col")
    devices = n_dyn * n_col
    lev = tracer.shape[2]
    cap = aerosol.shape[1] // devices

    def send(x, by_dyn, by_col):
        pairs = [
            (i * n_col + j, ((i + by_dyn) % n_dyn) * n_col + (j + by_col) % n_col)
            for i in range(n_dyn)
            for j in range(n_col)
        ]
        return lax.ppermute(x, ("dyn", "col"), pairs)

    owners = owners.reshape(1, -1)
    ex0, ex3, ey0, ey3 = edges(tracer, winds)
    xprev, xnext = send(ex3, 1, 0), send(ex0, -1, 0)
    nodes, tend = tendency_stage(tracer, winds)
    slots, table, temper_cells = columns_stage(owners, classes.reshape(1, -1), temper, devices)
    side0, side3 = sides(ey0, ey3, xprev, xnext)
    yprev, ynext = send(side3, 0, 1), send(side0, 0, -1)
    tracer_new, outgoing = tracer_stage(
        tracer.shape, nodes, tend, (xprev, xnext, yprev, ynext), owners, slots, table, temper_cells, cap
    )
    each = 2 * cap + 8
    arrived = exchange(outgoing.reshape(devices, each, lev)).reshape(-1, lev)
    result = radiate(arrived, aerosol[0], band_in, band_out, cap)
    back = exchange(result.reshape(devices, cap, 2 * lev)).reshape(-1, 2 * lev)
    return (tracer_new, gather(owners, slots, back, cap))


def solution(mesh):
    return jax.shard_map(
        shards,
        mesh=mesh,
        in_specs=(
            P("dyn", "col", None),
            P("dyn", "col", None),
            P(None, "dyn", "col", None),
            P(("dyn", "col"), None),
            P(("dyn", "col")),
            P(("dyn", "col"), None, None),
            P(),
            P(),
        ),
        out_specs=(P("dyn", "col", None), P(("dyn", "col"), None)),
        check_vma=False,
    )
```

```python
import functools
import math

import jax
import jax.numpy as jnp
import numpy as np
from jax import lax
from jax.experimental import pallas as pl
from jax.experimental.pallas import tpu as pltpu
from jax.sharding import PartitionSpec as P

STEP_SIZE = 0.1
F32, BF16, I32 = jnp.float32, jnp.bfloat16, jnp.int32
MIB = 1024 * 1024
LOG2E = 1.4426950408889634


def lagrange_tables():
    points = np.array([-1.0, -1.0 / math.sqrt(5.0), 1.0 / math.sqrt(5.0), 1.0])
    products = np.array(
        [np.prod([points[r] - points[k] for k in range(4) if k != r]) for r in range(4)]
    )
    derivative = np.zeros((4, 4))
    for r in range(4):
        for c in range(4):
            if r == c:
                derivative[r, c] = np.sum(
                    [1.0 / (points[r] - points[k]) for k in range(4) if k != r]
                )
            else:
                derivative[r, c] = products[r] / (products[c] * (points[r] - points[c]))
    average = np.array([[1.0 / 6.0, 5.0 / 6.0, 0.0, 0.0], [0.0, 0.0, 5.0 / 6.0, 1.0 / 6.0]])
    return (derivative, average)


GRAD, PG2 = lagrange_tables()


def combine(weights, pieces):
    total = None
    for weight, piece in zip(weights, pieces):
        if abs(float(weight)) > 1e-12:
            term = float(weight) * piece
            total = term if total is None else total + term
    return total


def cell_pair(nodes):
    halves = [[combine(PG2[a], [nodes[x][k] for x in range(4)]) for k in range(4)] for a in range(2)]
    return [[combine(PG2[b], halves[a]) for b in range(2)] for a in range(2)]


def call(kernel, out_shape, *args, vmem, flops=0, moved=0, **kw):
    return pl.pallas_call(
        kernel,
        out_shape=out_shape,
        compiler_params=pltpu.CompilerParams(vmem_limit_bytes=vmem * MIB),
        cost_estimate=pl.CostEstimate(flops=flops, bytes_accessed=moved, transcendentals=0),
        **kw,
    )(*args)


def full(shape):
    return pl.BlockSpec(shape, lambda *_: (0,) * len(shape))


def edges_kernel(tracer, winds, ex0, ex3, ey0, ey3, xs, xw, ys, yw, line, wind, strip, vstrip, sem):
    nx, ny, lev = tracer.shape
    ne = ny // 4
    copies = []
    for i, (x, x4, y) in enumerate(((0, 0, 0), (nx - 1, nx - 4, ny - 16))):
        copies.append((
            pltpu.make_async_copy(tracer.at[pl.ds(x4, 4)], xs.at[i], sem.at[i, 0]),
            pltpu.make_async_copy(winds.at[:, x], xw.at[i], sem.at[i, 1]),
            pltpu.make_async_copy(tracer.at[:, pl.ds(y, 16)], ys.at[i], sem.at[i, 2]),
            pltpu.make_async_copy(winds.at[:, :, pl.ds(y, 16)], yw.at[i], sem.at[i, 3]),
        ))
    for part in (0, 2):
        for group in copies:
            group[part].start()
            group[part + 1].start()

    for i, (node, out) in enumerate(((0, ex0), (3, ex3))):
        copies[i][0].wait()
        copies[i][1].wait()
        for x in range(4):
            line[pl.ds((4 * i + x) * ny, ny), :] = xs[i, x].astype(F32)
        for h in range(2):
            wind[pl.ds((2 * i + h) * ny, ny), :] = xw[i, h].astype(F32)
        nodes = [
            [line[pl.ds((4 * i + x) * ny + k, ne, stride=4), :] for k in range(4)] for x in range(4)
        ]
        for k in range(4):
            dx = combine(GRAD[node], [nodes[m][k] for m in range(4)])
            dy = combine(GRAD[k], nodes[node])
            u = wind[pl.ds(2 * i * ny + k, ne, stride=4), :]
            v = wind[pl.ds((2 * i + 1) * ny + k, ne, stride=4), :]
            out[pl.ds(k * ne, ne), :] = -(u * dx + v * dy)

    size = nx * 16
    for i, (base, node, out) in enumerate(((0, 0, ey0), (12, 3, ey3))):
        copies[i][2].wait()
        copies[i][3].wait()
        nel = nx // 4
        strip[pl.ds(i * size, size), :] = ys[i].astype(F32).reshape(size, lev)
        for h in range(2):
            vstrip[pl.ds((2 * i + h) * size, size), :] = yw[i, h].astype(F32).reshape(size, lev)
        nodes = [
            [strip[pl.ds(i * size + x * 16 + base + k, nel, stride=64), :] for k in range(4)]
            for x in range(4)
        ]
        for x in range(4):
            dx = combine(GRAD[x], [nodes[m][node] for m in range(4)])
            dy = combine(GRAD[node], nodes[x])
            at = x * 16 + base + node
            u = vstrip[pl.ds(2 * i * size + at, nel, stride=64), :]
            v = vstrip[pl.ds((2 * i + 1) * size + at, nel, stride=64), :]
            out[pl.ds(x, nel, stride=4), :] = -(u * dx + v * dy)


def edges(tracer, winds):
    nx, ny, lev = tracer.shape
    shapes = [(ny, lev)] * 2 + [(nx, lev)] * 2
    return call(
        edges_kernel,
        [jax.ShapeDtypeStruct(s, F32) for s in shapes],
        tracer, winds,
        vmem=53, flops=10**6, moved=3 * 10**6,
        in_specs=[pl.BlockSpec(memory_space=pltpu.HBM)] * 2,
        scratch_shapes=[
            pltpu.VMEM((2, 4, ny, lev), BF16),
            pltpu.VMEM((2, 2, ny, lev), BF16),
            pltpu.VMEM((2, nx, 16, lev), BF16),
            pltpu.VMEM((2, 2, nx, 16, lev), BF16),
            pltpu.VMEM((8 * ny, lev), F32),
            pltpu.VMEM((4 * ny, lev), F32),
            pltpu.VMEM((2 * nx * 16, lev), F32),
            pltpu.VMEM((4 * nx * 16, lev), F32),
            pltpu.SemaphoreType.DMA((2, 4)),
        ],
    )


def sides_kernel(ey0, ey3, xprev, xnext, out0, out3, line):
    nx, lev = ey0.shape
    ny = xprev.shape[0]
    position = lax.broadcasted_iota(I32, (nx, lev), 0) & 3
    for mid, row, out in ((ey0, 0, out0), (ey3, ny - 1, out3)):
        line[pl.ds(7, 1), :] = xprev[pl.ds(row, 1), :]
        line[pl.ds(8, nx), :] = mid[...]
        line[pl.ds(8 + nx, 1), :] = xnext[pl.ds(row, 1), :]
        here = line[pl.ds(8, nx), :]
        back = 0.5 * (here + line[pl.ds(7, nx), :])
        front = 0.5 * (here + line[pl.ds(9, nx), :])
        out[...] = jnp.where(position == 3, front, jnp.where(position == 0, back, here))


def sides(ey0, ey3, xprev, xnext):
    return call(
        sides_kernel,
        [jax.ShapeDtypeStruct(ey0.shape, F32)] * 2,
        ey0, ey3, xprev, xnext,
        vmem=4, flops=10**5, moved=2 * 10**5,
        scratch_shapes=[pltpu.VMEM((ey0.shape[0] + 16, ey0.shape[1]), F32)],
    )


GROUP = 32


def pack(cap, owners_ref, slot_ref, table_ref, values_ref, low_ref, out_ref):
    cols = owners_ref.shape[1]
    lev = out_ref.shape[1]
    rows = GROUP * cap
    each = 2 * cap + 8
    owner = owners_ref[...]
    high = owner // GROUP
    place = (owner - high * GROUP) * cap + slot_ref[...]
    sub = lax.broadcasted_iota(I32, (rows, cols), 0)
    low_ref[...] = (sub == place).astype(F32).astype(BF16)
    none = jnp.zeros((rows, cols), BF16)
    high_all = jnp.broadcast_to(high.astype(F32).astype(BF16), (rows, cols))
    for i in range(table_ref.shape[0] // GROUP):
        hot = jnp.where(high_all == jnp.full((rows, cols), float(i), BF16), low_ref[...], none)
        packed = jnp.dot(hot, values_ref[...], preferred_element_type=F32)
        pieces = []
        for o in range(GROUP):
            line = table_ref[pl.ds(i * GROUP + o, 1), :]
            pieces.append(packed[o * cap : (o + 1) * cap, :lev])
            pieces.append(packed[o * cap : (o + 1) * cap, lev:])
            pieces.append(jnp.broadcast_to(line, (8, lev)))
        out_ref[pl.ds(i * GROUP * each, GROUP * each), :] = jnp.concatenate(pieces, axis=0).astype(BF16)


def cells_of(nodes, cells_ref, row, ne):
    cells = cell_pair(nodes)
    for a in range(2):
        for b in range(2):
            cells_ref[pl.ds(row + a * 2 * ne + b, ne, stride=2), :] = cells[a][b]


def columns_kernel(owners_ref, classes_ref, temper_hbm, slot_ref, table_ref, out_ref,
                   temper_ref, nodes_ref, cells_ref, sem):
    copy = pltpu.make_async_copy(temper_hbm, temper_ref, sem)
    copy.start()
    cols = owners_ref.shape[1]
    nx, ny, lev = temper_ref.shape
    ne = ny // 4
    devices = table_ref.shape[0]
    chunk = 256
    sub = lax.broadcasted_iota(I32, (devices, chunk), 0)
    upper = (
        lax.broadcasted_iota(I32, (chunk, chunk), 0) < lax.broadcasted_iota(I32, (chunk, chunk), 1)
    ).astype(F32).astype(BF16)
    ones = jnp.ones((chunk, chunk), BF16)
    running = jnp.zeros((devices, chunk), F32)
    table = jnp.zeros((devices, 128), F32)
    slots_sub = lax.broadcasted_iota(I32, (128, chunk), 0)
    for i in range(cols // chunk):
        owner = owners_ref[:, pl.ds(i * chunk, chunk)]
        hit = sub == owner
        hot = hit.astype(F32)
        hot16 = hot.astype(BF16)
        earlier = running + jnp.dot(hot16, upper, preferred_element_type=F32)
        slot = jnp.sum(jnp.where(hit, earlier, 0.0), axis=0, keepdims=True).astype(I32)
        running = running + jnp.dot(hot16, ones, preferred_element_type=F32)
        slot_ref[:, pl.ds(i * chunk, chunk)] = slot
        cost = classes_ref[:, pl.ds(i * chunk, chunk)].astype(F32)
        placed = jnp.where(slots_sub == slot, cost, 0.0).astype(BF16)
        table = table + lax.dot_general(
            hot16, placed, (((1,), (1,)), ((), ())), preferred_element_type=F32
        )
    table_ref[...] = table
    copy.wait()

    def element(e, _):
        base = pl.multiple_of(e * 4 * ny, 8)
        for x in range(4):
            nodes_ref[pl.ds(base + x * ny, ny), :] = temper_ref[4 * e + x].astype(F32)
        nodes = [
            [nodes_ref[pl.ds(base + x * ny + k, ne, stride=4), :] for k in range(4)]
            for x in range(4)
        ]
        cells_of(nodes, cells_ref, pl.multiple_of(e * ny, 8), ne)
        return 0

    lax.fori_loop(0, nx // 4, element, 0, unroll=2)
    out_ref[...] = cells_ref[...].astype(BF16)


def columns_stage(owners, classes, temper, devices):
    nx, ny, lev = temper.shape
    cols = owners.shape[1]
    return call(
        columns_kernel,
        [
            jax.ShapeDtypeStruct((1, cols), I32),
            jax.ShapeDtypeStruct((devices, 128), F32),
            jax.ShapeDtypeStruct((cols, lev), BF16),
        ],
        owners, classes, temper,
        vmem=16, flops=10**9, moved=4 * 10**6,
        in_specs=[pl.BlockSpec(memory_space=pltpu.VMEM)] * 2
        + [pl.BlockSpec(memory_space=pltpu.HBM)],
        scratch_shapes=[
            pltpu.VMEM((nx, ny, lev), BF16),
            pltpu.VMEM((nx * ny, lev), F32),
            pltpu.VMEM((nx * ny // 4, lev), F32),
            pltpu.SemaphoreType.DMA,
        ],
    )


CHUNKS = 4


def tendency_kernel(tracer_ref, winds_ref, nodes_ref, tend_ref, u_ref, v_ref):
    nx, ny, lev = tracer_ref.shape
    ne = ny // 4

    def element(e, _):
        base = pl.multiple_of(e * 4 * ny, 8)
        for x in range(4):
            nodes_ref[pl.ds(base + x * ny, ny), :] = tracer_ref[4 * e + x].astype(F32)
            u_ref[pl.ds(base + x * ny, ny), :] = winds_ref[0, 4 * e + x].astype(F32)
            v_ref[pl.ds(base + x * ny, ny), :] = winds_ref[1, 4 * e + x].astype(F32)
        for t in range(ne // 8):
            off = t * 32
            nodes = [
                [nodes_ref[pl.ds(base + x * ny + off + k, 8, stride=4), :] for k in range(4)]
                for x in range(4)
            ]
            for x in range(4):
                for k in range(4):
                    dx = combine(GRAD[x], [nodes[m][k] for m in range(4)])
                    dy = combine(GRAD[k], nodes[x])
                    u = u_ref[pl.ds(base + x * ny + off + k, 8, stride=4), :]
                    v = v_ref[pl.ds(base + x * ny + off + k, 8, stride=4), :]
                    tend_ref[pl.ds(base + x * ny + k * ne + t * 8, 8), :] = -(u * dx + v * dy)
        return 0

    lax.fori_loop(0, nx // 4, element, 0, unroll=2)


def tendency_stage(tracer, winds):
    nx, ny, lev = tracer.shape
    in_vmem = pl.BlockSpec(memory_space=pltpu.VMEM)
    return call(
        tendency_kernel,
        [jax.ShapeDtypeStruct((nx * ny, lev), F32)] * 2,
        tracer, winds,
        vmem=20, flops=2 * 10**9, moved=8 * 10**6,
        in_specs=[in_vmem] * 2,
        out_specs=[in_vmem] * 2,
        scratch_shapes=[pltpu.VMEM((nx * ny, lev), F32)] * 2,
    )


def tracer_kernel(cap, nodes_ref, tend_ref, xprev, xnext, yprev, ynext, owners_ref, slot_ref,
                  table_ref, temper_ref, new_hbm, out_ref, new_ref, fresh_ref, cells_ref,
                  values_ref, low_ref, out_sem):
    nx, ny, lev = new_ref.shape
    ne = ny // 4
    part = nx // CHUNKS
    elements = nx // 4

    def put(c):
        rows = pl.ds(c * part, part)
        return pltpu.make_async_copy(new_ref.at[rows], new_hbm.at[rows], out_sem.at[c])

    first = lax.broadcasted_iota(I32, (ne, lev), 0) == 0
    last = lax.broadcasted_iota(I32, (ne, lev), 0) == ne - 1

    def assemble(e, _):
        base = pl.multiple_of(e * 4 * ny, 8)
        back = pl.multiple_of(jnp.maximum(e * 4 - 1, 0) * ny, 8)
        front = pl.multiple_of(jnp.minimum(e * 4 + 4, nx - 1) * ny, 8)
        rounded = []
        for x in range(4):
            lines = [tend_ref[pl.ds(base + x * ny + k * ne, ne), :] for k in range(4)]
            if x == 0:
                other = [
                    jnp.where(e == 0, xprev[pl.ds(k * ne, ne), :], tend_ref[pl.ds(back + k * ne, ne), :])
                    for k in range(4)
                ]
                lines = [0.5 * (lines[k] + other[k]) for k in range(4)]
            if x == 3:
                other = [
                    jnp.where(
                        e == elements - 1,
                        xnext[pl.ds(k * ne, ne), :],
                        tend_ref[pl.ds(front + k * ne, ne), :],
                    )
                    for k in range(4)
                ]
                lines = [0.5 * (lines[k] + other[k]) for k in range(4)]
            before = yprev[pl.ds(4 * e + x, 1), :]
            after = ynext[pl.ds(4 * e + x, 1), :]
            low = jnp.where(first, before, pltpu.roll(lines[3], 1, 0))
            high = jnp.where(last, after, pltpu.roll(lines[0], ne - 1, 0))
            whole = [0.5 * (lines[0] + low), lines[1], lines[2], 0.5 * (lines[3] + high)]
            row = []
            for k in range(4):
                where = pl.ds(base + x * ny + k, ne, stride=4)
                fresh = (nodes_ref[where, :] + STEP_SIZE * whole[k]).astype(BF16).astype(F32)
                fresh_ref[where, :] = fresh
                row.append(fresh)
            rounded.append(row)
            new_ref[4 * e + x] = fresh_ref[pl.ds(base + x * ny, ny), :].astype(BF16)
        cells_of(rounded, cells_ref, pl.multiple_of(e * ny, 8), ne)
        return 0

    per = part // 4
    for c in range(CHUNKS):
        lax.fori_loop(c * per, (c + 1) * per, assemble, 0, unroll=2)
        put(c).start()
    values_ref[:, :lev] = cells_ref[...].astype(BF16)
    values_ref[:, lev:] = temper_ref[...]
    pack(cap, owners_ref, slot_ref, table_ref, values_ref, low_ref, out_ref)
    for c in range(CHUNKS):
        put(c).wait()


def tracer_stage(shape, nodes, tend, halos, owners, slots, table, temper_cells, cap):
    nx, ny, lev = shape
    cols = owners.shape[1]
    devices = table.shape[0]
    in_vmem = pl.BlockSpec(memory_space=pltpu.VMEM)
    return call(
        functools.partial(tracer_kernel, cap),
        [
            jax.ShapeDtypeStruct((nx, ny, lev), BF16),
            jax.ShapeDtypeStruct((devices * (2 * cap + 8), lev), BF16),
        ],
        nodes, tend, *halos, owners, slots, table, temper_cells,
        vmem=30, flops=4 * 10**9, moved=8 * 10**6,
        in_specs=[in_vmem] * 10,
        out_specs=[pl.BlockSpec(memory_space=pltpu.HBM), in_vmem],
        scratch_shapes=[
            pltpu.VMEM((nx, ny, lev), BF16),
            pltpu.VMEM((nx * ny, lev), F32),
            pltpu.VMEM((cols, lev), F32),
            pltpu.VMEM((cols, 2 * lev), BF16),
            pltpu.VMEM((GROUP * cap, cols), BF16),
            pltpu.SemaphoreType.DMA((CHUNKS,)),
        ],
    )


PIECES = 2


def radiate_kernel(cap, x_ref, aerosol_hbm, win_ref, wout_ref, out_ref, aerosol_ref,
                   depth_a, depth_b, trans_a, trans_b, bound_a, bound_b, sem):
    blocks, rows, width = aerosol_ref.shape
    lev = x_ref.shape[1]
    each = 2 * cap + 8
    sources = rows // cap
    piece = rows // PIECES

    def fetches(block):
        return [
            pltpu.make_async_copy(
                aerosol_hbm.at[pl.ds(block * rows + j * piece, piece)],
                aerosol_ref.at[block, pl.ds(j * piece, piece)],
                sem.at[block, j],
            )
            for j in range(PIECES)
        ]

    for block in range(blocks):
        for copy in fetches(block):
            copy.start()

    lane = lax.broadcasted_iota(I32, (8, lev), 1)
    sub = lax.broadcasted_iota(I32, (8, lev), 0)
    ones = jnp.ones((lev, lev), BF16)

    def begin(block, bound):
        tracer, temper, mine = [], [], []
        for s in range(sources):
            lines = x_ref[pl.ds((block * sources + s) * each, each), :].astype(F32)
            tracer.append(lines[:cap])
            temper.append(lines[cap : 2 * cap])
            mine += [jnp.where(lane == sub + 8 * j, lines[2 * cap :], 0.0) for j in range(cap // 8)]
        state = jnp.concatenate(
            [jnp.concatenate(tracer, axis=0), jnp.concatenate(temper, axis=0)], axis=1
        ).astype(BF16)
        mine = jnp.concatenate(mine, axis=0).astype(BF16)
        cost = jnp.dot(mine, ones, preferred_element_type=F32)
        for g in range(1, 4):
            bound[g - 1] = jnp.where(cost > g - 0.5, 120.0, -1e30)
        return state

    half = width // 2

    def deepen(state, depth, h):
        at = pl.ds(h * half, half)
        depth[:, at] = jnp.dot(state, win_ref[:, at], preferred_element_type=F32)

    step, tile = 256, 128
    parts = width // step

    def middle(block, depth, bound, trans, chunks):
        for i, r in [(i, r) for i in chunks for r in range(0, rows, tile)]:
            at, line = pl.ds(i * step, step), pl.ds(r, tile)
            group = i * 4 // parts
            top = jnp.concatenate([bound[group - 1, line]] * (step // lev), axis=1) if group else 120.0
            capped = jnp.minimum(depth[line, at] * -LOG2E, top)
            soft = capped - jnp.log2(1.0 + jnp.exp2(capped))
            kept = jnp.exp2(soft * aerosol_ref[block, line, at].astype(F32)).astype(BF16)
            trans[line, at] = kept

    size = rows // 2

    def finish(block, trans, h):
        out_ref[pl.ds(block * rows + h * size, size), :] = jnp.dot(
            trans[pl.ds(h * size, size), :], wout_ref[...], preferred_element_type=F32
        ).astype(BF16)

    def advance(block, following, depth, bound, trans, depth_next, bound_next, before, trans_before):
        for copy in fetches(block):
            copy.wait()
        state = begin(following, bound_next)
        deepen(state, depth_next, 0)
        middle(block, depth, bound, trans, range(0, 2))
        finish(before, trans_before, 0)
        middle(block, depth, bound, trans, range(2, 4))
        finish(before, trans_before, 1)
        middle(block, depth, bound, trans, range(4, 6))
        deepen(state, depth_next, 1)
        middle(block, depth, bound, trans, range(6, parts))

    state = begin(0, bound_a)
    deepen(state, depth_a, 0)
    deepen(state, depth_a, 1)

    def pair(i, _):
        first = 2 * i
        later = jnp.minimum(first + 2, blocks - 1)
        before = jnp.maximum(first - 1, 0)
        advance(first, first + 1, depth_a, bound_a, trans_a, depth_b, bound_b, before, trans_b)
        advance(first + 1, later, depth_b, bound_b, trans_b, depth_a, bound_a, first, trans_a)
        return 0

    lax.fori_loop(0, blocks // 2, pair, 0)
    finish(blocks - 1, trans_b, 0)
    finish(blocks - 1, trans_b, 1)


def radiate(arrived, aerosol, band_in, band_out, cap):
    lev = arrived.shape[1]
    rows, width = aerosol.shape
    block = 16 * cap
    in_vmem = pl.BlockSpec(memory_space=pltpu.VMEM)
    return call(
        functools.partial(radiate_kernel, cap),
        jax.ShapeDtypeStruct((rows, 2 * lev), BF16),
        arrived, aerosol, band_in, band_out,
        vmem=46, flops=7 * 10**9, moved=20 * 10**6,
        in_specs=[in_vmem, pl.BlockSpec(memory_space=pltpu.HBM), in_vmem, in_vmem],
        scratch_shapes=[
            pltpu.VMEM((rows // block, block, width), BF16),
            pltpu.VMEM((block, width), F32),
            pltpu.VMEM((block, width), F32),
            pltpu.VMEM((block, width), BF16),
            pltpu.VMEM((block, width), BF16),
            pltpu.VMEM((3, block, lev), F32),
            pltpu.VMEM((3, block, lev), F32),
            pltpu.SemaphoreType.DMA((rows // block, PIECES)),
        ],
    )


def gather_kernel(cap, owners_ref, slot_ref, back_ref, out_hbm, out_ref, hot_ref, sem):
    cols, rows = out_ref.shape[0], back_ref.shape[0]
    block, wide = hot_ref.shape[1], 128
    lane = lax.broadcasted_iota(I32, (wide, wide), 1)
    none = jnp.zeros((wide, wide), BF16)

    def ship(i):
        at = pl.ds(i * block, block)
        return pltpu.make_async_copy(out_ref.at[at], out_hbm.at[at], sem.at[i])

    for i in range(cols // block):
        for j in range(block // wide):
            at = pl.ds(i * block + j * wide, wide)
            line = (owners_ref[:, at] * cap + slot_ref[:, at]).astype(F32)
            place = jnp.transpose(jnp.broadcast_to(line, (wide, wide))).astype(I32)
            high = (place >> 7).astype(F32).astype(BF16)
            low = (lane == (place & (wide - 1))).astype(F32).astype(BF16)
            for r in range(rows // wide):
                here = jnp.full((wide, wide), float(r), BF16)
                hot_ref[i % 2, pl.ds(j * wide, wide), pl.ds(r * wide, wide)] = jnp.where(
                    high == here, low, none
                )
        out_ref[pl.ds(i * block, block), :] = jnp.dot(
            hot_ref[i % 2], back_ref[...], preferred_element_type=F32
        ).astype(BF16)
        ship(i).start()
    for i in range(cols // block):
        ship(i).wait()


def gather(owners, slots, back, cap):
    return call(
        functools.partial(gather_kernel, cap),
        jax.ShapeDtypeStruct((owners.shape[1], back.shape[1]), BF16),
        owners, slots, back,
        vmem=24, flops=3 * 10**9, moved=3 * 10**6,
        in_specs=[pl.BlockSpec(memory_space=pltpu.VMEM)] * 3,
        out_specs=pl.BlockSpec(memory_space=pl.ANY),
        scratch_shapes=[
            pltpu.VMEM((owners.shape[1], back.shape[1]), BF16),
            pltpu.VMEM((2, owners.shape[1] // 4, back.shape[0]), BF16),
            pltpu.SemaphoreType.DMA((4,)),
        ],
    )


def exchange(x):
    return lax.all_to_all(x, ("dyn", "col"), split_axis=0, concat_axis=0, tiled=True)


def shards(tracer, temper, winds, owners, classes, aerosol, band_in, band_out):
    n_dyn, n_col = lax.axis_size("dyn"), lax.axis_size("col")
    devices = n_dyn * n_col
    lev = tracer.shape[2]
    cap = aerosol.shape[1] // devices

    def send(x, by_dyn, by_col):
        pairs = [
            (i * n_col + j, ((i + by_dyn) % n_dyn) * n_col + (j + by_col) % n_col)
            for i in range(n_dyn)
            for j in range(n_col)
        ]
        return lax.ppermute(x, ("dyn", "col"), pairs)

    owners = owners.reshape(1, -1)
    ex0, ex3, ey0, ey3 = edges(tracer, winds)
    xprev, xnext = send(ex3, 1, 0), send(ex0, -1, 0)
    nodes, tend = tendency_stage(tracer, winds)
    slots, table, temper_cells = columns_stage(owners, classes.reshape(1, -1), temper, devices)
    side0, side3 = sides(ey0, ey3, xprev, xnext)
    yprev, ynext = send(side3, 0, 1), send(side0, 0, -1)
    tracer_new, outgoing = tracer_stage(
        tracer.shape, nodes, tend, (xprev, xnext, yprev, ynext), owners, slots, table, temper_cells, cap
    )
    each = 2 * cap + 8
    arrived = exchange(outgoing.reshape(devices, each, lev)).reshape(-1, lev)
    result = radiate(arrived, aerosol[0], band_in, band_out, cap)
    back = exchange(result.reshape(devices, cap, 2 * lev)).reshape(-1, 2 * lev)
    return (tracer_new, gather(owners, slots, back, cap))


def solution(mesh):
    return jax.shard_map(
        shards,
        mesh=mesh,
        in_specs=(
            P("dyn", "col", None),
            P("dyn", "col", None),
            P(None, "dyn", "col", None),
            P(("dyn", "col"), None),
            P(("dyn", "col")),
            P(("dyn", "col"), None, None),
            P(),
            P(),
        ),
        out_specs=(P("dyn", "col", None), P(("dyn", "col"), None)),
        check_vma=False,
    )
```

```python
import functools
import math

import jax
import jax.numpy as jnp
import numpy as np
from jax import lax
from jax.experimental import pallas as pl
from jax.experimental.pallas import tpu as pltpu
from jax.sharding import PartitionSpec as P

STEP_SIZE = 0.1
F32, BF16, I32 = jnp.float32, jnp.bfloat16, jnp.int32
MIB = 1024 * 1024
LOG2E = 1.4426950408889634


def lagrange_tables():
    points = np.array([-1.0, -1.0 / math.sqrt(5.0), 1.0 / math.sqrt(5.0), 1.0])
    products = np.array(
        [np.prod([points[r] - points[k] for k in range(4) if k != r]) for r in range(4)]
    )
    derivative = np.zeros((4, 4))
    for r in range(4):
        for c in range(4):
            if r == c:
                derivative[r, c] = np.sum(
                    [1.0 / (points[r] - points[k]) for k in range(4) if k != r]
                )
            else:
                derivative[r, c] = products[r] / (products[c] * (points[r] - points[c]))
    average = np.array([[1.0 / 6.0, 5.0 / 6.0, 0.0, 0.0], [0.0, 0.0, 5.0 / 6.0, 1.0 / 6.0]])
    return (derivative, average)


GRAD, PG2 = lagrange_tables()


def combine(weights, pieces):
    total = None
    for weight, piece in zip(weights, pieces):
        if abs(float(weight)) > 1e-12:
            term = float(weight) * piece
            total = term if total is None else total + term
    return total


def cell_pair(nodes):
    halves = [[combine(PG2[a], [nodes[x][k] for x in range(4)]) for k in range(4)] for a in range(2)]
    return [[combine(PG2[b], halves[a]) for b in range(2)] for a in range(2)]


def call(kernel, out_shape, *args, vmem, flops=0, moved=0, **kw):
    return pl.pallas_call(
        kernel,
        out_shape=out_shape,
        compiler_params=pltpu.CompilerParams(vmem_limit_bytes=vmem * MIB),
        cost_estimate=pl.CostEstimate(flops=flops, bytes_accessed=moved, transcendentals=0),
        **kw,
    )(*args)


def full(shape):
    return pl.BlockSpec(shape, lambda *_: (0,) * len(shape))


def edges_kernel(tracer, winds, ex0, ex3, ey0, ey3, xs, xw, ys, yw, line, wind, strip, vstrip, sem):
    nx, ny, lev = tracer.shape
    ne = ny // 4
    copies = []
    for i, (x, x4, y) in enumerate(((0, 0, 0), (nx - 1, nx - 4, ny - 16))):
        copies.append((
            pltpu.make_async_copy(tracer.at[pl.ds(x4, 4)], xs.at[i], sem.at[i, 0]),
            pltpu.make_async_copy(winds.at[:, x], xw.at[i], sem.at[i, 1]),
            pltpu.make_async_copy(tracer.at[:, pl.ds(y, 16)], ys.at[i], sem.at[i, 2]),
            pltpu.make_async_copy(winds.at[:, :, pl.ds(y, 16)], yw.at[i], sem.at[i, 3]),
        ))
    for part in (0, 2):
        for group in copies:
            group[part].start()
            group[part + 1].start()

    for i, (node, out) in enumerate(((0, ex0), (3, ex3))):
        copies[i][0].wait()
        copies[i][1].wait()
        for x in range(4):
            line[pl.ds((4 * i + x) * ny, ny), :] = xs[i, x].astype(F32)
        for h in range(2):
            wind[pl.ds((2 * i + h) * ny, ny), :] = xw[i, h].astype(F32)
        nodes = [
            [line[pl.ds((4 * i + x) * ny + k, ne, stride=4), :] for k in range(4)] for x in range(4)
        ]
        for k in range(4):
            dx = combine(GRAD[node], [nodes[m][k] for m in range(4)])
            dy = combine(GRAD[k], nodes[node])
            u = wind[pl.ds(2 * i * ny + k, ne, stride=4), :]
            v = wind[pl.ds((2 * i + 1) * ny + k, ne, stride=4), :]
            out[pl.ds(k * ne, ne), :] = -(u * dx + v * dy)

    size = nx * 16
    for i, (base, node, out) in enumerate(((0, 0, ey0), (12, 3, ey3))):
        copies[i][2].wait()
        copies[i][3].wait()
        nel = nx // 4
        strip[pl.ds(i * size, size), :] = ys[i].astype(F32).reshape(size, lev)
        for h in range(2):
            vstrip[pl.ds((2 * i + h) * size, size), :] = yw[i, h].astype(F32).reshape(size, lev)
        nodes = [
            [strip[pl.ds(i * size + x * 16 + base + k, nel, stride=64), :] for k in range(4)]
            for x in range(4)
        ]
        for x in range(4):
            dx = combine(GRAD[x], [nodes[m][node] for m in range(4)])
            dy = combine(GRAD[node], nodes[x])
            at = x * 16 + base + node
            u = vstrip[pl.ds(2 * i * size + at, nel, stride=64), :]
            v = vstrip[pl.ds((2 * i + 1) * size + at, nel, stride=64), :]
            out[pl.ds(x, nel, stride=4), :] = -(u * dx + v * dy)


def edges(tracer, winds):
    nx, ny, lev = tracer.shape
    shapes = [(ny, lev)] * 2 + [(nx, lev)] * 2
    return call(
        edges_kernel,
        [jax.ShapeDtypeStruct(s, F32) for s in shapes],
        tracer, winds,
        vmem=53, flops=10**6, moved=3 * 10**6,
        in_specs=[pl.BlockSpec(memory_space=pltpu.HBM)] * 2,
        scratch_shapes=[
            pltpu.VMEM((2, 4, ny, lev), BF16),
            pltpu.VMEM((2, 2, ny, lev), BF16),
            pltpu.VMEM((2, nx, 16, lev), BF16),
            pltpu.VMEM((2, 2, nx, 16, lev), BF16),
            pltpu.VMEM((8 * ny, lev), F32),
            pltpu.VMEM((4 * ny, lev), F32),
            pltpu.VMEM((2 * nx * 16, lev), F32),
            pltpu.VMEM((4 * nx * 16, lev), F32),
            pltpu.SemaphoreType.DMA((2, 4)),
        ],
    )


def sides_kernel(ey0, ey3, xprev, xnext, out0, out3, line):
    nx, lev = ey0.shape
    ny = xprev.shape[0]
    position = lax.broadcasted_iota(I32, (nx, lev), 0) & 3
    for mid, row, out in ((ey0, 0, out0), (ey3, ny - 1, out3)):
        line[pl.ds(7, 1), :] = xprev[pl.ds(row, 1), :]
        line[pl.ds(8, nx), :] = mid[...]
        line[pl.ds(8 + nx, 1), :] = xnext[pl.ds(row, 1), :]
        here = line[pl.ds(8, nx), :]
        back = 0.5 * (here + line[pl.ds(7, nx), :])
        front = 0.5 * (here + line[pl.ds(9, nx), :])
        out[...] = jnp.where(position == 3, front, jnp.where(position == 0, back, here))


def sides(ey0, ey3, xprev, xnext):
    return call(
        sides_kernel,
        [jax.ShapeDtypeStruct(ey0.shape, F32)] * 2,
        ey0, ey3, xprev, xnext,
        vmem=4, flops=10**5, moved=2 * 10**5,
        scratch_shapes=[pltpu.VMEM((ey0.shape[0] + 16, ey0.shape[1]), F32)],
    )


GROUP = 32


def pack(cap, owners_ref, slot_ref, table_ref, values_ref, low_ref, out_ref):
    cols = owners_ref.shape[1]
    lev = out_ref.shape[1]
    rows = GROUP * cap
    each = 2 * cap + 8
    owner = owners_ref[...]
    high = owner // GROUP
    place = (owner - high * GROUP) * cap + slot_ref[...]
    sub = lax.broadcasted_iota(I32, (rows, cols), 0)
    low_ref[...] = (sub == place).astype(F32).astype(BF16)
    none = jnp.zeros((rows, cols), BF16)
    high_all = jnp.broadcast_to(high.astype(F32).astype(BF16), (rows, cols))
    for i in range(table_ref.shape[0] // GROUP):
        hot = jnp.where(high_all == jnp.full((rows, cols), float(i), BF16), low_ref[...], none)
        packed = jnp.dot(hot, values_ref[...], preferred_element_type=F32)
        pieces = []
        for o in range(GROUP):
            line = table_ref[pl.ds(i * GROUP + o, 1), :]
            pieces.append(packed[o * cap : (o + 1) * cap, :lev])
            pieces.append(packed[o * cap : (o + 1) * cap, lev:])
            pieces.append(jnp.broadcast_to(line, (8, lev)))
        out_ref[pl.ds(i * GROUP * each, GROUP * each), :] = jnp.concatenate(pieces, axis=0).astype(BF16)


def cells_of(nodes, cells_ref, row, ne):
    cells = cell_pair(nodes)
    for a in range(2):
        for b in range(2):
            cells_ref[pl.ds(row + a * 2 * ne + b, ne, stride=2), :] = cells[a][b]


def columns_kernel(owners_ref, classes_ref, temper_hbm, slot_ref, table_ref, out_ref,
                   temper_ref, nodes_ref, cells_ref, sem):
    copy = pltpu.make_async_copy(temper_hbm, temper_ref, sem)
    copy.start()
    cols = owners_ref.shape[1]
    nx, ny, lev = temper_ref.shape
    ne = ny // 4
    devices = table_ref.shape[0]
    chunk = 256
    sub = lax.broadcasted_iota(I32, (devices, chunk), 0)
    upper = (
        lax.broadcasted_iota(I32, (chunk, chunk), 0) < lax.broadcasted_iota(I32, (chunk, chunk), 1)
    ).astype(F32).astype(BF16)
    ones = jnp.ones((chunk, chunk), BF16)
    running = jnp.zeros((devices, chunk), F32)
    table = jnp.zeros((devices, 128), F32)
    slots_sub = lax.broadcasted_iota(I32, (128, chunk), 0)
    for i in range(cols // chunk):
        owner = owners_ref[:, pl.ds(i * chunk, chunk)]
        hit = sub == owner
        hot = hit.astype(F32)
        hot16 = hot.astype(BF16)
        earlier = running + jnp.dot(hot16, upper, preferred_element_type=F32)
        slot = jnp.sum(jnp.where(hit, earlier, 0.0), axis=0, keepdims=True).astype(I32)
        running = running + jnp.dot(hot16, ones, preferred_element_type=F32)
        slot_ref[:, pl.ds(i * chunk, chunk)] = slot
        cost = classes_ref[:, pl.ds(i * chunk, chunk)].astype(F32)
        placed = jnp.where(slots_sub == slot, cost, 0.0).astype(BF16)
        table = table + lax.dot_general(
            hot16, placed, (((1,), (1,)), ((), ())), preferred_element_type=F32
        )
    table_ref[...] = table
    copy.wait()

    def element(e, _):
        base = pl.multiple_of(e * 4 * ny, 8)
        for x in range(4):
            nodes_ref[pl.ds(base + x * ny, ny), :] = temper_ref[4 * e + x].astype(F32)
        nodes = [
            [nodes_ref[pl.ds(base + x * ny + k, ne, stride=4), :] for k in range(4)]
            for x in range(4)
        ]
        cells_of(nodes, cells_ref, pl.multiple_of(e * ny, 8), ne)
        return 0

    lax.fori_loop(0, nx // 4, element, 0, unroll=2)
    out_ref[...] = cells_ref[...].astype(BF16)


def columns_stage(owners, classes, temper, devices):
    nx, ny, lev = temper.shape
    cols = owners.shape[1]
    return call(
        columns_kernel,
        [
            jax.ShapeDtypeStruct((1, cols), I32),
            jax.ShapeDtypeStruct((devices, 128), F32),
            jax.ShapeDtypeStruct((cols, lev), BF16),
        ],
        owners, classes, temper,
        vmem=16, flops=10**9, moved=4 * 10**6,
        in_specs=[pl.BlockSpec(memory_space=pltpu.VMEM)] * 2
        + [pl.BlockSpec(memory_space=pltpu.HBM)],
        scratch_shapes=[
            pltpu.VMEM((nx, ny, lev), BF16),
            pltpu.VMEM((nx * ny, lev), F32),
            pltpu.VMEM((nx * ny // 4, lev), F32),
            pltpu.SemaphoreType.DMA,
        ],
    )


CHUNKS = 4


def tendency_kernel(tracer_ref, winds_ref, nodes_ref, tend_ref, u_ref, v_ref):
    nx, ny, lev = tracer_ref.shape
    ne = ny // 4

    def element(e, _):
        base = pl.multiple_of(e * 4 * ny, 8)
        for x in range(4):
            nodes_ref[pl.ds(base + x * ny, ny), :] = tracer_ref[4 * e + x].astype(F32)
            u_ref[pl.ds(base + x * ny, ny), :] = winds_ref[0, 4 * e + x].astype(F32)
            v_ref[pl.ds(base + x * ny, ny), :] = winds_ref[1, 4 * e + x].astype(F32)
        for t in range(ne // 8):
            off = t * 32
            nodes = [
                [nodes_ref[pl.ds(base + x * ny + off + k, 8, stride=4), :] for k in range(4)]
                for x in range(4)
            ]
            for x in range(4):
                for k in range(4):
                    dx = combine(GRAD[x], [nodes[m][k] for m in range(4)])
                    dy = combine(GRAD[k], nodes[x])
                    u = u_ref[pl.ds(base + x * ny + off + k, 8, stride=4), :]
                    v = v_ref[pl.ds(base + x * ny + off + k, 8, stride=4), :]
                    tend_ref[pl.ds(base + x * ny + k * ne + t * 8, 8), :] = -(u * dx + v * dy)
        return 0

    lax.fori_loop(0, nx // 4, element, 0, unroll=2)


def tendency_stage(tracer, winds):
    nx, ny, lev = tracer.shape
    in_vmem = pl.BlockSpec(memory_space=pltpu.VMEM)
    return call(
        tendency_kernel,
        [jax.ShapeDtypeStruct((nx * ny, lev), F32)] * 2,
        tracer, winds,
        vmem=20, flops=2 * 10**9, moved=8 * 10**6,
        in_specs=[in_vmem] * 2,
        out_specs=[in_vmem] * 2,
        scratch_shapes=[pltpu.VMEM((nx * ny, lev), F32)] * 2,
    )


def tracer_kernel(cap, nodes_ref, tend_ref, xprev, xnext, yprev, ynext, owners_ref, slot_ref,
                  table_ref, temper_ref, new_hbm, out_ref, new_ref, fresh_ref, cells_ref,
                  values_ref, low_ref, out_sem):
    nx, ny, lev = new_ref.shape
    ne = ny // 4
    part = nx // CHUNKS
    elements = nx // 4

    def put(c):
        rows = pl.ds(c * part, part)
        return pltpu.make_async_copy(new_ref.at[rows], new_hbm.at[rows], out_sem.at[c])

    first = lax.broadcasted_iota(I32, (ne, lev), 0) == 0
    last = lax.broadcasted_iota(I32, (ne, lev), 0) == ne - 1

    def assemble(e, _):
        base = pl.multiple_of(e * 4 * ny, 8)
        back = pl.multiple_of(jnp.maximum(e * 4 - 1, 0) * ny, 8)
        front = pl.multiple_of(jnp.minimum(e * 4 + 4, nx - 1) * ny, 8)
        rounded = []
        for x in range(4):
            lines = [tend_ref[pl.ds(base + x * ny + k * ne, ne), :] for k in range(4)]
            if x == 0:
                other = [
                    jnp.where(e == 0, xprev[pl.ds(k * ne, ne), :], tend_ref[pl.ds(back + k * ne, ne), :])
                    for k in range(4)
                ]
                lines = [0.5 * (lines[k] + other[k]) for k in range(4)]
            if x == 3:
                other = [
                    jnp.where(
                        e == elements - 1,
                        xnext[pl.ds(k * ne, ne), :],
                        tend_ref[pl.ds(front + k * ne, ne), :],
                    )
                    for k in range(4)
                ]
                lines = [0.5 * (lines[k] + other[k]) for k in range(4)]
            before = yprev[pl.ds(4 * e + x, 1), :]
            after = ynext[pl.ds(4 * e + x, 1), :]
            low = jnp.where(first, before, pltpu.roll(lines[3], 1, 0))
            high = jnp.where(last, after, pltpu.roll(lines[0], ne - 1, 0))
            whole = [0.5 * (lines[0] + low), lines[1], lines[2], 0.5 * (lines[3] + high)]
            row = []
            for k in range(4):
                where = pl.ds(base + x * ny + k, ne, stride=4)
                fresh = (nodes_ref[where, :] + STEP_SIZE * whole[k]).astype(BF16).astype(F32)
                fresh_ref[where, :] = fresh
                row.append(fresh)
            rounded.append(row)
            new_ref[4 * e + x] = fresh_ref[pl.ds(base + x * ny, ny), :].astype(BF16)
        cells_of(rounded, cells_ref, pl.multiple_of(e * ny, 8), ne)
        return 0

    per = part // 4
    for c in range(CHUNKS):
        lax.fori_loop(c * per, (c + 1) * per, assemble, 0, unroll=2)
        put(c).start()
    values_ref[:, :lev] = cells_ref[...].astype(BF16)
    values_ref[:, lev:] = temper_ref[...]
    pack(cap, owners_ref, slot_ref, table_ref, values_ref, low_ref, out_ref)
    for c in range(CHUNKS):
        put(c).wait()


def tracer_stage(shape, nodes, tend, halos, owners, slots, table, temper_cells, cap):
    nx, ny, lev = shape
    cols = owners.shape[1]
    devices = table.shape[0]
    in_vmem = pl.BlockSpec(memory_space=pltpu.VMEM)
    return call(
        functools.partial(tracer_kernel, cap),
        [
            jax.ShapeDtypeStruct((nx, ny, lev), BF16),
            jax.ShapeDtypeStruct((devices * (2 * cap + 8), lev), BF16),
        ],
        nodes, tend, *halos, owners, slots, table, temper_cells,
        vmem=30, flops=4 * 10**9, moved=8 * 10**6,
        in_specs=[in_vmem] * 10,
        out_specs=[pl.BlockSpec(memory_space=pltpu.HBM), in_vmem],
        scratch_shapes=[
            pltpu.VMEM((nx, ny, lev), BF16),
            pltpu.VMEM((nx * ny, lev), F32),
            pltpu.VMEM((cols, lev), F32),
            pltpu.VMEM((cols, 2 * lev), BF16),
            pltpu.VMEM((GROUP * cap, cols), BF16),
            pltpu.SemaphoreType.DMA((CHUNKS,)),
        ],
    )


PIECES = 2


def radiate_kernel(cap, x_ref, aerosol_hbm, win_ref, wout_ref, out_ref, aerosol_ref,
                   depth_a, depth_b, trans_a, trans_b, bound_a, bound_b, sem):
    blocks, rows, width = aerosol_ref.shape
    lev = x_ref.shape[1]
    each = 2 * cap + 8
    sources = rows // cap
    piece = rows // PIECES

    def fetches(block):
        return [
            pltpu.make_async_copy(
                aerosol_hbm.at[pl.ds(block * rows + j * piece, piece)],
                aerosol_ref.at[block, pl.ds(j * piece, piece)],
                sem.at[block, j],
            )
            for j in range(PIECES)
        ]

    for block in range(blocks):
        for copy in fetches(block):
            copy.start()

    lane = lax.broadcasted_iota(I32, (8, lev), 1)
    sub = lax.broadcasted_iota(I32, (8, lev), 0)
    ones = jnp.ones((lev, lev), BF16)

    def begin(block, bound):
        tracer, temper, mine = [], [], []
        for s in range(sources):
            lines = x_ref[pl.ds((block * sources + s) * each, each), :].astype(F32)
            tracer.append(lines[:cap])
            temper.append(lines[cap : 2 * cap])
            mine += [jnp.where(lane == sub + 8 * j, lines[2 * cap :], 0.0) for j in range(cap // 8)]
        state = jnp.concatenate(
            [jnp.concatenate(tracer, axis=0), jnp.concatenate(temper, axis=0)], axis=1
        ).astype(BF16)
        mine = jnp.concatenate(mine, axis=0).astype(BF16)
        cost = jnp.dot(mine, ones, preferred_element_type=F32)
        for g in range(1, 4):
            bound[g - 1] = jnp.where(cost > g - 0.5, 120.0, -1e30)
        return state

    half = width // 2

    def deepen(state, depth, h):
        at = pl.ds(h * half, half)
        depth[:, at] = jnp.dot(state, win_ref[:, at], preferred_element_type=F32)

    step, tile = 256, 32
    parts = width // step

    def middle(block, depth, bound, trans, chunks):
        for i, r in [(i, r) for i in chunks for r in range(0, rows, tile)]:
            at, line = pl.ds(i * step, step), pl.ds(r, tile)
            group = i * 4 // parts
            top = jnp.concatenate([bound[group - 1, line]] * (step // lev), axis=1) if group else 120.0
            capped = jnp.minimum(depth[line, at] * -LOG2E, top)
            soft = capped - jnp.log2(1.0 + jnp.exp2(capped))
            kept = jnp.exp2(soft * aerosol_ref[block, line, at].astype(F32)).astype(BF16)
            trans[line, at] = kept

    size = rows // 2

    def finish(block, trans, h):
        out_ref[pl.ds(block * rows + h * size, size), :] = jnp.dot(
            trans[pl.ds(h * size, size), :], wout_ref[...], preferred_element_type=F32
        ).astype(BF16)

    def advance(block, following, depth, bound, trans, depth_next, bound_next, before, trans_before):
        for copy in fetches(block):
            copy.wait()
        state = begin(following, bound_next)
        deepen(state, depth_next, 0)
        middle(block, depth, bound, trans, range(0, 2))
        finish(before, trans_before, 0)
        middle(block, depth, bound, trans, range(2, 4))
        finish(before, trans_before, 1)
        middle(block, depth, bound, trans, range(4, 6))
        deepen(state, depth_next, 1)
        middle(block, depth, bound, trans, range(6, parts))

    state = begin(0, bound_a)
    deepen(state, depth_a, 0)
    deepen(state, depth_a, 1)

    def pair(i, _):
        first = 2 * i
        later = jnp.minimum(first + 2, blocks - 1)
        before = jnp.maximum(first - 1, 0)
        advance(first, first + 1, depth_a, bound_a, trans_a, depth_b, bound_b, before, trans_b)
        advance(first + 1, later, depth_b, bound_b, trans_b, depth_a, bound_a, first, trans_a)
        return 0

    lax.fori_loop(0, blocks // 2, pair, 0)
    finish(blocks - 1, trans_b, 0)
    finish(blocks - 1, trans_b, 1)


def radiate(arrived, aerosol, band_in, band_out, cap):
    lev = arrived.shape[1]
    rows, width = aerosol.shape
    block = 16 * cap
    in_vmem = pl.BlockSpec(memory_space=pltpu.VMEM)
    return call(
        functools.partial(radiate_kernel, cap),
        jax.ShapeDtypeStruct((rows, 2 * lev), BF16),
        arrived, aerosol, band_in, band_out,
        vmem=46, flops=7 * 10**9, moved=20 * 10**6,
        in_specs=[in_vmem, pl.BlockSpec(memory_space=pltpu.HBM), in_vmem, in_vmem],
        scratch_shapes=[
            pltpu.VMEM((rows // block, block, width), BF16),
            pltpu.VMEM((block, width), F32),
            pltpu.VMEM((block, width), F32),
            pltpu.VMEM((block, width), BF16),
            pltpu.VMEM((block, width), BF16),
            pltpu.VMEM((3, block, lev), F32),
            pltpu.VMEM((3, block, lev), F32),
            pltpu.SemaphoreType.DMA((rows // block, PIECES)),
        ],
    )


def gather_kernel(cap, owners_ref, slot_ref, back_ref, out_hbm, out_ref, hot_ref, sem):
    cols, rows = out_ref.shape[0], back_ref.shape[0]
    block, wide = hot_ref.shape[1], 128
    lane = lax.broadcasted_iota(I32, (wide, wide), 1)
    none = jnp.zeros((wide, wide), BF16)

    def ship(i):
        at = pl.ds(i * block, block)
        return pltpu.make_async_copy(out_ref.at[at], out_hbm.at[at], sem.at[i])

    for i in range(cols // block):
        for j in range(block // wide):
            at = pl.ds(i * block + j * wide, wide)
            line = (owners_ref[:, at] * cap + slot_ref[:, at]).astype(F32)
            place = jnp.transpose(jnp.broadcast_to(line, (wide, wide))).astype(I32)
            high = (place >> 7).astype(F32).astype(BF16)
            low = (lane == (place & (wide - 1))).astype(F32).astype(BF16)
            for r in range(rows // wide):
                here = jnp.full((wide, wide), float(r), BF16)
                hot_ref[i % 2, pl.ds(j * wide, wide), pl.ds(r * wide, wide)] = jnp.where(
                    high == here, low, none
                )
        out_ref[pl.ds(i * block, block), :] = jnp.dot(
            hot_ref[i % 2], back_ref[...], preferred_element_type=F32
        ).astype(BF16)
        ship(i).start()
    for i in range(cols // block):
        ship(i).wait()


def gather(owners, slots, back, cap):
    return call(
        functools.partial(gather_kernel, cap),
        jax.ShapeDtypeStruct((owners.shape[1], back.shape[1]), BF16),
        owners, slots, back,
        vmem=24, flops=3 * 10**9, moved=3 * 10**6,
        in_specs=[pl.BlockSpec(memory_space=pltpu.VMEM)] * 3,
        out_specs=pl.BlockSpec(memory_space=pl.ANY),
        scratch_shapes=[
            pltpu.VMEM((owners.shape[1], back.shape[1]), BF16),
            pltpu.VMEM((2, owners.shape[1] // 4, back.shape[0]), BF16),
            pltpu.SemaphoreType.DMA((4,)),
        ],
    )


def exchange(x):
    return lax.all_to_all(x, ("dyn", "col"), split_axis=0, concat_axis=0, tiled=True)


def shards(tracer, temper, winds, owners, classes, aerosol, band_in, band_out):
    n_dyn, n_col = lax.axis_size("dyn"), lax.axis_size("col")
    devices = n_dyn * n_col
    lev = tracer.shape[2]
    cap = aerosol.shape[1] // devices

    def send(x, by_dyn, by_col):
        pairs = [
            (i * n_col + j, ((i + by_dyn) % n_dyn) * n_col + (j + by_col) % n_col)
            for i in range(n_dyn)
            for j in range(n_col)
        ]
        return lax.ppermute(x, ("dyn", "col"), pairs)

    owners = owners.reshape(1, -1)
    ex0, ex3, ey0, ey3 = edges(tracer, winds)
    xprev, xnext = send(ex3, 1, 0), send(ex0, -1, 0)
    nodes, tend = tendency_stage(tracer, winds)
    slots, table, temper_cells = columns_stage(owners, classes.reshape(1, -1), temper, devices)
    side0, side3 = sides(ey0, ey3, xprev, xnext)
    yprev, ynext = send(side3, 0, 1), send(side0, 0, -1)
    tracer_new, outgoing = tracer_stage(
        tracer.shape, nodes, tend, (xprev, xnext, yprev, ynext), owners, slots, table, temper_cells, cap
    )
    each = 2 * cap + 8
    arrived = exchange(outgoing.reshape(devices, each, lev)).reshape(-1, lev)
    result = radiate(arrived, aerosol[0], band_in, band_out, cap)
    back = exchange(result.reshape(devices, cap, 2 * lev)).reshape(-1, 2 * lev)
    return (tracer_new, gather(owners, slots, back, cap))


def solution(mesh):
    return jax.shard_map(
        shards,
        mesh=mesh,
        in_specs=(
            P("dyn", "col", None),
            P("dyn", "col", None),
            P(None, "dyn", "col", None),
            P(("dyn", "col"), None),
            P(("dyn", "col")),
            P(("dyn", "col"), None, None),
            P(),
            P(),
        ),
        out_specs=(P("dyn", "col", None), P(("dyn", "col"), None)),
        check_vma=False,
    )
```
